512 devices in a mesh: tm: 64 (over x, z), tok: 8 (over y, core).
Axes of the slice: x: 4, y: 4, z: 16, core: 2. Of those that a mesh axis runs over, the one named last changes fastest.
Arguments:
- anchor: float32 [4, 4, 1024], P(None, None, 'tok'), may hold values from -6 to 6
- latents: float32 [64, 4, 4, 1024], P('tm', None, None, 'tok'), may hold values from -6 to 6
- noise_draws: float32 [64, 4, 4, 1024], P('tm', None, None, 'tok'), may hold values from -6 to 6
- slot_steps: int32 [64, 2], P('tm'), may hold values from 0 to 999, as said below
- class_labels: int32 [4], replicated, may hold values from 0 to 999
- in_weight: bfloat16 [4, 1152], replicated, may hold values from -3 to 3
- time_weight: bfloat16 [256, 1152], replicated, may hold values from -0.375 to 0.375
- class_table: bfloat16 [1000, 1152], replicated, may hold values from -6 to 6
- mod_weight: bfloat16 [1152, 3456], P(None, 'tok'), may hold values from -0.09375 to 0.09375
- qkv_weight: bfloat16 [1152, 1728], P('tm'), may hold values from -0.25 to 0.25
- out_weight: bfloat16 [576, 1152], P('tm'), may hold values from -0.25 to 0.25
- final_weight: bfloat16 [4, 1152], replicated, may hold values from -0.1875 to 0.1875
Outputs:
- updated: float32 [64, 4, 4, 1024], P('tm', None, None, 'tok')
- errors: float32 [64, 4], P('tm')
The draws below stay inside these ranges and needn't reach their ends.
Inputs may be any that keep to these rules, and one draw needn't show every extreme that they name: `slot_steps`: column 0 is the timestep a slot starts from, column 1 the one it steps to, smaller than column 0; each slot starts where the slot before it ends; slot 0 starts at 999 and the last slot steps to 0.
All inputs are finite; a program needn't handle non-finite values.
Results may differ from the reference program's by a relative error of at most 0.0025.
Values may be sent and summed in bfloat16 or wider, within the bound.
A program may use at most 128 MiB of HBM per device.

```python
import math
import jax
import jax.numpy as jnp
from jax import lax

D = 1152
HEAD = 72
HEADS = 8
CHAN = 4
CLASSES = 1000
FREQ = 256
SIDE = 32
SAMPLES = 4
TOKENS = 1024
WINDOW = 64


def draw_slot_steps(key, part):
    key = jax.random.fold_in(key, 11)
    chosen = jax.random.permutation(key, 998)[:WINDOW - 1].astype(jnp.int32) + 1
    ordered = -jnp.sort(-chosen)
    targets = jnp.concatenate([ordered, jnp.array([0], dtype=jnp.int32)]).astype(jnp.int32)
    starts = jnp.concatenate([jnp.array([999], dtype=jnp.int32), targets[:-1]]).astype(jnp.int32)
    return jnp.stack([starts, targets], axis=1).astype(jnp.int32)


def with_ends(values, rng, low, top_value):
    spot = [jax.random.randint(jax.random.fold_in(rng, axis), (), 0, length) for axis, length in enumerate(values.shape)]
    widest = values.shape.index(max(values.shape))
    neighbour = spot[:widest] + [(spot[widest] + 1) % values.shape[widest]] + spot[widest + 1:]
    return values.at[tuple(spot)].set(low).at[tuple(neighbour)].set(top_value)


def level_of(own_key, extent, pieces, smallest, high):
    def one(position, shards_of):
        heights = jax.random.uniform(jax.random.fold_in(jax.random.fold_in(own_key, 6), position), (shards_of,), jnp.float32, smallest / len(pieces), high / len(pieces))
        return jnp.repeat(jnp.exp(heights), extent[position] // shards_of).reshape((-1,) + (1,) * (len(extent) - position - 1))

    gain = one(*pieces[0])
    for cut in pieces[1:]:
        gain = gain * one(*cut)
    return gain


def centred(stream_key, shape, spread, limit, cuts=(), kind=jnp.bfloat16):
    result = spread * jax.random.normal(stream_key, shape, jnp.float32)
    if cuts:
        result = result * level_of(stream_key, shape, cuts, -0.22, 0.18)
    return jnp.clip(result, -limit, limit).astype(kind)


def setup_inputs(seed: int = 0) -> dict:
    key_list = jax.random.split(jax.random.key(seed), 13)
    return {
        "anchor": centred(key_list[0], (SAMPLES, CHAN, TOKENS), 1.0, 6.0, ((2, 8),), jnp.float32),
        "latents": centred(key_list[1], (WINDOW, SAMPLES, CHAN, TOKENS), 1.0, 6.0, ((0, 64), (3, 8)), jnp.float32),
        "noise_draws": centred(key_list[2], (WINDOW, SAMPLES, CHAN, TOKENS), 1.0, 6.0, ((0, 64), (3, 8)), jnp.float32),
        "slot_steps": draw_slot_steps(jax.random.fold_in(key_list[12], 71), 0),
        "class_labels": with_ends(jax.random.randint(key_list[4], (SAMPLES,), 0, CLASSES), jax.random.fold_in(key_list[4], 1), 0, CLASSES - 1).astype(jnp.int32),
        "in_weight": centred(key_list[5], (CHAN, D), CHAN ** -0.5, 3.0),
        "time_weight": centred(key_list[6], (FREQ, D), FREQ ** -0.5, 0.375),
        "class_table": centred(key_list[7], (CLASSES, D), 1.0, 6.0),
        "mod_weight": centred(key_list[8], (D, 3 * D), (4 * D) ** -0.5, 0.09375, ((1, 8),)),
        "qkv_weight": centred(key_list[9], (D, 3 * HEADS * HEAD), (D // 2) ** -0.5, 0.25, ((0, 64),)),
        "out_weight": centred(key_list[10], (HEADS * HEAD, D), (HEADS * HEAD) ** -0.5, 0.25, ((0, 64),)),
        "final_weight": centred(key_list[11], (CHAN, D), D ** -0.5, 0.1875),
    }


def layer_norm(values):
    centered = values - lax.optimization_barrier(jnp.mean(values, axis=-1, keepdims=True))
    variance = lax.optimization_barrier(jnp.mean(centered * centered, axis=-1, keepdims=True))
    return centered * lax.rsqrt(variance + 1e-06)

def position_table(positions):
    quarter = D // 4
    angular = jnp.exp(-math.log(10000.0) * jnp.arange(quarter, dtype=jnp.float32) / quarter)
    row_pos = (positions // SIDE).astype(jnp.float32)[:, None] * angular[None, :]
    col_pos = (positions % SIDE).astype(jnp.float32)[:, None] * angular[None, :]
    return jnp.concatenate([jnp.sin(row_pos), jnp.cos(row_pos), jnp.sin(col_pos), jnp.cos(col_pos)], axis=-1)

def time_features(t_from):
    half_freq = FREQ // 2
    angular = jnp.exp(-math.log(10000.0) * jnp.arange(half_freq, dtype=jnp.float32) / half_freq)
    phases = t_from * angular
    return jnp.concatenate([jnp.cos(phases), jnp.sin(phases)])[None, :]

def signal_level(step_value):
    return 0.005 + 0.99 * jnp.cos(0.4 * math.pi * step_value / 1000.0) ** 2

def coefficients(t_from, t_to):
    level_from = signal_level(t_from)
    level_to = signal_level(t_to)
    keep_coef = jnp.sqrt(level_to / level_from)
    noise_coef = 0.5 * jnp.sqrt((1.0 - level_to) / (1.0 - level_from)) * jnp.sqrt(1.0 - level_from / level_to)
    eps_coef = jnp.sqrt(1.0 - level_to - noise_coef * noise_coef) - keep_coef * jnp.sqrt(1.0 - level_from)
    return (keep_coef, noise_coef, eps_coef)

def reference(anchor, latents, noise_draws, slot_steps, class_labels, in_weight, time_weight, class_table, mod_weight, qkv_weight, out_weight, final_weight):
    priors = jnp.concatenate([anchor[None], latents[:-1]], axis=0)
    pos_table = position_table(jnp.arange(TOKENS, dtype=jnp.int32))
    class_embed = class_table[class_labels].astype(jnp.float32)
    scale_factor = 1.0 / math.sqrt(HEAD)
    samples = anchor.shape[0]

    def one_slot(inputs):
        prior, steps_here, noise_here = inputs
        t_from = steps_here[0].astype(jnp.float32)
        t_to = steps_here[1].astype(jnp.float32)
        embedded = jnp.einsum('bcl,cd->bld', prior, in_weight.astype(jnp.float32), precision=lax.Precision.HIGHEST) + pos_table[None]
        time_embed = jnp.dot(time_features(t_from), time_weight.astype(jnp.float32), precision=lax.Precision.HIGHEST)
        condition_vec = jax.nn.silu(time_embed + class_embed).astype(jnp.bfloat16)
        modulation = jnp.dot(condition_vec, mod_weight, preferred_element_type=jnp.float32)
        shift_m = modulation[:, :D]
        scale_m = modulation[:, D:2 * D]
        gate_m = modulation[:, 2 * D:]
        normed = (layer_norm(embedded) * (1.0 + scale_m[:, None]) + shift_m[:, None]).astype(jnp.bfloat16)
        qkv_all = jnp.dot(normed.reshape(samples * TOKENS, D), qkv_weight, preferred_element_type=jnp.float32).astype(jnp.bfloat16)
        qkv_all = qkv_all.reshape(samples, TOKENS, 3, HEADS, HEAD)
        queries = qkv_all[:, :, 0].astype(jnp.float32)
        key_rows = qkv_all[:, :, 1].astype(jnp.float32)
        value_rows = qkv_all[:, :, 2].astype(jnp.float32)
        scores = jnp.einsum('bqhd,bkhd->bhqk', queries, key_rows) * scale_factor
        exp_scores = jnp.exp(scores)
        totals = lax.optimization_barrier(jnp.sum(exp_scores, axis=3))
        exp_b = lax.optimization_barrier(exp_scores.astype(jnp.bfloat16)).astype(jnp.float32)
        weighted = jnp.einsum('bhqk,bkhd->bqhd', exp_b, value_rows)
        attended = (weighted / jnp.transpose(totals, (0, 2, 1))[..., None]).astype(jnp.bfloat16)
        projected = jnp.dot(attended.reshape(samples * TOKENS, HEADS * HEAD), out_weight, preferred_element_type=jnp.float32)
        hidden_state = embedded + gate_m[:, None] * projected.reshape(samples, TOKENS, D)
        final_normed = layer_norm(hidden_state).astype(jnp.bfloat16)
        predicted = jnp.einsum('bld,cd->bcl', final_normed.astype(jnp.float32), final_weight.astype(jnp.float32))
        keep_coef, noise_coef, eps_coef = coefficients(t_from, t_to)
        return (keep_coef - 1.0) * prior + eps_coef * predicted + noise_coef * noise_here
    drifts = lax.map(one_slot, (priors, slot_steps, noise_draws))
    updated = anchor[None] + jnp.cumsum(drifts, axis=0)
    change = updated - latents
    errors = lax.optimization_barrier(jnp.mean(change * change, axis=(2, 3)))
    return (updated, errors)
```

```python
import math

import jax
import jax.numpy as jnp
import ml_dtypes
import numpy as np
from jax import lax
from jax.experimental import pallas as pl
from jax.experimental.pallas import tpu as pltpu
from jax.sharding import PartitionSpec as P

MESH = pl.DeviceIdType.MESH
D = 1152
HEAD = 72
HEADS = 8
CHAN = 4
FREQ = 256
SIDE = 32
TOKENS = 1024
IMAGES = 4
NX, NZ, NT = 4, 16, 8
SLOTS = NX * NZ
HP = 80
POSK = 6 * SIDE
KX = POSK + 16
HALF = 512
F32 = jnp.float32
BF16 = jnp.bfloat16


def split3(values):
    high = values.astype(BF16).astype(F32)
    rest = values - high
    mid = rest.astype(BF16).astype(F32)
    return high, mid, rest - mid


def position_constants():
    quarter = D // 4
    angular = np.exp(np.float32(-math.log(10000.0)) * np.arange(quarter, dtype=np.float32) / np.float32(quarter)).astype(np.float32)
    angles = (np.arange(SIDE, dtype=np.float32)[:, None] * angular[None, :]).astype(np.float32)
    pair = np.concatenate([np.sin(angles), np.cos(angles)], axis=1).astype(np.float32)
    table = np.zeros((D, POSK), dtype=ml_dtypes.bfloat16)
    rest = pair
    for part in range(3):
        term = rest.astype(ml_dtypes.bfloat16)
        rest = rest - term.astype(np.float32)
        table[: D // 2, part * SIDE : (part + 1) * SIDE] = term.T
        table[D // 2 :, (3 + part) * SIDE : (4 + part) * SIDE] = term.T
    tokens = np.arange(TOKENS)
    select = np.zeros((POSK, TOKENS), dtype=ml_dtypes.bfloat16)
    for part in range(3):
        select[part * SIDE + tokens // SIDE, tokens] = 1
        select[(3 + part) * SIDE + tokens % SIDE, tokens] = 1
    return table, select


def kernel(
    coef_ref, lat_ref, anchor_ref, noise_ref, feat_ref, cls_ref, fw_ref,
    wmain_ref, wrem_ref, wo_ref, time_hbm, mod_hbm, table_hbm, select_hbm,
    upd_ref, err_ref,
    time_w, mod_w, table, xs, psrc, pr, mod_s, mod_r, mod_t, bc,
    zw, zr, wf, wx, wt, zo, of, wob, emb, own, normed, att_s, att_r,
    dr_r, tx_r, er_r, er_s,
    loc_sem, pr_send, pr_recv, mod_send, mod_recv, zw_send, zw_recv, zr_send, zr_recv,
    wx_send, wx_recv, zo_send, zo_recv, ox_send, ox_recv, sib_send, sib_recv,
    att_send, att_recv, dr_send, dr_recv, tx_send, tx_recv, er_send, er_recv,
):
    slot = lax.axis_index("tm")
    tok = lax.axis_index("tok")
    x = lax.div(slot, NZ)
    z = lax.rem(slot, NZ)
    core = lax.rem(tok, 2)
    sibling = tok + 1 - 2 * core

    def z_peer(k):
        return (x * NZ + lax.rem(z + k, NZ), tok)

    def x_peer(k):
        return (lax.rem(x + k, NX) * NZ + z, tok)

    def t_peer(k):
        return (slot, lax.rem(tok + k, NT))

    def each(count, action, first=1):
        def step(k, carry):
            action(k)
            return carry

        lax.fori_loop(first, count, step, 0)

    def remote(src, dst, send, recv, device):
        return pltpu.make_async_remote_copy(
            src_ref=src, dst_ref=dst, send_sem=send, recv_sem=recv, device_id=device, device_id_type=MESH
        )

    loads = [
        pltpu.make_async_copy(time_hbm, time_w, loc_sem.at[0]),
        pltpu.make_async_copy(mod_hbm, mod_w, loc_sem.at[1]),
        pltpu.make_async_copy(table_hbm, table, loc_sem.at[2]),
        pltpu.make_async_copy(select_hbm, xs.at[pl.ds(0, POSK)], loc_sem.at[3]),
    ]
    for load in loads:
        load.start()

    barrier = pltpu.get_barrier_semaphore()

    def greet(device):
        pl.semaphore_signal(barrier, inc=1, device_id=device, device_id_type=MESH)

    each(NZ, lambda k: greet(z_peer(k)))
    each(NX, lambda k: greet(x_peer(k)))
    each(NT, lambda k: greet(t_peer(k)))
    before = lax.rem(slot + SLOTS - 1, SLOTS)
    after = lax.rem(slot + 1, SLOTS)
    each(NT, lambda k: greet((before, k)), first=0)
    psrc[...] = jnp.where(slot == SLOTS - 1, anchor_ref[...], lat_ref[0])
    zw[z] = wmain_ref[...]
    zr[z] = wrem_ref[...]
    zo[z] = wo_ref[...]
    pl.semaphore_wait(barrier, NZ - 1 + NX - 1 + NT - 1 + NT)

    def prior_copy(k):
        return remote(psrc, pr.at[tok], pr_send.at[k], pr_recv.at[tok], (after, k))

    def prior_arrival(k):
        return remote(psrc, pr.at[k], pr_send.at[k], pr_recv.at[k], (after, k))

    def zw_copy(k):
        return remote(zw.at[z], zw.at[z], zw_send.at[k], zw_recv.at[k], z_peer(k))

    def zr_copy(k):
        return remote(zr.at[z], zr.at[z], zr_send.at[k], zr_recv.at[k], z_peer(k))

    def zo_copy(k):
        return remote(zo.at[z], zo.at[z], zo_send.at[k], zo_recv.at[k], z_peer(k))

    def wx_copy(k):
        return remote(wx.at[x], wx.at[x], wx_send.at[k], wx_recv.at[k], x_peer(k))

    def ox_copy(k):
        return remote(wob.at[core, x], wob.at[core, x], ox_send.at[k], ox_recv.at[k], x_peer(k))

    def mod_copy(k):
        return remote(mod_s, mod_r.at[tok], mod_send.at[k], mod_recv.at[k], t_peer(k))

    def att_copy(b, k):
        there = lax.rem(tok + k, NT)
        return remote(att_s.at[b, there], att_r.at[b, tok], att_send.at[b, k], att_recv.at[b, k], t_peer(k))

    each(NT, lambda k: prior_copy(k).start(), first=0)

    def start_w(k):
        zw_copy(k).start()
        zr_copy(k).start()

    each(NZ, start_w)

    loads[0].wait()
    high, mid, low = split3(feat_ref[...])
    feats = jnp.concatenate([high, mid, low, jnp.zeros((5, FREQ), F32)], axis=0).astype(BF16)
    parts = jnp.dot(feats, time_w[...], preferred_element_type=F32)
    value = parts[0:1] + parts[1:2] + parts[2:3] + cls_ref[...]
    condition = (value / (1.0 + jnp.exp(-value))).astype(BF16)
    loads[1].wait()
    mod_s[:, 432:512] = jnp.zeros((8, 80), F32)
    mod_s[:, 0:432] = jnp.dot(condition, mod_w[...], preferred_element_type=F32)
    mod_r[tok] = mod_s[...]
    each(NT, lambda k: mod_copy(k).start())
    loads[2].wait()
    loads[3].wait()
    each(NT, lambda k: mod_copy(k).wait())
    for source in range(NT):
        mod_t[source * 432 : source * 432 + 432] = jnp.transpose(mod_r[source])[0:432]
    for b in range(IMAGES):
        bc[b, 0] = jnp.broadcast_to(1.0 + mod_t[D : 2 * D, b : b + 1], (D, 128))
        bc[b, 1] = jnp.broadcast_to(mod_t[0:D, b : b + 1], (D, 128))
    each(NT, lambda k: prior_arrival(k).wait(), first=0)

    rows = 48

    def embed(step, carry):
        b, part = lax.div(step, 2), lax.rem(step, 2)
        line = jnp.concatenate([pr[4 * part + t, b] for t in range(4)], axis=1)
        high, mid, low = split3(line)
        split = jnp.concatenate([high, mid, low, jnp.zeros((4, HALF), F32)], axis=0)
        lanes = pl.ds(pl.multiple_of(part * HALF, HALF), HALF)
        xs[POSK:KX, lanes] = split.astype(BF16)
        emb[...] = jnp.dot(table[...], xs[:, lanes], preferred_element_type=F32)

        def add(r, total):
            chunk = emb[pl.ds(pl.multiple_of(r * rows, rows), rows)]
            return total + jnp.sum(chunk.reshape(rows // 8, 8, HALF), axis=0)

        total = lax.fori_loop(0, D // rows, add, jnp.zeros((8, HALF), F32))
        mean = jnp.sum(total, axis=0, keepdims=True) * (1.0 / D)

        def square(r, total):
            chunk = emb[pl.ds(pl.multiple_of(r * rows, rows), rows)] - mean
            return total + jnp.sum((chunk * chunk).reshape(rows // 8, 8, HALF), axis=0)

        total = lax.fori_loop(0, D // rows, square, jnp.zeros((8, HALF), F32))
        inverse = lax.rsqrt(jnp.sum(total, axis=0, keepdims=True) * (1.0 / D) + 1e-06)

        def scale(r, carry):
            here = pl.ds(pl.multiple_of(r * rows, rows), rows)
            gain, shift = bc[b, 0, here], bc[b, 1, here]
            for t in range(4):
                cut = slice(t * 128, t * 128 + 128)
                out = (emb[here, cut] - mean[:, cut]) * inverse[:, cut] * gain + shift
                normed[b, here, pl.ds(pl.multiple_of(part * HALF + t * 128, 128), 128)] = out.astype(BF16)
            return carry

        lax.fori_loop(0, D // rows, scale, 0)

        @pl.when(part == lax.div(tok, 4))
        def _():
            mine = pl.ds(pl.multiple_of(lax.rem(tok, 4) * 128, 128), 128)
            own[b] = emb[:, mine]

        return carry

    lax.fori_loop(0, 4, embed, 0)

    def arrive_w(k):
        zw_copy(k).wait()
        zr_copy(k).wait()

    each(NZ, arrive_w)
    each(NZ, lambda k: zo_copy(k).start())
    for i in range(NZ):
        wf[18 * i : 18 * i + 16] = zw[i].astype(F32)
        wf[18 * i + 16 : 18 * i + 18] = zr[i]
    wx[x] = wf[...].astype(BF16)
    each(NX, lambda k: wx_copy(k).start())
    lax.fori_loop(4, 8, embed, 0)
    each(NX, lambda k: wx_copy(k).wait())
    wt[...] = jnp.transpose(wx[...].reshape(D, 256))

    factor = math.log2(math.e) / math.sqrt(HEAD)
    block = 256

    def attend(b, carry):
        qkv = jnp.dot(wt[...], normed[b], preferred_element_type=F32)
        queries = qkv[0:HEAD].astype(BF16)
        keys = qkv[HEAD : 2 * HEAD].astype(BF16)
        values = jnp.concatenate([qkv[2 * HEAD : 3 * HEAD], jnp.ones((8, TOKENS), F32)], axis=0).astype(BF16)
        for i in range(TOKENS // block):
            scores = lax.dot_general(
                keys, queries[:, i * block : (i + 1) * block], (((0,), (0,)), ((), ())), preferred_element_type=F32
            )
            weights = jnp.exp2(scores * factor).astype(BF16)
            summed = jnp.dot(values, weights, preferred_element_type=F32)
            out = (summed / summed[HEAD : HEAD + 1]).astype(BF16)
            for t in range(2):
                att_s[b, 2 * i + t] = out[:, t * 128 : t * 128 + 128]
        att_r[b, tok] = att_s[b, tok]
        each(NT, lambda k: att_copy(b, k).start())
        return carry

    lax.fori_loop(0, 2, attend, 0)

    each(NZ, lambda k: zo_copy(k).wait())
    for i in range(NZ):
        base = 9 * i + (HP - HEAD) * (i // 8)
        of[base : base + 9] = zo[i].astype(F32)[0:9]
    for h in range(2):
        of[h * HP + HEAD : (h + 1) * HP] = jnp.zeros((HP - HEAD, 640), F32)
    wob[core, x] = of[...].astype(BF16)
    each(NX, lambda k: ox_copy(k).start())
    lax.fori_loop(2, 4, attend, 0)
    each(NX, lambda k: ox_copy(k).wait())
    share = remote(wob.at[core], wob.at[core], sib_send, sib_recv, (slot, sibling))
    share.start()
    other = remote(wob.at[1 - core], wob.at[1 - core], sib_send, sib_recv, (slot, sibling))
    each(NT, lambda k: [att_copy(b, k).wait() for b in range(IMAGES)])
    share.wait_send()
    other.wait_recv()

    attended = jnp.concatenate([att_r[b].reshape(HEADS * HP, 128) for b in range(IMAGES)], axis=1)
    contract = (((0,), (0,)), ((), ()))
    emb[0:640] = lax.dot_general(wob[0].reshape(HEADS * HP, 640), attended, contract, preferred_element_type=F32)
    emb[640:D] = lax.dot_general(wob[1].reshape(HEADS * HP, 640)[:, 128:640], attended, contract, preferred_element_type=F32)

    def hidden(r, total):
        here = pl.ds(pl.multiple_of(r * rows, rows), rows)
        gates = mod_t[pl.ds(pl.multiple_of(2 * D + r * rows, rows), rows)]
        sums = []
        for b in range(IMAGES):
            cut = slice(b * 128, b * 128 + 128)
            value = own[b, here] + gates[:, b : b + 1] * emb[here, cut]
            emb[here, cut] = value
            sums.append(jnp.sum(value.reshape(rows // 8, 8, 128), axis=0))
        return total + jnp.concatenate(sums, axis=1)

    total = lax.fori_loop(0, D // rows, hidden, jnp.zeros((8, HALF), F32))
    mean = jnp.sum(total, axis=0, keepdims=True) * (1.0 / D)

    def square(r, total):
        chunk = emb[pl.ds(pl.multiple_of(r * rows, rows), rows)] - mean
        return total + jnp.sum((chunk * chunk).reshape(rows // 8, 8, HALF), axis=0)

    total = lax.fori_loop(0, D // rows, square, jnp.zeros((8, HALF), F32))
    inverse = lax.rsqrt(jnp.sum(total, axis=0, keepdims=True) * (1.0 / D) + 1e-06)
    final = ((emb[...] - mean) * inverse).astype(BF16)
    predicted = jnp.dot(fw_ref[...], final, preferred_element_type=F32)

    keep, eps, noise = coef_ref[0], coef_ref[1], coef_ref[2]
    for b in range(IMAGES):
        dr_r[z, b] = keep * pr[tok, b] + eps * predicted[0:CHAN, b * 128 : b * 128 + 128] + noise * noise_ref[0, b]

    def dr_copy(k):
        return remote(dr_r.at[z], dr_r.at[z], dr_send.at[k], dr_recv.at[k], z_peer(k))

    def tx_copy(k):
        return remote(tx_r.at[x], tx_r.at[x], tx_send.at[k], tx_recv.at[k], x_peer(k))

    each(NZ, lambda k: dr_copy(k).start())
    each(NZ, lambda k: dr_copy(k).wait())
    nothing = jnp.zeros((IMAGES, CHAN, 128), F32)
    whole, reached = nothing, nothing
    for i in range(NZ):
        term = dr_r[i]
        whole = whole + term
        reached = reached + jnp.where(i <= z, term, nothing)
    tx_r[x] = whole
    each(NX, lambda k: tx_copy(k).start())
    each(NX, lambda k: tx_copy(k).wait())
    earlier = nothing
    for i in range(NX):
        earlier = earlier + jnp.where(i < x, tx_r[i], nothing)
    updated = anchor_ref[...] + (earlier + reached)
    upd_ref[0] = updated
    change = updated - lat_ref[0]
    er_s[...] = jnp.sum(change * change, axis=1)
    er_r[tok] = er_s[...]

    def er_copy(k):
        return remote(er_s, er_r.at[tok], er_send.at[k], er_recv.at[k], t_peer(k))

    each(NT, lambda k: er_copy(k).start())
    each(NT, lambda k: er_copy(k).wait())
    err_ref[...] = jnp.sum(jnp.sum(er_r[...], axis=0), axis=1, keepdims=True) * (1.0 / (CHAN * TOKENS))


def time_features(t_from):
    half_freq = FREQ // 2
    angular = jnp.exp(-math.log(10000.0) * jnp.arange(half_freq, dtype=F32) / half_freq)
    phases = t_from * angular
    return jnp.concatenate([jnp.cos(phases), jnp.sin(phases)])[None, :]


def signal_level(step_value):
    return 0.005 + 0.99 * jnp.cos(0.4 * math.pi * step_value / 1000.0) ** 2


def coefficients(t_from, t_to):
    level_from = signal_level(t_from)
    level_to = signal_level(t_to)
    keep_coef = jnp.sqrt(level_to / level_from)
    noise_coef = 0.5 * jnp.sqrt((1.0 - level_to) / (1.0 - level_from)) * jnp.sqrt(1.0 - level_from / level_to)
    eps_coef = jnp.sqrt(1.0 - level_to - noise_coef * noise_coef) - keep_coef * jnp.sqrt(1.0 - level_from)
    return (keep_coef, noise_coef, eps_coef)


def body(
    anchor, latents, noise_draws, slot_steps, class_labels, in_weight, time_weight, class_table,
    mod_weight, qkv_weight, out_weight, final_weight,
):
    tok = lax.axis_index("tok")
    t_from = slot_steps[0, 0].astype(F32)
    t_to = slot_steps[0, 1].astype(F32)
    keep_coef, noise_coef, eps_coef = coefficients(t_from, t_to)
    coef = jnp.stack([keep_coef - 1.0, eps_coef, noise_coef])
    features = time_features(t_from)
    classes = jnp.concatenate(
        [lax.dynamic_slice(class_table, (class_labels[b], 0), (1, D)) for b in range(IMAGES)]
        + [jnp.zeros((4, D), BF16)],
        axis=0,
    ).astype(F32)
    head_cols = jnp.concatenate(
        [lax.dynamic_slice(qkv_weight, (0, HEAD * (HEADS * i + tok)), (18, HEAD)) for i in range(3)]
        + [jnp.zeros((18, 40), BF16)],
        axis=1,
    )
    w_main = head_cols[:16]
    w_rem = head_cols[16:].astype(F32)
    wo = jnp.pad(lax.dynamic_slice(out_weight, (0, 512 * lax.rem(tok, 2)), (9, 640)), ((0, 7), (0, 0)))
    table, select = position_constants()
    turned = in_weight.T
    table = jnp.concatenate(
        [jnp.asarray(table), turned, turned, turned, jnp.zeros((D, 4), BF16)], axis=1
    )
    vmem = pl.BlockSpec(memory_space=pltpu.VMEM)
    anywhere = pl.BlockSpec(memory_space=pl.ANY)
    dma = pltpu.SemaphoreType.DMA
    updated, errors = pl.pallas_call(
        kernel,
        out_shape=(
            jax.ShapeDtypeStruct((1, IMAGES, CHAN, 128), F32),
            jax.ShapeDtypeStruct((IMAGES, 1), F32),
        ),
        in_specs=[pl.BlockSpec(memory_space=pltpu.SMEM)] + [vmem] * 9 + [anywhere] * 4,
        out_specs=(vmem, vmem),
        scratch_shapes=[
            pltpu.VMEM((FREQ, D), BF16),
            pltpu.VMEM((D, 432), BF16),
            pltpu.VMEM((D, KX), BF16),
            pltpu.VMEM((KX, TOKENS), BF16),
            pltpu.VMEM((IMAGES, CHAN, 128), F32),
            pltpu.VMEM((NT, IMAGES, CHAN, 128), F32),
            pltpu.VMEM((8, 512), F32),
            pltpu.VMEM((NT, 8, 512), F32),
            pltpu.VMEM((3 * D, 8), F32),
            pltpu.VMEM((IMAGES, 2, D, 128), F32),
            pltpu.VMEM((NZ, 16, 256), BF16),
            pltpu.VMEM((NZ, 2, 256), F32),
            pltpu.VMEM((18 * NZ, 256), F32),
            pltpu.VMEM((NX, 18 * NZ, 256), BF16),
            pltpu.VMEM((256, D), BF16),
            pltpu.VMEM((NZ, 16, 640), BF16),
            pltpu.VMEM((2 * HP, 640), F32),
            pltpu.VMEM((2, NX, 2 * HP, 640), BF16),
            pltpu.VMEM((D, HALF), F32),
            pltpu.VMEM((IMAGES, D, 128), F32),
            pltpu.VMEM((IMAGES, D, TOKENS), BF16),
            pltpu.VMEM((IMAGES, NT, HP, 128), BF16),
            pltpu.VMEM((IMAGES, NT, HP, 128), BF16),
            pltpu.VMEM((NZ, IMAGES, CHAN, 128), F32),
            pltpu.VMEM((NX, IMAGES, CHAN, 128), F32),
            pltpu.VMEM((NT, IMAGES, 128), F32),
            pltpu.VMEM((IMAGES, 128), F32),
            dma((4,)),
            dma((NT,)), dma((NT,)),
            dma((NT,)), dma((NT,)),
            dma((NZ,)), dma((NZ,)),
            dma((NZ,)), dma((NZ,)),
            dma((NX,)), dma((NX,)),
            dma((NZ,)), dma((NZ,)),
            dma((NX,)), dma((NX,)),
            dma, dma,
            dma((IMAGES, NT)), dma((IMAGES, NT)),
            dma((NZ,)), dma((NZ,)),
            dma((NX,)), dma((NX,)),
            dma((NT,)), dma((NT,)),
        ],
        compiler_params=pltpu.CompilerParams(
            collective_id=0, has_side_effects=True, vmem_limit_bytes=56 * 1024 * 1024
        ),
        cost_estimate=pl.CostEstimate(flops=6_000_000_000, bytes_accessed=8_000_000, transcendentals=4_200_000),
    )(
        coef, latents, anchor, noise_draws, features, classes, final_weight,
        w_main, w_rem, wo, time_weight, mod_weight, table, jnp.asarray(select),
    )
    return updated, errors.reshape(1, IMAGES)


def solution(mesh):
    in_specs = (
        P(None, None, "tok"),
        P("tm", None, None, "tok"),
        P("tm", None, None, "tok"),
        P("tm", None),
        P(),
        P(),
        P(),
        P(),
        P(None, "tok"),
        P("tm", None),
        P("tm", None),
        P(),
    )
    out_specs = (P("tm", None, None, "tok"), P("tm", None))
    return jax.shard_map(body, mesh=mesh, in_specs=in_specs, out_specs=out_specs, check_vma=False)
```

```python
import math

import jax
import jax.numpy as jnp
import ml_dtypes
import numpy as np
from jax import lax
from jax.experimental import pallas as pl
from jax.experimental.pallas import tpu as pltpu
from jax.sharding import PartitionSpec as P

MESH = pl.DeviceIdType.MESH
D = 1152
HEAD = 72
HEADS = 8
CHAN = 4
CLASSES = 1000
FREQ = 256
SIDE = 32
TOKENS = 1024
IMAGES = 4
NX, NZ, NT = 4, 16, 8
SLOTS = NX * NZ
HP = 80
CHUNK = 9
PIECE = 48
HALF = 512
F32 = jnp.float32
BF16 = jnp.bfloat16


def split3(values):
    high = values.astype(BF16).astype(F32)
    rest = values - high
    mid = rest.astype(BF16).astype(F32)
    return high, mid, rest - mid


def split2(values):
    high = values.astype(BF16)
    return high, (values - high.astype(F32)).astype(BF16)


def position_constants():
    quarter = D // 4
    angular = np.exp(np.float32(-math.log(10000.0)) * np.arange(quarter, dtype=np.float32) / np.float32(quarter)).astype(np.float32)
    angles = (np.arange(SIDE, dtype=np.float32)[:, None] * angular[None, :]).astype(np.float64)
    pair = np.concatenate([np.sin(angles), np.cos(angles)], axis=1)
    table = np.zeros((D, 128))
    table[: D // 2, 0:SIDE] = pair.T
    table[D // 2 :, SIDE : 2 * SIDE] = pair.T
    table = table - table.mean(axis=0, keepdims=True)
    tokens = np.arange(TOKENS)
    spread = (table[:, tokens // SIDE] + table[:, SIDE + tokens % SIDE]) ** 2
    half_freq = FREQ // 2
    freq = np.exp(-math.log(10000.0) * np.arange(half_freq) / half_freq)
    return (
        table.astype(np.float32),
        spread.mean(axis=0)[None, :].astype(np.float32),
        freq[None, :].astype(np.float32),
    )


def signal_level(step_value):
    return 0.005 + 0.99 * jnp.cos(0.4 * math.pi * step_value / 1000.0) ** 2


def coefficients(t_from, t_to):
    level_from = signal_level(t_from)
    level_to = signal_level(t_to)
    keep_coef = jnp.sqrt(level_to / level_from)
    noise_coef = 0.5 * jnp.sqrt((1.0 - level_to) / (1.0 - level_from)) * jnp.sqrt(1.0 - level_from / level_to)
    eps_coef = jnp.sqrt(1.0 - level_to - noise_coef * noise_coef) - keep_coef * jnp.sqrt(1.0 - level_from)
    return (keep_coef, noise_coef, eps_coef)


def kernel(
    steps_ref, labels_ref, lat_ref, anchor_ref, noise_ref, freq_ref, cls_ref, fw_ref, inw_ref, spread_ref,
    wq_ref, wo_ref, time_hbm, mod_hbm, table_hbm,
    upd_ref, err_ref,
    time_w, mod_w, table, tcat, xs, xo, psrc, pr, mod_s, mod_r, mod_t, rb, ab, shifts,
    zw, zr, wf, wx, wt, zo, po, of, wob, emb, own, att_s, att_r,
    dr_r, tx_r, er_r, er_s, invs,
    loc_sem, pr_send, pr_recv, mod_send, mod_recv, zw_send, zw_recv, zr_send, zr_recv,
    wx_send, wx_recv, zo_send, zo_recv, ox_send, ox_recv, sib_send, sib_recv,
    att_send, att_recv, dr_send, dr_recv, tx_send, tx_recv, er_send, er_recv,
):
    slot = lax.axis_index("tm")
    tok = lax.axis_index("tok")
    x = lax.div(slot, NZ)
    z = lax.rem(slot, NZ)
    core = lax.rem(tok, 2)
    sibling = tok + 1 - 2 * core

    def z_peer(k):
        return (x * NZ + lax.rem(z + k, NZ), tok)

    def x_peer(k):
        return (lax.rem(x + k, NX) * NZ + z, tok)

    def t_peer(k):
        return (slot, lax.rem(tok + k, NT))

    def each(count, action, first=1):
        def step(k, carry):
            action(k)
            return carry

        lax.fori_loop(first, count, step, 0)

    def remote(src, dst, send, recv, device):
        return pltpu.make_async_remote_copy(
            src_ref=src, dst_ref=dst, send_sem=send, recv_sem=recv, device_id=device, device_id_type=MESH
        )

    loads = [
        pltpu.make_async_copy(time_hbm, time_w, loc_sem.at[0]),
        pltpu.make_async_copy(mod_hbm, mod_w, loc_sem.at[1]),
        pltpu.make_async_copy(table_hbm, table, loc_sem.at[2]),
    ]
    for load in loads:
        load.start()

    barrier = pltpu.get_barrier_semaphore()

    def greet(device):
        pl.semaphore_signal(barrier, inc=1, device_id=device, device_id_type=MESH)

    each(NZ, lambda k: greet(z_peer(k)))
    each(NX, lambda k: greet(x_peer(k)))
    each(NT, lambda k: greet(t_peer(k)))
    before = lax.rem(slot + SLOTS - 1, SLOTS)
    after = lax.rem(slot + 1, SLOTS)
    each(NT, lambda k: greet((before, k)), first=0)
    psrc[...] = jnp.where(slot == SLOTS - 1, anchor_ref[...], lat_ref[0])
    for t in range(NT):

        @pl.when(tok == t)
        def _():
            wide = wq_ref[...].astype(F32)
            cols = [wide[:, HEAD * (HEADS * i + t) : HEAD * (HEADS * i + t + 1)] for i in range(3)]
            packed = jnp.concatenate(cols + [jnp.zeros((18, 40), F32)], axis=1)
            zw[z] = packed[0:16].astype(BF16)
            zr[z] = packed[16:18]

    grid = lax.broadcasted_iota(jnp.int32, (SIDE, TOKENS), 1)
    line = lax.broadcasted_iota(jnp.int32, (SIDE, TOKENS), 0)
    chosen = [jnp.where(line == (grid >> 5), 1.0, 0.0), jnp.where(line == (grid & 31), 1.0, 0.0)]
    chosen = jnp.concatenate(chosen + [jnp.zeros((64, TOKENS), F32)], axis=0).astype(BF16)
    xs[0:128] = chosen
    xs[128:256] = chosen
    po[...] = jnp.zeros((PIECE, 128), F32)
    for c in range(2):

        @pl.when(core == c)
        def _():
            wide = wo_ref[...].astype(F32)
            for i in range(5 - c):
                k = 5 * c + i
                po[CHUNK * i : CHUNK * i + CHUNK] = wide[:, 128 * k : 128 * k + 128]

    zo[z] = po[...].astype(BF16)
    pl.semaphore_wait(barrier, NZ - 1 + NX - 1 + NT - 1 + NT)

    def prior_copy(k):
        return remote(psrc, pr.at[tok], pr_send.at[k], pr_recv.at[tok], (after, k))

    def prior_arrival(k):
        return remote(psrc, pr.at[k], pr_send.at[k], pr_recv.at[k], (after, k))

    def zw_copy(k):
        return remote(zw.at[z], zw.at[z], zw_send.at[k], zw_recv.at[k], z_peer(k))

    def zr_copy(k):
        return remote(zr.at[z], zr.at[z], zr_send.at[k], zr_recv.at[k], z_peer(k))

    def zo_copy(k):
        return remote(zo.at[z], zo.at[z], zo_send.at[k], zo_recv.at[k], z_peer(k))

    def wx_copy(k):
        return remote(wx.at[x], wx.at[x], wx_send.at[k], wx_recv.at[k], x_peer(k))

    def ox_copy(k):
        return remote(wob.at[core, x], wob.at[core, x], ox_send.at[k], ox_recv.at[k], x_peer(k))

    def mod_copy(k):
        return remote(mod_s, mod_r.at[tok], mod_send.at[k], mod_recv.at[k], t_peer(k))

    def att_copy(b, k):
        there = lax.rem(tok + k, NT)
        return remote(att_s.at[b, there], att_r.at[b, tok], att_send.at[b, k], att_recv.at[b, k], t_peer(k))

    each(NT, lambda k: prior_copy(k).start(), first=0)

    def start_w(k):
        zw_copy(k).start()
        zr_copy(k).start()

    each(NZ, start_w)

    t_from = jnp.full((1, 128), steps_ref[0, 0].astype(F32))
    t_to = jnp.full((1, 128), steps_ref[0, 1].astype(F32))
    phases = t_from * freq_ref[...]
    features = jnp.concatenate([jnp.cos(phases), jnp.sin(phases)], axis=1)
    high, mid, low = split3(features)
    feats = jnp.concatenate([high, mid, low, jnp.zeros((5, FREQ), F32)], axis=0).astype(BF16)
    row8 = lax.broadcasted_iota(jnp.int32, (8, CLASSES), 0)
    col8 = lax.broadcasted_iota(jnp.int32, (8, CLASSES), 1)
    hot = jnp.zeros((8, CLASSES), F32)
    for b in range(IMAGES):
        hot = hot + jnp.where((row8 == b) & (col8 == labels_ref[b]), 1.0, 0.0)
    classes = jnp.dot(hot.astype(BF16), cls_ref[...], preferred_element_type=F32)
    loads[0].wait()
    parts = jnp.dot(feats, time_w[...], preferred_element_type=F32)
    value = parts[0:1] + parts[1:2] + parts[2:3] + classes
    condition = (value / (1.0 + jnp.exp(-value))).astype(BF16)
    loads[1].wait()
    mod_s[:, 432:512] = jnp.zeros((8, 80), F32)
    mod_s[:, 0:432] = lax.dot_general(
        condition, mod_w[...], (((1,), (1,)), ((), ())), preferred_element_type=F32
    )
    mod_r[tok] = mod_s[...]
    each(NT, lambda k: mod_copy(k).start())

    loads[2].wait()
    inw = inw_ref[...].astype(F32)
    inw = inw - jnp.mean(inw, axis=1, keepdims=True)
    pad = jnp.concatenate([jnp.zeros((64, D), F32), inw, inw, jnp.zeros((56, D), F32)], axis=0)
    centred = table[...] + jnp.transpose(pad)
    table[...] = centred
    high, low = split2(centred)
    tcat[:, 0:128] = high
    tcat[:, 128:256] = low
    inner = jnp.dot(
        jnp.concatenate([inw, inw], axis=0), centred, preferred_element_type=F32, precision=lax.Precision.HIGHEST
    )
    lane = lax.broadcasted_iota(jnp.int32, (8, 128), 1)
    cross = jnp.where(lane < 64, inner, 0.0)
    crosses = jnp.concatenate(list(split3(cross)) + [jnp.zeros((8, 128), F32)], axis=0).astype(BF16)
    crosses = jnp.dot(crosses, xs[0:128], preferred_element_type=F32)
    crosses = (crosses[0:8] + crosses[8:16] + crosses[16:24])[0:CHAN]

    each(NT, lambda k: mod_copy(k).wait())
    for source in range(NT):
        mod_t[source * 432 : source * 432 + 432] = jnp.transpose(mod_r[source])[0:432]
    rows = 128

    def gains(r, carry):
        here = pl.ds(pl.multiple_of(r * rows, rows), rows)
        shift = mod_t[here]
        gain = 1.0 + mod_t[pl.ds(pl.multiple_of(D + r * rows, rows), rows)]
        lanes = lax.broadcasted_iota(jnp.int32, (rows, 128), 1)
        base = table[here]
        for b in range(IMAGES):
            value = jnp.where(lanes == 72, shift[:, b : b + 1], gain[:, b : b + 1] * base)
            high, low = split2(value)
            rb[here, 256 * b : 256 * b + 128] = high
            rb[here, 256 * b + 128 : 256 * b + 256] = low
        return carry

    lax.fori_loop(0, D // rows, gains, 0)
    each(NT, lambda k: prior_arrival(k).wait(), first=0)

    def place(b):
        line = jnp.concatenate([pr[t, b] for t in range(NT)], axis=1)
        high = line.astype(BF16).astype(F32)
        low = line - high
        nought = jnp.zeros((CHAN, TOKENS), F32)
        xs[64:80] = jnp.concatenate([high, low, nought, nought], axis=0).astype(BF16)
        xs[192:208] = jnp.concatenate([high, nought, nought, nought], axis=0).astype(BF16)
        return line

    for b in range(IMAGES):
        line = place(b)
        squares = 2.0 * crosses
        for c in range(CHAN):
            squares = squares + inner[0:CHAN, 64 + c : 65 + c] * line[c : c + 1]
        variance = spread_ref[...] + jnp.sum(line * squares, axis=0, keepdims=True) * (1.0 / D)
        invs[b] = lax.rsqrt(jnp.maximum(variance, 0.0) + 1e-06)
        xo[:, b * 128 : b * 128 + 128] = xs[:, pl.ds(pl.multiple_of(tok * 128, 128), 128)]

    def arrive_w(k):
        zw_copy(k).wait()
        zr_copy(k).wait()

    each(NZ, arrive_w)
    each(NZ, lambda k: zo_copy(k).start())
    for i in range(NZ):
        wf[18 * i : 18 * i + 16] = zw[i].astype(F32)
        wf[18 * i + 16 : 18 * i + 18] = zr[i]
    wx[x] = wf[...].astype(BF16)
    each(NX, lambda k: wx_copy(k).start())
    own[...] = jnp.dot(tcat[...], xo[...], preferred_element_type=F32)
    each(NX, lambda k: wx_copy(k).wait())
    wt[...] = jnp.transpose(wx[...].reshape(D, 256))
    folded = jnp.dot(wt[...], rb[...], preferred_element_type=F32)
    for b in range(IMAGES):
        both = folded[:, 256 * b : 256 * b + 128] + folded[:, 256 * b + 128 : 256 * b + 256]
        high, low = split2(both)
        ab[b, :, 0:128] = high
        ab[b, :, 128:256] = low
        shifts[b] = jnp.broadcast_to(both[:, 72:73], (256, 128))

    factor = math.log2(math.e) / math.sqrt(HEAD)
    block = 256

    def attend(b, carry):
        place(b)
        shift = jnp.concatenate([shifts[b]] * NT, axis=1)
        qkv = jnp.dot(ab[b], xs[...], preferred_element_type=F32) * invs[b] + shift
        queries = jnp.concatenate([qkv[0:HEAD], jnp.zeros((128 - HEAD, TOKENS), F32)], axis=0).astype(BF16)
        keys = jnp.transpose(qkv[HEAD : HEAD + 128]).astype(BF16)
        values = jnp.concatenate([qkv[2 * HEAD : 3 * HEAD], jnp.ones((8, TOKENS), F32)], axis=0).astype(BF16)
        for i in range(TOKENS // block):
            scores = jnp.dot(keys, queries[:, i * block : (i + 1) * block], preferred_element_type=F32)
            weights = jnp.exp2(scores * factor).astype(BF16)
            summed = jnp.dot(values, weights, preferred_element_type=F32)
            out = (summed / summed[HEAD : HEAD + 1]).astype(BF16)
            for t in range(2):
                att_s[b, 2 * i + t] = out[:, t * 128 : t * 128 + 128]
        att_r[b, tok] = att_s[b, tok]
        each(NT, lambda k: att_copy(b, k).start())
        return carry

    lax.fori_loop(0, 1, attend, 0)

    each(NZ, lambda k: zo_copy(k).wait())
    for i in range(NZ):
        base = 9 * i + (HP - HEAD) * (i // 8)
        piece = zo[i].astype(F32)
        for k in range(5):
            of[base : base + CHUNK, 128 * k : 128 * k + 128] = piece[CHUNK * k : CHUNK * k + CHUNK]
    for h in range(2):
        of[h * HP + HEAD : (h + 1) * HP] = jnp.zeros((HP - HEAD, 640), F32)
    wob[core, x] = of[...].astype(BF16)
    each(NX, lambda k: ox_copy(k).start())
    lax.fori_loop(1, 4, attend, 0)
    each(NX, lambda k: ox_copy(k).wait())
    share = remote(wob.at[core], wob.at[core], sib_send, sib_recv, (slot, sibling))
    share.start()
    other = remote(wob.at[1 - core], wob.at[1 - core], sib_send, sib_recv, (slot, sibling))
    each(NT, lambda k: [att_copy(b, k).wait() for b in range(IMAGES)])
    share.wait_send()
    other.wait_recv()

    attended = jnp.concatenate([att_r[b].reshape(HEADS * HP, 128) for b in range(IMAGES)], axis=1)
    contract = (((0,), (0,)), ((), ()))
    emb[0:640] = lax.dot_general(wob[0].reshape(HEADS * HP, 640), attended, contract, preferred_element_type=F32)
    emb[640:D] = lax.dot_general(wob[1].reshape(HEADS * HP, 640)[:, 0:512], attended, contract, preferred_element_type=F32)

    def hidden(r, total):
        here = pl.ds(pl.multiple_of(r * rows, rows), rows)
        gates = mod_t[pl.ds(pl.multiple_of(2 * D + r * rows, rows), rows)]
        sums = []
        for b in range(IMAGES):
            cut = slice(b * 128, b * 128 + 128)
            value = own[here, cut] + gates[:, b : b + 1] * emb[here, cut]
            emb[here, cut] = value
            sums.append(jnp.sum(value.reshape(rows // 8, 8, 128), axis=0))
        return total + jnp.concatenate(sums, axis=1)

    total = lax.fori_loop(0, D // rows, hidden, jnp.zeros((8, HALF), F32))
    mean = jnp.sum(total, axis=0, keepdims=True) * (1.0 / D)

    def square(r, total):
        chunk = emb[pl.ds(pl.multiple_of(r * rows, rows), rows)] - mean
        return total + jnp.sum((chunk * chunk).reshape(rows // 8, 8, HALF), axis=0)

    total = lax.fori_loop(0, D // rows, square, jnp.zeros((8, HALF), F32))
    inverse = lax.rsqrt(jnp.sum(total, axis=0, keepdims=True) * (1.0 / D) + 1e-06)
    final = ((emb[...] - mean) * inverse).astype(BF16)
    predicted = jnp.dot(fw_ref[...], final, preferred_element_type=F32)

    keep, noise, eps = coefficients(t_from, t_to)
    for b in range(IMAGES):
        dr_r[z, b] = (keep - 1.0) * pr[tok, b] + eps * predicted[0:CHAN, b * 128 : b * 128 + 128] + noise * noise_ref[0, b]

    def dr_copy(k):
        return remote(dr_r.at[z], dr_r.at[z], dr_send.at[k], dr_recv.at[k], z_peer(k))

    def tx_copy(k):
        return remote(tx_r.at[x], tx_r.at[x], tx_send.at[k], tx_recv.at[k], x_peer(k))

    each(NZ, lambda k: dr_copy(k).start())
    each(NZ, lambda k: dr_copy(k).wait())
    nothing = jnp.zeros((IMAGES, CHAN, 128), F32)
    whole, reached = nothing, nothing
    for i in range(NZ):
        term = dr_r[i]
        whole = whole + term
        reached = reached + jnp.where(i <= z, term, nothing)
    tx_r[x] = whole
    each(NX, lambda k: tx_copy(k).start())
    each(NX, lambda k: tx_copy(k).wait())
    earlier = nothing
    for i in range(NX):
        earlier = earlier + jnp.where(i < x, tx_r[i], nothing)
    updated = anchor_ref[...] + (earlier + reached)
    upd_ref[0] = updated
    change = updated - lat_ref[0]
    er_s[...] = jnp.sum(change * change, axis=1)
    er_r[tok] = er_s[...]

    def er_copy(k):
        return remote(er_s, er_r.at[tok], er_send.at[k], er_recv.at[k], t_peer(k))

    each(NT, lambda k: er_copy(k).start())
    each(NT, lambda k: er_copy(k).wait())
    summed = jnp.sum(jnp.sum(er_r[...], axis=0), axis=1, keepdims=True) * (1.0 / (CHAN * TOKENS))
    spot = lax.broadcasted_iota(jnp.int32, (IMAGES, 128), 0) == lax.broadcasted_iota(jnp.int32, (IMAGES, 128), 1)
    err_ref[...] = jnp.sum(jnp.where(spot, summed, 0.0), axis=0, keepdims=True)[:, 0:IMAGES]


def body(
    anchor, latents, noise_draws, slot_steps, class_labels, in_weight, time_weight, class_table,
    mod_weight, qkv_weight, out_weight, final_weight,
):
    table, spread, freq = (jnp.asarray(value) for value in position_constants())
    vmem = pl.BlockSpec(memory_space=pltpu.VMEM)
    anywhere = pl.BlockSpec(memory_space=pl.ANY)
    dma = pltpu.SemaphoreType.DMA
    updated, errors = pl.pallas_call(
        kernel,
        out_shape=(
            jax.ShapeDtypeStruct((1, IMAGES, CHAN, 128), F32),
            jax.ShapeDtypeStruct((1, IMAGES), F32),
        ),
        in_specs=[pl.BlockSpec(memory_space=pltpu.SMEM)] * 2 + [vmem] * 10 + [anywhere] * 3,
        out_specs=(vmem, vmem),
        scratch_shapes=[
            pltpu.VMEM((FREQ, D), BF16),
            pltpu.VMEM((432, D), BF16),
            pltpu.VMEM((D, 128), F32),
            pltpu.VMEM((D, 256), BF16),
            pltpu.VMEM((256, TOKENS), BF16),
            pltpu.VMEM((256, HALF), BF16),
            pltpu.VMEM((IMAGES, CHAN, 128), F32),
            pltpu.VMEM((NT, IMAGES, CHAN, 128), F32),
            pltpu.VMEM((8, 512), F32),
            pltpu.VMEM((NT, 8, 512), F32),
            pltpu.VMEM((3 * D, 8), F32),
            pltpu.VMEM((D, 256 * IMAGES), BF16),
            pltpu.VMEM((IMAGES, 256, 256), BF16),
            pltpu.VMEM((IMAGES, 256, 128), F32),
            pltpu.VMEM((NZ, 16, 256), BF16),
            pltpu.VMEM((NZ, 2, 256), F32),
            pltpu.VMEM((18 * NZ, 256), F32),
            pltpu.VMEM((NX, 18 * NZ, 256), BF16),
            pltpu.VMEM((256, D), BF16),
            pltpu.VMEM((NZ, PIECE, 128), BF16),
            pltpu.VMEM((PIECE, 128), F32),
            pltpu.VMEM((2 * HP, 640), F32),
            pltpu.VMEM((2, NX, 2 * HP, 640), BF16),
            pltpu.VMEM((D, HALF), F32),
            pltpu.VMEM((D, HALF), F32),
            pltpu.VMEM((IMAGES, NT, HP, 128), BF16),
            pltpu.VMEM((IMAGES, NT, HP, 128), BF16),
            pltpu.VMEM((NZ, IMAGES, CHAN, 128), F32),
            pltpu.VMEM((NX, IMAGES, CHAN, 128), F32),
            pltpu.VMEM((NT, IMAGES, 128), F32),
            pltpu.VMEM((IMAGES, 128), F32),
            pltpu.VMEM((IMAGES, 1, TOKENS), F32),
            dma((3,)),
            dma((NT,)), dma((NT,)),
            dma((NT,)), dma((NT,)),
            dma((NZ,)), dma((NZ,)),
            dma((NZ,)), dma((NZ,)),
            dma((NX,)), dma((NX,)),
            dma((NZ,)), dma((NZ,)),
            dma((NX,)), dma((NX,)),
            dma, dma,
            dma((IMAGES, NT)), dma((IMAGES, NT)),
            dma((NZ,)), dma((NZ,)),
            dma((NX,)), dma((NX,)),
            dma((NT,)), dma((NT,)),
        ],
        compiler_params=pltpu.CompilerParams(
            collective_id=0, has_side_effects=True, vmem_limit_bytes=56 * 1024 * 1024
        ),
        cost_estimate=pl.CostEstimate(flops=6_000_000_000, bytes_accessed=8_000_000, transcendentals=4_200_000),
    )(
        slot_steps, class_labels, latents, anchor, noise_draws, freq, class_table, final_weight, in_weight, spread,
        qkv_weight, out_weight, time_weight, mod_weight.T, table,
    )
    return updated, errors


def solution(mesh):
    in_specs = (
        P(None, None, "tok"),
        P("tm", None, None, "tok"),
        P("tm", None, None, "tok"),
        P("tm", None),
        P(),
        P(),
        P(),
        P(),
        P(None, "tok"),
        P("tm", None),
        P("tm", None),
        P(),
    )
    out_specs = (P("tm", None, None, "tok"), P("tm", None))
    return jax.shard_map(body, mesh=mesh, in_specs=in_specs, out_specs=out_specs, check_vma=False)
```

```python
import math

import jax
import jax.numpy as jnp
import ml_dtypes
import numpy as np
from jax import lax
from jax.experimental import pallas as pl
from jax.experimental.pallas import tpu as pltpu
from jax.sharding import PartitionSpec as P

MESH = pl.DeviceIdType.MESH
D = 1152
HEAD = 72
HEADS = 8
CHAN = 4
CLASSES = 1000
FREQ = 256
SIDE = 32
TOKENS = 1024
IMAGES = 4
NX, NZ, NT = 4, 16, 8
SLOTS = NX * NZ
HP = 80
CHUNK = 9
PIECE = 48
HALF = 512
F32 = jnp.float32
BF16 = jnp.bfloat16


def split3(values):
    high = values.astype(BF16).astype(F32)
    rest = values - high
    mid = rest.astype(BF16).astype(F32)
    return high, mid, rest - mid


def split2(values):
    high = values.astype(BF16)
    return high, (values - high.astype(F32)).astype(BF16)


def position_constants():
    quarter = D // 4
    angular = np.exp(np.float32(-math.log(10000.0)) * np.arange(quarter, dtype=np.float32) / np.float32(quarter)).astype(np.float32)
    angles = (np.arange(SIDE, dtype=np.float32)[:, None] * angular[None, :]).astype(np.float64)
    pair = np.concatenate([np.sin(angles), np.cos(angles)], axis=1)
    table = np.zeros((D, 128))
    table[: D // 2, 0:SIDE] = pair.T
    table[D // 2 :, SIDE : 2 * SIDE] = pair.T
    table = table - table.mean(axis=0, keepdims=True)
    tokens = np.arange(TOKENS)
    spread = (table[:, tokens // SIDE] + table[:, SIDE + tokens % SIDE]) ** 2
    half_freq = FREQ // 2
    freq = np.exp(-math.log(10000.0) * np.arange(half_freq) / half_freq)
    return (
        table.astype(np.float32),
        spread.mean(axis=0)[None, :].astype(np.float32),
        freq[None, :].astype(np.float32),
    )


def signal_level(step_value):
    return 0.005 + 0.99 * jnp.cos(0.4 * math.pi * step_value / 1000.0) ** 2


def coefficients(t_from, t_to):
    level_from = signal_level(t_from)
    level_to = signal_level(t_to)
    keep_coef = jnp.sqrt(level_to / level_from)
    noise_coef = 0.5 * jnp.sqrt((1.0 - level_to) / (1.0 - level_from)) * jnp.sqrt(1.0 - level_from / level_to)
    eps_coef = jnp.sqrt(1.0 - level_to - noise_coef * noise_coef) - keep_coef * jnp.sqrt(1.0 - level_from)
    return (keep_coef, noise_coef, eps_coef)


def kernel(
    steps_ref, labels_ref, lat_ref, anchor_ref, noise_ref, freq_ref, cls_ref, fw_ref, inw_ref, spread_ref,
    wq_ref, wo_ref, time_hbm, mod_hbm, table_hbm,
    out_ref,
    time_w, mod_w, table, tcat, xs, xo, psrc, pr, mod_s, mod_r, mod_t, rb, ab, shifts,
    zw, zr, wf, wx, wt, zo, po, of, wob, emb, own, att_s, att_r,
    dr_r, sc_s, sc_r, tx_r, er_r, er_s, invs,
    loc_sem, pr_send, pr_recv, mod_send, mod_recv, zw_send, zw_recv, zr_send, zr_recv,
    wx_send, wx_recv, zo_send, zo_recv, ox_send, ox_recv, sib_send, sib_recv,
    att_send, att_recv, dr_send, dr_recv, tx_send, tx_recv, er_send, er_recv,
):
    slot = lax.axis_index("tm")
    tok = lax.axis_index("tok")
    x = lax.div(slot, NZ)
    z = lax.rem(slot, NZ)
    core = lax.rem(tok, 2)
    sibling = tok + 1 - 2 * core

    kind, turn = lax.rem(z, 4), lax.div(z, 4)
    place_z = 4 * kind + turn
    family = pl.ds(pl.multiple_of(4 * kind, 4), 4)
    near = (0, 1, NZ - 1, 2)

    def z_peer(k):
        return (x * NZ + lax.rem(z + k, NZ), tok)

    def x_peer(k):
        return (lax.rem(x + k, NX) * NZ + z, tok)

    def t_peer(k):
        return (slot, lax.rem(tok + k, NT))

    def each(count, action, first=1):
        for k in range(first, count):
            action(k)

    def remote(src, dst, send, recv, device):
        return pltpu.make_async_remote_copy(
            src_ref=src, dst_ref=dst, send_sem=send, recv_sem=recv, device_id=device, device_id_type=MESH
        )

    loads = [
        pltpu.make_async_copy(time_hbm, time_w, loc_sem.at[0]),
        pltpu.make_async_copy(mod_hbm, mod_w, loc_sem.at[1]),
        pltpu.make_async_copy(table_hbm, table, loc_sem.at[2]),
    ]
    for load in loads:
        load.start()

    barrier = pltpu.get_barrier_semaphore()

    def greet(device):
        pl.semaphore_signal(barrier, inc=1, device_id=device, device_id_type=MESH)

    each(4, lambda k: greet(z_peer(4 * k)))
    each(4, lambda k: greet(z_peer(NZ - near[k])))
    each(NX, lambda k: greet(x_peer(k)))
    each(NT, lambda k: greet(t_peer(k)))
    before = lax.rem(slot + SLOTS - 1, SLOTS)
    after = lax.rem(slot + 1, SLOTS)
    each(NT, lambda k: greet((before, k)), first=0)
    psrc[...] = jnp.where(slot == SLOTS - 1, anchor_ref[...], lat_ref[0])
    for t in range(NT):

        @pl.when(tok == t)
        def _():
            wide = wq_ref[...].astype(F32)
            cols = [wide[:, HEAD * (HEADS * i + t) : HEAD * (HEADS * i + t + 1)] for i in range(3)]
            packed = jnp.concatenate(cols + [jnp.zeros((18, 40), F32)], axis=1)
            zw[place_z] = packed[0:16].astype(BF16)
            zr[place_z] = packed[16:18]

    grid = lax.broadcasted_iota(jnp.int32, (SIDE, TOKENS), 1)
    line = lax.broadcasted_iota(jnp.int32, (SIDE, TOKENS), 0)
    chosen = [jnp.where(line == (grid >> 5), 1.0, 0.0), jnp.where(line == (grid & 31), 1.0, 0.0)]
    chosen = jnp.concatenate(chosen + [jnp.zeros((64, TOKENS), F32)], axis=0).astype(BF16)
    xs[0:128] = chosen
    xs[128:256] = chosen
    po[...] = jnp.zeros((PIECE, 128), F32)
    for c in range(2):

        @pl.when(core == c)
        def _():
            wide = wo_ref[...].astype(F32)
            for i in range(5 - c):
                k = 5 * c + i
                po[CHUNK * i : CHUNK * i + CHUNK] = wide[:, 128 * k : 128 * k + 128]

    zo[place_z] = po[...].astype(BF16)
    pl.semaphore_wait(barrier, 3 + 3 + NX - 1 + NT - 1 + NT)

    def prior_copy(k):
        return remote(psrc, pr.at[tok], pr_send.at[k], pr_recv.at[tok], (after, k))

    def prior_arrival(k):
        return remote(psrc, pr.at[k], pr_send.at[k], pr_recv.at[k], (after, k))

    def far_copies(pairs, k):
        return [
            remote(ref.at[place_z], ref.at[place_z], send.at[k], recv.at[k], z_peer(4 * k)) for ref, send, recv in pairs
        ]

    def near_copies(pairs, k):
        return [
            remote(ref.at[family], ref.at[family], send.at[3 + k], recv.at[3 + k], z_peer(near[k]))
            for ref, send, recv in pairs
        ]

    w_pairs = [(zw, zw_send, zw_recv), (zr, zr_send, zr_recv)]
    o_pairs = [(zo, zo_send, zo_recv)]

    def start(copies):
        for copy in copies:
            copy.start()

    def finish(copies):
        for copy in copies:
            copy.wait()

    def wx_copy(k):
        return remote(wx.at[x], wx.at[x], wx_send.at[k], wx_recv.at[k], x_peer(k))

    def ox_copy(k):
        return remote(wob.at[core, x], wob.at[core, x], ox_send.at[k], ox_recv.at[k], x_peer(k))

    def mod_copy(k):
        return remote(mod_s, mod_r.at[tok], mod_send.at[k], mod_recv.at[k], t_peer(k))

    def att_copy(b, k):
        there = lax.rem(tok + k, NT)
        return remote(att_s.at[b, there], att_r.at[b, tok], att_send.at[b, k], att_recv.at[b, k], t_peer(k))

    each(NT, lambda k: prior_copy(k).start(), first=0)

    each(4, lambda k: start(far_copies(w_pairs, k)))

    t_from = jnp.full((1, 128), steps_ref[0, 0].astype(F32))
    t_to = jnp.full((1, 128), steps_ref[0, 1].astype(F32))
    phases = t_from * freq_ref[...]
    features = jnp.concatenate([jnp.cos(phases), jnp.sin(phases)], axis=1)
    high, mid, low = split3(features)
    feats = jnp.concatenate([high, mid, low, jnp.zeros((5, FREQ), F32)], axis=0).astype(BF16)
    row8 = lax.broadcasted_iota(jnp.int32, (8, CLASSES), 0)
    col8 = lax.broadcasted_iota(jnp.int32, (8, CLASSES), 1)
    hot = jnp.zeros((8, CLASSES), F32)
    for b in range(IMAGES):
        hot = hot + jnp.where((row8 == b) & (col8 == labels_ref[b]), 1.0, 0.0)
    classes = jnp.dot(hot.astype(BF16), cls_ref[...], preferred_element_type=F32)
    loads[0].wait()
    parts = jnp.dot(feats, time_w[...], preferred_element_type=F32)
    value = parts[0:1] + parts[1:2] + parts[2:3] + classes
    condition = (value / (1.0 + jnp.exp(-value))).astype(BF16)
    loads[1].wait()
    mod_s[:, 432:512] = jnp.zeros((8, 80), F32)
    mod_s[:, 0:432] = lax.dot_general(
        condition, mod_w[...], (((1,), (1,)), ((), ())), preferred_element_type=F32
    )
    mod_r[tok] = mod_s[...]
    each(NT, lambda k: mod_copy(k).start())
    each(4, lambda k: finish(far_copies(w_pairs, k)))
    each(4, lambda k: start(near_copies(w_pairs, k)))

    loads[2].wait()
    inw = inw_ref[...].astype(F32)
    inw = inw - jnp.mean(inw, axis=1, keepdims=True)
    pad = jnp.concatenate([jnp.zeros((64, D), F32), inw, inw, jnp.zeros((56, D), F32)], axis=0)
    centred = table[...] + jnp.transpose(pad)
    table[...] = centred
    high, low = split2(centred)
    tcat[:, 0:128] = high
    tcat[:, 128:256] = low
    inner = jnp.dot(
        jnp.concatenate([inw, inw], axis=0), centred, preferred_element_type=F32, precision=lax.Precision.HIGHEST
    )
    lane = lax.broadcasted_iota(jnp.int32, (8, 128), 1)
    cross = jnp.where(lane < 64, inner, 0.0)
    crosses = jnp.concatenate(list(split3(cross)) + [jnp.zeros((8, 128), F32)], axis=0).astype(BF16)
    crosses = jnp.dot(crosses, xs[0:128], preferred_element_type=F32)
    crosses = (crosses[0:8] + crosses[8:16] + crosses[16:24])[0:CHAN]

    each(NT, lambda k: mod_copy(k).wait())
    for source in range(NT):
        mod_t[source * 432 : source * 432 + 432] = jnp.transpose(mod_r[source])[0:432]

    each(4, lambda k: finish(near_copies(w_pairs, k)))
    each(4, lambda k: start(far_copies(o_pairs, k)))
    for i in range(NZ):
        member = 4 * (i % 4) + i // 4
        wf[18 * i : 18 * i + 16] = zw[member].astype(F32)
        wf[18 * i + 16 : 18 * i + 18] = zr[member]
    wx[x] = wf[...].astype(BF16)
    each(NX, lambda k: wx_copy(k).start())
    rows = 128

    def gains(r, carry):
        here = pl.ds(pl.multiple_of(r * rows, rows), rows)
        shift = mod_t[here]
        gain = 1.0 + mod_t[pl.ds(pl.multiple_of(D + r * rows, rows), rows)]
        lanes = lax.broadcasted_iota(jnp.int32, (rows, 128), 1)
        base = table[here]
        for b in range(IMAGES):
            value = jnp.where(lanes == 72, shift[:, b : b + 1], gain[:, b : b + 1] * base)
            high, low = split2(value)
            rb[here, 256 * b : 256 * b + 128] = high
            rb[here, 256 * b + 128 : 256 * b + 256] = low
        return carry

    lax.fori_loop(0, D // rows, gains, 0)
    each(4, lambda k: finish(far_copies(o_pairs, k)))
    each(4, lambda k: start(near_copies(o_pairs, k)))
    each(NT, lambda k: prior_arrival(k).wait(), first=0)

    def place(b):
        line = jnp.concatenate([pr[t, b] for t in range(NT)], axis=1)
        high = line.astype(BF16).astype(F32)
        low = line - high
        nought = jnp.zeros((CHAN, TOKENS), F32)
        xs[64:80] = jnp.concatenate([high, low, nought, nought], axis=0).astype(BF16)
        xs[192:208] = jnp.concatenate([high, nought, nought, nought], axis=0).astype(BF16)
        return line

    for b in range(IMAGES):
        line = place(b)
        squares = 2.0 * crosses
        for c in range(CHAN):
            squares = squares + inner[0:CHAN, 64 + c : 65 + c] * line[c : c + 1]
        variance = spread_ref[...] + jnp.sum(line * squares, axis=0, keepdims=True) * (1.0 / D)
        invs[b] = lax.rsqrt(jnp.maximum(variance, 0.0) + 1e-06)
        xo[:, b * 128 : b * 128 + 128] = xs[:, pl.ds(pl.multiple_of(tok * 128, 128), 128)]

    own[...] = jnp.dot(tcat[...], xo[...], preferred_element_type=F32)
    each(4, lambda k: finish(near_copies(o_pairs, k)))
    for i in range(NZ):
        base = 9 * i + (HP - HEAD) * (i // 8)
        piece = zo[4 * (i % 4) + i // 4].astype(F32)
        for k in range(5):
            of[base : base + CHUNK, 128 * k : 128 * k + 128] = piece[CHUNK * k : CHUNK * k + CHUNK]
    for h in range(2):
        of[h * HP + HEAD : (h + 1) * HP] = jnp.zeros((HP - HEAD, 640), F32)
    wob[core, x] = of[...].astype(BF16)
    each(NX, lambda k: wx_copy(k).wait())
    each(NX, lambda k: ox_copy(k).start())
    wt[...] = jnp.transpose(wx[...].reshape(D, 256))
    folded = jnp.dot(wt[...], rb[...], preferred_element_type=F32)
    for b in range(IMAGES):
        both = folded[:, 256 * b : 256 * b + 128] + folded[:, 256 * b + 128 : 256 * b + 256]
        high, low = split2(both)
        ab[b, :, 0:128] = high
        ab[b, :, 128:256] = low
        shifts[b] = jnp.broadcast_to(both[:, 72:73], (256, 128))

    factor = math.log2(math.e) / math.sqrt(HEAD)
    block = 256

    def attend(b, carry):
        place(b)
        shift = jnp.concatenate([shifts[b]] * NT, axis=1)
        qkv = jnp.dot(ab[b], xs[...], preferred_element_type=F32) * invs[b] + shift
        queries = jnp.concatenate([qkv[0:HEAD], jnp.zeros((128 - HEAD, TOKENS), F32)], axis=0).astype(BF16)
        keys = jnp.transpose(qkv[HEAD : HEAD + 128]).astype(BF16)
        values = jnp.concatenate([qkv[2 * HEAD : 3 * HEAD], jnp.ones((8, TOKENS), F32)], axis=0).astype(BF16)
        for i in range(TOKENS // block):
            scores = jnp.dot(keys, queries[:, i * block : (i + 1) * block], preferred_element_type=F32)
            weights = jnp.exp2(scores * factor).astype(BF16)
            summed = jnp.dot(values, weights, preferred_element_type=F32)
            out = (summed * (1.0 / summed[HEAD : HEAD + 1])).astype(BF16)
            for t in range(2):
                att_s[b, 2 * i + t] = out[:, t * 128 : t * 128 + 128]
        att_r[b, tok] = att_s[b, tok]
        each(NT, lambda k: att_copy(b, k).start())
        return carry

    lax.fori_loop(0, 3, attend, 0)
    each(NX, lambda k: ox_copy(k).wait())
    share = remote(wob.at[core], wob.at[core], sib_send, sib_recv, (slot, sibling))
    share.start()
    other = remote(wob.at[1 - core], wob.at[1 - core], sib_send, sib_recv, (slot, sibling))
    lax.fori_loop(3, 4, attend, 0)
    each(NT, lambda k: [att_copy(b, k).wait() for b in range(IMAGES)])
    share.wait_send()
    other.wait_recv()

    attended = jnp.concatenate([att_r[b].reshape(HEADS * HP, 128) for b in range(IMAGES)], axis=1)
    contract = (((0,), (0,)), ((), ()))
    emb[0:640] = lax.dot_general(wob[0].reshape(HEADS * HP, 640), attended, contract, preferred_element_type=F32)
    emb[640:D] = lax.dot_general(wob[1].reshape(HEADS * HP, 640)[:, 0:512], attended, contract, preferred_element_type=F32)

    def hidden(r, total):
        here = pl.ds(pl.multiple_of(r * rows, rows), rows)
        gates = mod_t[pl.ds(pl.multiple_of(2 * D + r * rows, rows), rows)]
        sums = []
        for b in range(IMAGES):
            cut = slice(b * 128, b * 128 + 128)
            value = own[here, cut] + gates[:, b : b + 1] * emb[here, cut]
            emb[here, cut] = value
            sums.append(jnp.sum(value.reshape(rows // 8, 8, 128), axis=0))
        return total + jnp.concatenate(sums, axis=1)

    total = lax.fori_loop(0, D // rows, hidden, jnp.zeros((8, HALF), F32))
    mean = jnp.sum(total, axis=0, keepdims=True) * (1.0 / D)

    def square(r, total):
        chunk = emb[pl.ds(pl.multiple_of(r * rows, rows), rows)] - mean
        return total + jnp.sum((chunk * chunk).reshape(rows // 8, 8, HALF), axis=0)

    total = lax.fori_loop(0, D // rows, square, jnp.zeros((8, HALF), F32))
    inverse = lax.rsqrt(jnp.sum(total, axis=0, keepdims=True) * (1.0 / D) + 1e-06)
    final = ((emb[...] - mean) * inverse).astype(BF16)
    predicted = jnp.dot(fw_ref[...], final, preferred_element_type=F32)

    keep, noise, eps = coefficients(t_from, t_to)
    for b in range(IMAGES):
        dr_r[turn, b] = (keep - 1.0) * pr[tok, b] + eps * predicted[0:CHAN, b * 128 : b * 128 + 128] + noise * noise_ref[0, b]

    def dr_copy(k):
        return remote(dr_r.at[turn], dr_r.at[turn], dr_send.at[k], dr_recv.at[k], z_peer(4 * k))

    def sc_copy(k):
        return remote(sc_s.at[k], sc_r.at[k], dr_send.at[3 + k], dr_recv.at[3 + k], z_peer(near[k]))

    def tx_copy(k):
        return remote(tx_r.at[x], tx_r.at[x], tx_send.at[k], tx_recv.at[k], x_peer(k))

    each(4, lambda k: dr_copy(k).start())
    each(4, lambda k: dr_copy(k).wait())
    nothing = jnp.zeros((IMAGES, CHAN, 128), F32)

    def upto(last):
        total = nothing
        for i in range(4):
            total = total + jnp.where(i <= last, dr_r[i], nothing)
        return total

    whole = upto(3)
    for k in range(1, 4):
        there = lax.rem(z + near[k], NZ)
        sc_s[k, 0] = upto(lax.div(there, 4) - jnp.where(kind > lax.rem(there, 4), 1, 0))
        sc_s[k, 1] = whole
    each(4, lambda k: sc_copy(k).start())
    reached = upto(turn)
    for k in range(1, 4):
        sc_copy(k).wait()
    for k in range(1, 4):
        reached = reached + sc_r[k, 0]
        whole = whole + sc_r[k, 1]
    tx_r[x] = whole
    each(NX, lambda k: tx_copy(k).start())
    each(NX, lambda k: tx_copy(k).wait())
    earlier = nothing
    for i in range(NX):
        earlier = earlier + jnp.where(i < x, tx_r[i], nothing)
    updated = anchor_ref[...] + (earlier + reached)
    out_ref[:, 0:CHAN] = updated
    change = updated - lat_ref[0]
    er_s[...] = jnp.sum(change * change, axis=1)
    er_r[tok] = er_s[...]

    def er_copy(k):
        return remote(er_s, er_r.at[tok], er_send.at[k], er_recv.at[k], t_peer(k))

    each(NT, lambda k: er_copy(k).start())
    each(NT, lambda k: er_copy(k).wait())
    summed = jnp.sum(jnp.sum(er_r[...], axis=0), axis=1, keepdims=True) * (1.0 / (CHAN * TOKENS))
    for b in range(IMAGES):
        out_ref[b, CHAN:8] = jnp.broadcast_to(summed[b : b + 1], (CHAN, 128))


def body(
    anchor, latents, noise_draws, slot_steps, class_labels, in_weight, time_weight, class_table,
    mod_weight, qkv_weight, out_weight, final_weight,
):
    table, spread, freq = (jnp.asarray(value) for value in position_constants())
    vmem = pl.BlockSpec(memory_space=pltpu.VMEM)
    anywhere = pl.BlockSpec(memory_space=pl.ANY)
    dma = pltpu.SemaphoreType.DMA
    result = pl.pallas_call(
        kernel,
        out_shape=jax.ShapeDtypeStruct((IMAGES, 8, 128), F32),
        in_specs=[pl.BlockSpec(memory_space=pltpu.SMEM)] * 2 + [vmem] * 10 + [anywhere] * 3,
        out_specs=vmem,
        scratch_shapes=[
            pltpu.VMEM((FREQ, D), BF16),
            pltpu.VMEM((432, D), BF16),
            pltpu.VMEM((D, 128), F32),
            pltpu.VMEM((D, 256), BF16),
            pltpu.VMEM((256, TOKENS), BF16),
            pltpu.VMEM((256, HALF), BF16),
            pltpu.VMEM((IMAGES, CHAN, 128), F32),
            pltpu.VMEM((NT, IMAGES, CHAN, 128), F32),
            pltpu.VMEM((8, 512), F32),
            pltpu.VMEM((NT, 8, 512), F32),
            pltpu.VMEM((3 * D, 8), F32),
            pltpu.VMEM((D, 256 * IMAGES), BF16),
            pltpu.VMEM((IMAGES, 256, 256), BF16),
            pltpu.VMEM((IMAGES, 256, 128), F32),
            pltpu.VMEM((NZ, 16, 256), BF16),
            pltpu.VMEM((NZ, 2, 256), F32),
            pltpu.VMEM((18 * NZ, 256), F32),
            pltpu.VMEM((NX, 18 * NZ, 256), BF16),
            pltpu.VMEM((256, D), BF16),
            pltpu.VMEM((NZ, PIECE, 128), BF16),
            pltpu.VMEM((PIECE, 128), F32),
            pltpu.VMEM((2 * HP, 640), F32),
            pltpu.VMEM((2, NX, 2 * HP, 640), BF16),
            pltpu.VMEM((D, HALF), F32),
            pltpu.VMEM((D, HALF), F32),
            pltpu.VMEM((IMAGES, NT, HP, 128), BF16),
            pltpu.VMEM((IMAGES, NT, HP, 128), BF16),
            pltpu.VMEM((4, IMAGES, CHAN, 128), F32),
            pltpu.VMEM((4, 2, IMAGES, CHAN, 128), F32),
            pltpu.VMEM((4, 2, IMAGES, CHAN, 128), F32),
            pltpu.VMEM((NX, IMAGES, CHAN, 128), F32),
            pltpu.VMEM((NT, IMAGES, 128), F32),
            pltpu.VMEM((IMAGES, 128), F32),
            pltpu.VMEM((IMAGES, 1, TOKENS), F32),
            dma((3,)),
            dma((NT,)), dma((NT,)),
            dma((NT,)), dma((NT,)),
            dma((8,)), dma((8,)),
            dma((8,)), dma((8,)),
            dma((NX,)), dma((NX,)),
            dma((8,)), dma((8,)),
            dma((NX,)), dma((NX,)),
            dma, dma,
            dma((IMAGES, NT)), dma((IMAGES, NT)),
            dma((8,)), dma((8,)),
            dma((NX,)), dma((NX,)),
            dma((NT,)), dma((NT,)),
        ],
        compiler_params=pltpu.CompilerParams(
            collective_id=0, has_side_effects=True, vmem_limit_bytes=56 * 1024 * 1024
        ),
        cost_estimate=pl.CostEstimate(flops=6_000_000_000, bytes_accessed=8_000_000, transcendentals=4_200_000),
    )(
        slot_steps, class_labels, latents, anchor, noise_draws, freq, class_table, final_weight, in_weight, spread,
        qkv_weight, out_weight, time_weight, mod_weight.T, table,
    )
    return result[None, :, 0:CHAN], result[None, :, CHAN, 0]


def solution(mesh):
    in_specs = (
        P(None, None, "tok"),
        P("tm", None, None, "tok"),
        P("tm", None, None, "tok"),
        P("tm", None),
        P(),
        P(),
        P(),
        P(),
        P(None, "tok"),
        P("tm", None),
        P("tm", None),
        P(),
    )
    out_specs = (P("tm", None, None, "tok"), P("tm", None))
    return jax.shard_map(body, mesh=mesh, in_specs=in_specs, out_specs=out_specs, check_vma=False)
```

```python
import math

import jax
import jax.numpy as jnp
import ml_dtypes
import numpy as np
from jax import lax
from jax.experimental import pallas as pl
from jax.experimental.pallas import tpu as pltpu
from jax.sharding import PartitionSpec as P

MESH = pl.DeviceIdType.MESH
D = 1152
HEAD = 72
HEADS = 8
CHAN = 4
CLASSES = 1000
FREQ = 256
SIDE = 32
TOKENS = 1024
IMAGES = 4
NX, NZ, NT = 4, 16, 8
SLOTS = NX * NZ
HP = 80
CHUNK = 9
PIECE = 48
HALF = 512
F32 = jnp.float32
BF16 = jnp.bfloat16


def split3(values):
    high = values.astype(BF16).astype(F32)
    rest = values - high
    mid = rest.astype(BF16).astype(F32)
    return high, mid, rest - mid


def split2(values):
    high = values.astype(BF16)
    return high, (values - high.astype(F32)).astype(BF16)


def position_constants():
    quarter = D // 4
    angular = np.exp(np.float32(-math.log(10000.0)) * np.arange(quarter, dtype=np.float32) / np.float32(quarter)).astype(np.float32)
    angles = (np.arange(SIDE, dtype=np.float32)[:, None] * angular[None, :]).astype(np.float64)
    pair = np.concatenate([np.sin(angles), np.cos(angles)], axis=1)
    table = np.zeros((D, 128))
    table[: D // 2, 0:SIDE] = pair.T
    table[D // 2 :, SIDE : 2 * SIDE] = pair.T
    table = table - table.mean(axis=0, keepdims=True)
    tokens = np.arange(TOKENS)
    spread = (table[:, tokens // SIDE] + table[:, SIDE + tokens % SIDE]) ** 2
    half_freq = FREQ // 2
    freq = np.exp(-math.log(10000.0) * np.arange(half_freq) / half_freq)
    return (
        table.astype(np.float32),
        spread.mean(axis=0)[None, :].astype(np.float32),
        freq[None, :].astype(np.float32),
    )


def signal_level(step_value):
    return 0.005 + 0.99 * jnp.cos(0.4 * math.pi * step_value / 1000.0) ** 2


def coefficients(t_from, t_to):
    level_from = signal_level(t_from)
    level_to = signal_level(t_to)
    keep_coef = jnp.sqrt(level_to / level_from)
    noise_coef = 0.5 * jnp.sqrt((1.0 - level_to) / (1.0 - level_from)) * jnp.sqrt(1.0 - level_from / level_to)
    eps_coef = jnp.sqrt(1.0 - level_to - noise_coef * noise_coef) - keep_coef * jnp.sqrt(1.0 - level_from)
    return (keep_coef, noise_coef, eps_coef)


def kernel(
    steps_ref, labels_ref, lat_ref, anchor_ref, noise_ref, freq_ref, cls_ref, fw_ref, inw_ref, spread_ref,
    wq_ref, wo_ref, time_hbm, mod_hbm, table_hbm,
    upd_ref, err_ref,
    time_w, mod_w, table, tcat, xs, xo, psrc, pr, mod_s, mod_r, gain_rows, gate_t, ab, shifts,
    zw, zr, wf, wx, wt, zo, po, of, wob, wot, emb, own, query_s, key_s, value_s, att_s, att_r,
    dr_r, tx_r, er_r, er_s, invs,
    loc_sem, pr_send, pr_recv, mod_send, mod_recv, zw_send, zw_recv, zr_send, zr_recv,
    wx_send, wx_recv, zo_send, zo_recv, ox_send, ox_recv, sib_send, sib_recv,
    att_send, att_recv, dr_send, dr_recv, tx_send, tx_recv, er_send, er_recv,
):
    slot = lax.axis_index("tm")
    tok = lax.axis_index("tok")
    x = lax.div(slot, NZ)
    z = lax.rem(slot, NZ)
    core = lax.rem(tok, 2)
    sibling = tok + 1 - 2 * core

    def z_peer(k):
        return (x * NZ + lax.rem(z + k, NZ), tok)

    def x_peer(k):
        return (lax.rem(x + k, NX) * NZ + z, tok)

    def t_peer(k):
        return (slot, lax.rem(tok + k, NT))

    def each(count, action, first=1):
        def step(k, carry):
            action(k)
            return carry

        lax.fori_loop(first, count, step, 0)

    def remote(src, dst, send, recv, device):
        return pltpu.make_async_remote_copy(
            src_ref=src, dst_ref=dst, send_sem=send, recv_sem=recv, device_id=device, device_id_type=MESH
        )

    loads = [
        pltpu.make_async_copy(time_hbm, time_w, loc_sem.at[0]),
        pltpu.make_async_copy(mod_hbm, mod_w, loc_sem.at[1]),
        pltpu.make_async_copy(table_hbm, table, loc_sem.at[2]),
    ]
    for load in loads:
        load.start()

    barrier = pltpu.get_barrier_semaphore()

    def greet(device):
        pl.semaphore_signal(barrier, inc=1, device_id=device, device_id_type=MESH)

    each(NZ, lambda k: greet(z_peer(k)))
    each(NX, lambda k: greet(x_peer(k)))
    each(NT, lambda k: greet(t_peer(k)))
    before = lax.rem(slot + SLOTS - 1, SLOTS)
    after = lax.rem(slot + 1, SLOTS)
    each(NT, lambda k: greet((before, k)), first=0)
    psrc[...] = jnp.where(slot == SLOTS - 1, anchor_ref[...], lat_ref[0])
    for t in range(NT):

        @pl.when(tok == t)
        def _():
            wide = wq_ref[...].astype(F32)
            cols = [wide[:, HEAD * (HEADS * i + t) : HEAD * (HEADS * i + t + 1)] for i in range(3)]
            packed = jnp.concatenate(cols + [jnp.zeros((18, 40), F32)], axis=1)
            zw[z] = packed[0:16].astype(BF16)
            zr[z] = packed[16:18]

    pl.semaphore_wait(barrier, NZ - 1 + NX - 1 + NT - 1 + NT)

    def prior_copy(k):
        return remote(psrc, pr.at[tok], pr_send.at[k], pr_recv.at[tok], (after, k))

    def prior_arrival(k):
        return remote(psrc, pr.at[k], pr_send.at[k], pr_recv.at[k], (after, k))

    def zw_copy(k):
        return remote(zw.at[z], zw.at[z], zw_send.at[k], zw_recv.at[k], z_peer(k))

    def zr_copy(k):
        return remote(zr.at[z], zr.at[z], zr_send.at[k], zr_recv.at[k], z_peer(k))

    def zo_copy(k):
        return remote(zo.at[z], zo.at[z], zo_send.at[k], zo_recv.at[k], z_peer(k))

    def wx_copy(k):
        return remote(wx.at[x], wx.at[x], wx_send.at[k], wx_recv.at[k], x_peer(k))

    def ox_copy(k):
        return remote(wob.at[core, x], wob.at[core, x], ox_send.at[k], ox_recv.at[k], x_peer(k))

    def mod_copy(k):
        return remote(mod_s, mod_r.at[tok], mod_send.at[k], mod_recv.at[k], t_peer(k))

    def att_copy(b, k):
        there = lax.rem(tok + k, NT)
        return remote(att_s.at[b, there], att_r.at[b, tok], att_send.at[b, k], att_recv.at[b, k], t_peer(k))

    def start_w(k):
        zw_copy(k).start()
        zr_copy(k).start()

    each(NZ, start_w)
    each(NT, lambda k: prior_copy(k).start(), first=0)

    grid = lax.broadcasted_iota(jnp.int32, (SIDE, TOKENS), 1)
    line = lax.broadcasted_iota(jnp.int32, (SIDE, TOKENS), 0)
    chosen = [jnp.where(line == (grid >> 5), 1.0, 0.0), jnp.where(line == (grid & 31), 1.0, 0.0)]
    chosen = jnp.concatenate(chosen + [jnp.zeros((64, TOKENS), F32)], axis=0).astype(BF16)
    for b in range(IMAGES):
        xs[b, 0:128] = chosen
        xs[b, 128:256] = chosen
    po[...] = jnp.zeros((PIECE, 128), F32)
    for c in range(2):

        @pl.when(core == c)
        def _():
            wide = wo_ref[...].astype(F32)
            for i in range(5 - c):
                k = 5 * c + i
                po[CHUNK * i : CHUNK * i + CHUNK] = wide[:, 128 * k : 128 * k + 128]

    zo[z] = po[...].astype(BF16)
    t_from = jnp.full((1, 128), steps_ref[0, 0].astype(F32))
    t_to = jnp.full((1, 128), steps_ref[0, 1].astype(F32))
    phases = t_from * freq_ref[...]
    features = jnp.concatenate([jnp.cos(phases), jnp.sin(phases)], axis=1)
    high, mid, low = split3(features)
    feats = jnp.concatenate([high, mid, low, jnp.zeros((5, FREQ), F32)], axis=0).astype(BF16)
    row8 = lax.broadcasted_iota(jnp.int32, (8, CLASSES), 0)
    col8 = lax.broadcasted_iota(jnp.int32, (8, CLASSES), 1)
    hot = jnp.zeros((8, CLASSES), F32)
    for b in range(IMAGES):
        hot = hot + jnp.where((row8 == b) & (col8 == labels_ref[b]), 1.0, 0.0)
    classes = jnp.dot(hot.astype(BF16), cls_ref[...], preferred_element_type=F32)
    loads[0].wait()
    parts = jnp.dot(feats, time_w[...], preferred_element_type=F32)
    value = parts[0:1] + parts[1:2] + parts[2:3] + classes
    condition = (value / (1.0 + jnp.exp(-value))).astype(BF16)
    loads[1].wait()
    mod_s[:, 432:512] = jnp.zeros((8, 80), F32)
    mod_s[:, 0:432] = lax.dot_general(
        condition, mod_w[...], (((1,), (1,)), ((), ())), preferred_element_type=F32
    )
    mod_r[tok] = mod_s[...]
    each(NT, lambda k: mod_copy(k).start())

    loads[2].wait()
    inw = inw_ref[...].astype(F32)
    inw = inw - jnp.mean(inw, axis=1, keepdims=True)
    pad = jnp.concatenate([jnp.zeros((64, D), F32), inw, inw, jnp.zeros((56, D), F32)], axis=0)
    centred = table[...] + jnp.transpose(pad)
    table[...] = centred
    high, low = split2(centred)
    tcat[:, 0:128] = high
    tcat[:, 128:256] = low
    inner = jnp.dot(
        jnp.concatenate([inw, inw], axis=0), centred, preferred_element_type=F32, precision=lax.Precision.HIGHEST
    )
    lane = lax.broadcasted_iota(jnp.int32, (8, 128), 1)
    cross = jnp.where(lane < 64, inner, 0.0)
    crosses = jnp.concatenate(list(split3(cross)) + [jnp.zeros((8, 128), F32)], axis=0).astype(BF16)
    crosses = jnp.dot(crosses, chosen, preferred_element_type=F32)
    crosses = (crosses[0:8] + crosses[8:16] + crosses[16:24])[0:CHAN]

    each(NT, lambda k: mod_copy(k).wait())
    shift_rows = jnp.concatenate([mod_r[0][:, 0:432], mod_r[1][:, 0:432], mod_r[2][:, 0:288]], axis=1)
    gain_rows[...] = 1.0 + jnp.concatenate(
        [mod_r[2][:, 288:432], mod_r[3][:, 0:432], mod_r[4][:, 0:432], mod_r[5][:, 0:144]], axis=1
    )
    gates = jnp.concatenate([mod_r[5][:, 144:432], mod_r[6][:, 0:432], mod_r[7][:, 0:432]], axis=1)
    shift_split = jnp.concatenate(split2(shift_rows), axis=0)
    gates = jnp.transpose(gates)
    for b in range(IMAGES):
        gate_t[:, b * 128 : b * 128 + 128] = jnp.broadcast_to(gates[:, b : b + 1], (D, 128))
    rows = 128
    each(NT, lambda k: prior_arrival(k).wait(), first=0)

    def place(b):
        line = jnp.concatenate([pr[t, b] for t in range(NT)], axis=1)
        high = line.astype(BF16).astype(F32)
        low = line - high
        nought = jnp.zeros((CHAN, TOKENS), F32)
        xs[b, 64:80] = jnp.concatenate([high, low, nought, nought], axis=0).astype(BF16)
        xs[b, 192:208] = jnp.concatenate([high, nought, nought, nought], axis=0).astype(BF16)
        return line

    for b in range(IMAGES):
        line = place(b)
        squares = 2.0 * crosses
        for c in range(CHAN):
            squares = squares + inner[0:CHAN, 64 + c : 65 + c] * line[c : c + 1]
        variance = spread_ref[...] + jnp.sum(line * squares, axis=0, keepdims=True) * (1.0 / D)
        invs[b] = lax.rsqrt(jnp.maximum(variance, 0.0) + 1e-06)
        xo[:, b * 128 : b * 128 + 128] = xs[b, :, pl.ds(pl.multiple_of(tok * 128, 128), 128)]

    def arrive_w(k):
        zw_copy(k).wait()
        zr_copy(k).wait()

    each(NZ, arrive_w)
    each(NZ, lambda k: zo_copy(k).start())
    for i in range(NZ):
        wf[18 * i : 18 * i + 16] = zw[i].astype(F32)
        wf[18 * i + 16 : 18 * i + 18] = zr[i]
    wx[x] = wf[...].astype(BF16)
    each(NX, lambda k: wx_copy(k).start())
    own[...] = jnp.dot(tcat[...], xo[...], preferred_element_type=F32)
    each(NX, lambda k: wx_copy(k).wait())
    wt[...] = jnp.transpose(wx[...].reshape(D, 256))
    wide = wt[...].astype(F32)
    moved = lax.dot_general(wt[...], shift_split, (((1,), (1,)), ((), ())), preferred_element_type=F32)
    moved = moved[:, 0:8] + moved[:, 8:16]
    for b in range(IMAGES):
        both = jnp.concatenate(split2(wide * gain_rows[b : b + 1]), axis=0)
        folded = jnp.dot(both, tcat[...], preferred_element_type=F32)
        both = folded[0:256, 0:128] + folded[0:256, 128:256] + folded[256:512, 0:128]
        high, low = split2(both)
        ab[b, :, 0:128] = high
        ab[b, :, 128:256] = low
        shifts[b] = jnp.broadcast_to(moved[:, b : b + 1], (256, 128))

    factor = math.log2(math.e) / math.sqrt(HEAD)
    block = 256

    share = remote(wob.at[core], wob.at[core], sib_send, sib_recv, (slot, sibling))
    other = remote(wob.at[1 - core], wob.at[1 - core], sib_send, sib_recv, (slot, sibling))

    def prepare(b):
        shift = jnp.concatenate([shifts[b]] * NT, axis=1)
        qkv = jnp.dot(ab[b], xs[b], preferred_element_type=F32) * invs[b] + shift
        queries = jnp.concatenate([qkv[0:HEAD] * factor, jnp.zeros((128 - HEAD, TOKENS), F32)], axis=0)
        query_s[b % 2] = queries.astype(BF16)
        key_s[b % 2] = jnp.transpose(qkv[HEAD : HEAD + 128]).astype(BF16)
        values = jnp.concatenate([qkv[2 * HEAD : 3 * HEAD], jnp.ones((8, TOKENS), F32)], axis=0)
        value_s[b % 2] = values.astype(BF16)

    def scores_of(b, i):
        here = query_s[b % 2, :, i * block : (i + 1) * block]
        return jnp.dot(key_s[b % 2], here, preferred_element_type=F32)

    blocks = TOKENS // block
    prepare(0)
    for b in range(IMAGES):
        scores = scores_of(b, 0)
        for i in range(blocks):
            following = scores_of(b, i + 1) if i + 1 < blocks else None
            if i == 1 and b + 1 < IMAGES:
                prepare(b + 1)
            weights = jnp.exp2(scores).astype(BF16)
            summed = jnp.dot(value_s[b % 2], weights, preferred_element_type=F32)
            out = (summed * (1.0 / summed[HEAD : HEAD + 1])).astype(BF16)
            for t in range(2):
                att_s[b, 2 * i + t] = out[:, t * 128 : t * 128 + 128]
            scores = following
        att_r[b, tok] = att_s[b, tok]
        each(NT, lambda k: att_copy(b, k).start())
        if b == 0:
                each(NZ, lambda k: zo_copy(k).wait())
                for i in range(NZ):
                    base = 9 * i + (HP - HEAD) * (i // 8)
                    piece = zo[i].astype(F32)
                    for k in range(5):
                        of[base : base + CHUNK, 128 * k : 128 * k + 128] = piece[CHUNK * k : CHUNK * k + CHUNK]
                for h in range(2):
                    of[h * HP + HEAD : (h + 1) * HP] = jnp.zeros((HP - HEAD, 640), F32)
                wob[core, x] = of[...].astype(BF16)
                each(NX, lambda k: ox_copy(k).start())
        if b == 2:
            each(NX, lambda k: ox_copy(k).wait())
            share.start()

    share.wait_send()
    other.wait_recv()
    for h in range(2):
        turned = jnp.transpose(wob[h].reshape(HEADS * HP, 640))
        wot[640 * h : 640 * h + 640] = turned
    each(NT, lambda k: [att_copy(b, k).wait() for b in range(IMAGES)])
    attended = jnp.concatenate([att_r[b].reshape(HEADS * HP, 128) for b in range(IMAGES)], axis=1)
    emb[...] = jnp.dot(wot[0:D], attended, preferred_element_type=F32)

    def hidden(r, total):
        here = pl.ds(pl.multiple_of(r * rows, rows), rows)
        sums = []
        for b in range(IMAGES):
            cut = slice(b * 128, b * 128 + 128)
            value = own[here, cut] + gate_t[here, cut] * emb[here, cut]
            emb[here, cut] = value
            sums.append(jnp.sum(value.reshape(rows // 8, 8, 128), axis=0))
        return total + jnp.concatenate(sums, axis=1)

    total = lax.fori_loop(0, D // rows, hidden, jnp.zeros((8, HALF), F32))
    mean = jnp.sum(total, axis=0, keepdims=True) * (1.0 / D)

    def square(r, total):
        chunk = emb[pl.ds(pl.multiple_of(r * rows, rows), rows)] - mean
        return total + jnp.sum((chunk * chunk).reshape(rows // 8, 8, HALF), axis=0)

    total = lax.fori_loop(0, D // rows, square, jnp.zeros((8, HALF), F32))
    inverse = lax.rsqrt(jnp.sum(total, axis=0, keepdims=True) * (1.0 / D) + 1e-06)
    final = ((emb[...] - mean) * inverse).astype(BF16)
    predicted = jnp.dot(fw_ref[...], final, preferred_element_type=F32)

    keep, noise, eps = coefficients(t_from, t_to)
    for b in range(IMAGES):
        dr_r[z, b] = (keep - 1.0) * pr[tok, b] + eps * predicted[0:CHAN, b * 128 : b * 128 + 128] + noise * noise_ref[0, b]

    def dr_copy(k):
        return remote(dr_r.at[z], dr_r.at[z], dr_send.at[k], dr_recv.at[k], z_peer(k))

    def tx_copy(k):
        return remote(tx_r.at[x], tx_r.at[x], tx_send.at[k], tx_recv.at[k], x_peer(k))

    each(NZ, lambda k: dr_copy(k).start())
    each(NZ, lambda k: dr_copy(k).wait())
    nothing = jnp.zeros((IMAGES, CHAN, 128), F32)
    whole, reached = nothing, nothing
    for i in range(NZ):
        term = dr_r[i]
        whole = whole + term
        reached = reached + jnp.where(i <= z, term, nothing)
    tx_r[x] = whole
    each(NX, lambda k: tx_copy(k).start())
    each(NX, lambda k: tx_copy(k).wait())
    earlier = nothing
    for i in range(NX):
        earlier = earlier + jnp.where(i < x, tx_r[i], nothing)
    updated = anchor_ref[...] + (earlier + reached)
    upd_ref[0] = updated
    change = updated - lat_ref[0]
    er_s[...] = jnp.sum(change * change, axis=1)
    er_r[tok] = er_s[...]

    def er_copy(k):
        return remote(er_s, er_r.at[tok], er_send.at[k], er_recv.at[k], t_peer(k))

    each(NT, lambda k: er_copy(k).start())
    each(NT, lambda k: er_copy(k).wait())
    summed = jnp.sum(jnp.sum(er_r[...], axis=0), axis=1, keepdims=True) * (1.0 / (CHAN * TOKENS))
    spot = lax.broadcasted_iota(jnp.int32, (IMAGES, 128), 0) == lax.broadcasted_iota(jnp.int32, (IMAGES, 128), 1)
    err_ref[...] = jnp.sum(jnp.where(spot, summed, 0.0), axis=0, keepdims=True)[:, 0:IMAGES]


def body(
    anchor, latents, noise_draws, slot_steps, class_labels, in_weight, time_weight, class_table,
    mod_weight, qkv_weight, out_weight, final_weight,
):
    table, spread, freq = (jnp.asarray(value) for value in position_constants())
    vmem = pl.BlockSpec(memory_space=pltpu.VMEM)
    anywhere = pl.BlockSpec(memory_space=pl.ANY)
    dma = pltpu.SemaphoreType.DMA
    updated, errors = pl.pallas_call(
        kernel,
        out_shape=(
            jax.ShapeDtypeStruct((1, IMAGES, CHAN, 128), F32),
            jax.ShapeDtypeStruct((1, IMAGES), F32),
        ),
        in_specs=[pl.BlockSpec(memory_space=pltpu.SMEM)] * 2 + [vmem] * 10 + [anywhere] * 3,
        out_specs=(vmem, vmem),
        scratch_shapes=[
            pltpu.VMEM((FREQ, D), BF16),
            pltpu.VMEM((432, D), BF16),
            pltpu.VMEM((D, 128), F32),
            pltpu.VMEM((D, 256), BF16),
            pltpu.VMEM((IMAGES, 256, TOKENS), BF16),
            pltpu.VMEM((256, HALF), BF16),
            pltpu.VMEM((IMAGES, CHAN, 128), F32),
            pltpu.VMEM((NT, IMAGES, CHAN, 128), F32),
            pltpu.VMEM((8, 512), F32),
            pltpu.VMEM((NT, 8, 512), F32),
            pltpu.VMEM((8, D), F32),
            pltpu.VMEM((D, HALF), F32),
            pltpu.VMEM((IMAGES, 256, 256), BF16),
            pltpu.VMEM((IMAGES, 256, 128), F32),
            pltpu.VMEM((NZ, 16, 256), BF16),
            pltpu.VMEM((NZ, 2, 256), F32),
            pltpu.VMEM((18 * NZ, 256), F32),
            pltpu.VMEM((NX, 18 * NZ, 256), BF16),
            pltpu.VMEM((256, D), BF16),
            pltpu.VMEM((NZ, PIECE, 128), BF16),
            pltpu.VMEM((PIECE, 128), F32),
            pltpu.VMEM((2 * HP, 640), F32),
            pltpu.VMEM((2, NX, 2 * HP, 640), BF16),
            pltpu.VMEM((1280, 640), BF16),
            pltpu.VMEM((D, HALF), F32),
            pltpu.VMEM((D, HALF), F32),
            pltpu.VMEM((2, 128, TOKENS), BF16),
            pltpu.VMEM((2, TOKENS, 128), BF16),
            pltpu.VMEM((2, HP, TOKENS), BF16),
            pltpu.VMEM((IMAGES, NT, HP, 128), BF16),
            pltpu.VMEM((IMAGES, NT, HP, 128), BF16),
            pltpu.VMEM((NZ, IMAGES, CHAN, 128), F32),
            pltpu.VMEM((NX, IMAGES, CHAN, 128), F32),
            pltpu.VMEM((NT, IMAGES, 128), F32),
            pltpu.VMEM((IMAGES, 128), F32),
            pltpu.VMEM((IMAGES, 1, TOKENS), F32),
            dma((3,)),
            dma((NT,)), dma((NT,)),
            dma((NT,)), dma((NT,)),
            dma((NZ,)), dma((NZ,)),
            dma((NZ,)), dma((NZ,)),
            dma((NX,)), dma((NX,)),
            dma((NZ,)), dma((NZ,)),
            dma((NX,)), dma((NX,)),
            dma, dma,
            dma((IMAGES, NT)), dma((IMAGES, NT)),
            dma((NZ,)), dma((NZ,)),
            dma((NX,)), dma((NX,)),
            dma((NT,)), dma((NT,)),
        ],
        compiler_params=pltpu.CompilerParams(
            collective_id=0, has_side_effects=True, vmem_limit_bytes=56 * 1024 * 1024
        ),
        cost_estimate=pl.CostEstimate(flops=6_000_000_000, bytes_accessed=8_000_000, transcendentals=4_200_000),
    )(
        slot_steps, class_labels, latents, anchor, noise_draws, freq, class_table, final_weight, in_weight, spread,
        qkv_weight, out_weight, time_weight, mod_weight.T, table,
    )
    return updated, errors


def solution(mesh):
    in_specs = (
        P(None, None, "tok"),
        P("tm", None, None, "tok"),
        P("tm", None, None, "tok"),
        P("tm", None),
        P(),
        P(),
        P(),
        P(),
        P(None, "tok"),
        P("tm", None),
        P("tm", None),
        P(),
    )
    out_specs = (P("tm", None, None, "tok"), P("tm", None))
    return jax.shard_map(body, mesh=mesh, in_specs=in_specs, out_specs=out_specs, check_vma=False)
```

```python
import math

import jax
import jax.numpy as jnp
import ml_dtypes
import numpy as np
from jax import lax
from jax.experimental import pallas as pl
from jax.experimental.pallas import tpu as pltpu
from jax.sharding import PartitionSpec as P

MESH = pl.DeviceIdType.MESH
D = 1152
HEAD = 72
HEADS = 8
CHAN = 4
CLASSES = 1000
FREQ = 256
SIDE = 32
TOKENS = 1024
IMAGES = 4
NX, NZ, NT = 4, 16, 8
SLOTS = NX * NZ
HP = 80
CHUNK = 9
HALF = 512
F32 = jnp.float32
BF16 = jnp.bfloat16


def split3(values):
    high = values.astype(BF16).astype(F32)
    rest = values - high
    mid = rest.astype(BF16).astype(F32)
    return high, mid, rest - mid


def split2(values):
    high = values.astype(BF16)
    return high, (values - high.astype(F32)).astype(BF16)


def position_constants():
    quarter = D // 4
    angular = np.exp(np.float32(-math.log(10000.0)) * np.arange(quarter, dtype=np.float32) / np.float32(quarter)).astype(np.float32)
    angles = (np.arange(SIDE, dtype=np.float32)[:, None] * angular[None, :]).astype(np.float64)
    pair = np.concatenate([np.sin(angles), np.cos(angles)], axis=1)
    table = np.zeros((D, 128))
    table[: D // 2, 0:SIDE] = pair.T
    table[D // 2 :, SIDE : 2 * SIDE] = pair.T
    table = table - table.mean(axis=0, keepdims=True)
    tokens = np.arange(TOKENS)
    spread = (table[:, tokens // SIDE] + table[:, SIDE + tokens % SIDE]) ** 2
    half_freq = FREQ // 2
    freq = np.exp(-math.log(10000.0) * np.arange(half_freq) / half_freq)
    return (
        table.astype(np.float32),
        spread.mean(axis=0)[None, :].astype(np.float32),
        freq[None, :].astype(np.float32),
    )


def signal_level(step_value):
    return 0.005 + 0.99 * jnp.cos(0.4 * math.pi * step_value / 1000.0) ** 2


def coefficients(t_from, t_to):
    level_from = signal_level(t_from)
    level_to = signal_level(t_to)
    keep_coef = jnp.sqrt(level_to / level_from)
    noise_coef = 0.5 * jnp.sqrt((1.0 - level_to) / (1.0 - level_from)) * jnp.sqrt(1.0 - level_from / level_to)
    eps_coef = jnp.sqrt(1.0 - level_to - noise_coef * noise_coef) - keep_coef * jnp.sqrt(1.0 - level_from)
    return (keep_coef, noise_coef, eps_coef)


def kernel(
    steps_ref, labels_ref, lat_ref, anchor_ref, noise_ref, freq_ref, cls_ref, fw_ref, inw_ref, spread_ref,
    wq_ref, wo_ref, time_hbm, mod_hbm, table_hbm,
    upd_ref, err_ref,
    time_w, mod_w, table, tcat, xs, xo, psrc, pr, mod_s, mod_r, gain_rows, gate_t, ab, shifts,
    zw, zr, wf, wx, wt, zo, of, wob, w8, wot, emb, own, query_s, key_s, value_s, att_s, att_r,
    dr_r, tx_r, er_r, er_s, invs,
    loc_sem, pr_send, pr_recv, mod_send, mod_recv, zw_send, zw_recv, zr_send, zr_recv,
    wx_send, wx_recv, zo_send, zo_recv, ox_send, ox_recv, oy_send, oy_recv, sib_send, sib_recv,
    att_send, att_recv, dr_send, dr_recv, tx_send, tx_recv, er_send, er_recv,
):
    slot = lax.axis_index("tm")
    tok = lax.axis_index("tok")
    x = lax.div(slot, NZ)
    z = lax.rem(slot, NZ)
    core = lax.rem(tok, 2)
    sibling = tok + 1 - 2 * core

    def z_peer(k):
        return (x * NZ + lax.rem(z + k, NZ), tok)

    def x_peer(k):
        return (lax.rem(x + k, NX) * NZ + z, tok)

    def t_peer(k):
        return (slot, lax.rem(tok + k, NT))

    def each(count, action, first=1):
        def step(k, carry):
            action(k)
            return carry

        lax.fori_loop(first, count, step, 0)

    def remote(src, dst, send, recv, device):
        return pltpu.make_async_remote_copy(
            src_ref=src, dst_ref=dst, send_sem=send, recv_sem=recv, device_id=device, device_id_type=MESH
        )

    loads = [
        pltpu.make_async_copy(time_hbm, time_w, loc_sem.at[0]),
        pltpu.make_async_copy(mod_hbm, mod_w, loc_sem.at[1]),
        pltpu.make_async_copy(table_hbm, table, loc_sem.at[2]),
    ]
    for load in loads:
        load.start()

    barrier = pltpu.get_barrier_semaphore()

    def greet(device):
        pl.semaphore_signal(barrier, inc=1, device_id=device, device_id_type=MESH)

    each(NZ, lambda k: greet(z_peer(k)))
    each(NX, lambda k: greet(x_peer(k)))
    each(NT, lambda k: greet(t_peer(k)))
    before = lax.rem(slot + SLOTS - 1, SLOTS)
    after = lax.rem(slot + 1, SLOTS)
    each(NT, lambda k: greet((before, k)), first=0)
    psrc[...] = jnp.where(slot == SLOTS - 1, anchor_ref[...], lat_ref[0])
    for t in range(NT):

        @pl.when(tok == t)
        def _():
            wide = wq_ref[...].astype(F32)
            cols = [wide[:, HEAD * (HEADS * i + t) : HEAD * (HEADS * i + t + 1)] for i in range(3)]
            packed = jnp.concatenate(cols + [jnp.zeros((18, 40), F32)], axis=1)
            zw[z] = packed[0:16].astype(BF16)
            zr[z] = packed[16:18]

    own_rows = wo_ref[:, pl.ds(pl.multiple_of(tok * 128, 128), 128)].astype(F32)
    last_rows = wo_ref[:, 8 * 128 : 9 * 128].astype(F32)
    last_rows = jnp.where(core == 0, last_rows[0:7], jnp.concatenate([last_rows[7:9], jnp.zeros((5, 128), F32)], axis=0))
    zo[z] = jnp.concatenate([own_rows, last_rows], axis=0).astype(BF16)
    pl.semaphore_wait(barrier, NZ - 1 + NX - 1 + NT - 1 + NT)

    def prior_copy(k):
        return remote(psrc, pr.at[tok], pr_send.at[k], pr_recv.at[tok], (after, k))

    def prior_arrival(k):
        return remote(psrc, pr.at[k], pr_send.at[k], pr_recv.at[k], (after, k))

    def zw_copy(k):
        return remote(zw.at[z], zw.at[z], zw_send.at[k], zw_recv.at[k], z_peer(k))

    def zr_copy(k):
        return remote(zr.at[z], zr.at[z], zr_send.at[k], zr_recv.at[k], z_peer(k))

    def zo_copy(k):
        return remote(zo.at[z], zo.at[z], zo_send.at[k], zo_recv.at[k], z_peer(k))

    def wx_copy(k):
        return remote(wx.at[x], wx.at[x], wx_send.at[k], wx_recv.at[k], x_peer(k))

    def ox_copies(k):
        return [
            remote(wob.at[tok, x], wob.at[tok, x], ox_send.at[k], ox_recv.at[k], x_peer(k)),
            remote(w8.at[core, x], w8.at[core, x], ox_send.at[NX + k], ox_recv.at[NX + k], x_peer(k)),
        ]

    def oy_copy(k):
        there = 2 * lax.rem(lax.div(tok, 2) + k, 4) + core
        return remote(wob.at[tok], wob.at[tok], oy_send.at[k], oy_recv.at[k], (slot, there))

    def share_copies(side):
        return [
            remote(wob.at[2 * q + side], wob.at[2 * q + side], sib_send.at[q], sib_recv.at[q], (slot, sibling))
            for q in range(4)
        ] + [remote(w8.at[side], w8.at[side], sib_send.at[4], sib_recv.at[4], (slot, sibling))]

    def start(copies):
        for copy in copies:
            copy.start()

    def finish(copies):
        for copy in copies:
            copy.wait()

    def mod_copy(k):
        return remote(mod_s, mod_r.at[tok], mod_send.at[k], mod_recv.at[k], t_peer(k))

    def att_copy(b, k):
        there = lax.rem(tok + k, NT)
        return remote(att_s.at[b, there], att_r.at[b, tok], att_send.at[b, k], att_recv.at[b, k], t_peer(k))

    def start_w(k):
        zw_copy(k).start()
        zr_copy(k).start()

    each(NZ, start_w)
    each(NT, lambda k: prior_copy(k).start(), first=0)
    each(NZ, lambda k: zo_copy(k).start())

    grid = lax.broadcasted_iota(jnp.int32, (SIDE, TOKENS), 1)
    line = lax.broadcasted_iota(jnp.int32, (SIDE, TOKENS), 0)
    chosen = [jnp.where(line == (grid >> 5), 1.0, 0.0), jnp.where(line == (grid & 31), 1.0, 0.0)]
    chosen = jnp.concatenate(chosen + [jnp.zeros((64, TOKENS), F32)], axis=0).astype(BF16)
    for b in range(IMAGES):
        xs[b, 0:128] = chosen
        xs[b, 128:256] = chosen
    t_from = jnp.full((1, 128), steps_ref[0, 0].astype(F32))
    t_to = jnp.full((1, 128), steps_ref[0, 1].astype(F32))
    phases = t_from * freq_ref[...]
    features = jnp.concatenate([jnp.cos(phases), jnp.sin(phases)], axis=1)
    high, mid, low = split3(features)
    feats = jnp.concatenate([high, mid, low, jnp.zeros((5, FREQ), F32)], axis=0).astype(BF16)
    row8 = lax.broadcasted_iota(jnp.int32, (8, CLASSES), 0)
    col8 = lax.broadcasted_iota(jnp.int32, (8, CLASSES), 1)
    hot = jnp.zeros((8, CLASSES), F32)
    for b in range(IMAGES):
        hot = hot + jnp.where((row8 == b) & (col8 == labels_ref[b]), 1.0, 0.0)
    classes = jnp.dot(hot.astype(BF16), cls_ref[...], preferred_element_type=F32)
    loads[0].wait()
    parts = jnp.dot(feats, time_w[...], preferred_element_type=F32)
    value = parts[0:1] + parts[1:2] + parts[2:3] + classes
    condition = (value / (1.0 + jnp.exp(-value))).astype(BF16)
    loads[1].wait()
    mod_s[:, 432:512] = jnp.zeros((8, 80), F32)
    mod_s[:, 0:432] = lax.dot_general(
        condition, mod_w[...], (((1,), (1,)), ((), ())), preferred_element_type=F32
    )
    mod_r[tok] = mod_s[...]
    each(NT, lambda k: mod_copy(k).start())

    loads[2].wait()
    inw = inw_ref[...].astype(F32)
    inw = inw - jnp.mean(inw, axis=1, keepdims=True)
    pad = jnp.concatenate([jnp.zeros((64, D), F32), inw, inw, jnp.zeros((56, D), F32)], axis=0)
    centred = table[...] + jnp.transpose(pad)
    table[...] = centred
    high, low = split2(centred)
    tcat[:, 0:128] = high
    tcat[:, 128:256] = low
    inner = jnp.dot(
        jnp.concatenate([inw, inw], axis=0), centred, preferred_element_type=F32, precision=lax.Precision.HIGHEST
    )
    lane = lax.broadcasted_iota(jnp.int32, (8, 128), 1)
    cross = jnp.where(lane < 64, inner, 0.0)
    crosses = jnp.concatenate(list(split3(cross)) + [jnp.zeros((8, 128), F32)], axis=0).astype(BF16)
    crosses = jnp.dot(crosses, chosen, preferred_element_type=F32)
    crosses = (crosses[0:8] + crosses[8:16] + crosses[16:24])[0:CHAN]

    each(NT, lambda k: mod_copy(k).wait())
    shift_rows = jnp.concatenate([mod_r[0][:, 0:432], mod_r[1][:, 0:432], mod_r[2][:, 0:288]], axis=1)
    gain_rows[...] = 1.0 + jnp.concatenate(
        [mod_r[2][:, 288:432], mod_r[3][:, 0:432], mod_r[4][:, 0:432], mod_r[5][:, 0:144]], axis=1
    )
    gates = jnp.concatenate([mod_r[5][:, 144:432], mod_r[6][:, 0:432], mod_r[7][:, 0:432]], axis=1)
    shift_split = jnp.concatenate(split2(shift_rows), axis=0)
    gates = jnp.transpose(gates)
    for b in range(IMAGES):
        gate_t[:, b * 128 : b * 128 + 128] = jnp.broadcast_to(gates[:, b : b + 1], (D, 128))
    rows = 128
    each(NT, lambda k: prior_arrival(k).wait(), first=0)

    def place(b):
        line = jnp.concatenate([pr[t, b] for t in range(NT)], axis=1)
        high = line.astype(BF16).astype(F32)
        low = line - high
        nought = jnp.zeros((CHAN, TOKENS), F32)
        xs[b, 64:80] = jnp.concatenate([high, low, nought, nought], axis=0).astype(BF16)
        xs[b, 192:208] = jnp.concatenate([high, nought, nought, nought], axis=0).astype(BF16)
        return line

    for b in range(IMAGES):
        line = place(b)
        squares = 2.0 * crosses
        for c in range(CHAN):
            squares = squares + inner[0:CHAN, 64 + c : 65 + c] * line[c : c + 1]
        variance = spread_ref[...] + jnp.sum(line * squares, axis=0, keepdims=True) * (1.0 / D)
        invs[b] = lax.rsqrt(jnp.maximum(variance, 0.0) + 1e-06)
        xo[:, b * 128 : b * 128 + 128] = xs[b, :, pl.ds(pl.multiple_of(tok * 128, 128), 128)]

    def arrive_w(k):
        zw_copy(k).wait()
        zr_copy(k).wait()

    each(NZ, arrive_w)
    for i in range(NZ):
        wf[18 * i : 18 * i + 16] = zw[i].astype(F32)
        wf[18 * i + 16 : 18 * i + 18] = zr[i]
    wx[x] = wf[...].astype(BF16)
    each(NX, lambda k: wx_copy(k).start())
    each(NZ, lambda k: zo_copy(k).wait())
    of[...] = jnp.zeros((2, 2 * HP, 128), F32)
    for i in range(NZ):
        base = 9 * i + (HP - HEAD) * (i // 8)
        of[0, base : base + CHUNK] = zo[i].astype(F32)[0:CHUNK]
    for c in range(2):

        @pl.when(core == c)
        def _():
            for i in range(NZ):
                base = 9 * i + (HP - HEAD) * (i // 8)
                piece = zo[i].astype(F32)
                if c == 0:
                    of[1, base : base + 7] = piece[9:16]
                else:
                    of[1, base + 7 : base + 9] = piece[9:11]

    wob[tok, x] = of[0].astype(BF16)
    w8[core, x] = of[1].astype(BF16)
    each(NX, lambda k: start(ox_copies(k)))
    own[...] = jnp.dot(tcat[...], xo[...], preferred_element_type=F32)
    each(NX, lambda k: wx_copy(k).wait())
    wt[...] = jnp.transpose(wx[...].reshape(D, 256))
    wide = wt[...].astype(F32)
    moved = lax.dot_general(wt[...], shift_split, (((1,), (1,)), ((), ())), preferred_element_type=F32)
    moved = moved[:, 0:8] + moved[:, 8:16]
    for b in range(IMAGES):
        both = jnp.concatenate(split2(wide * gain_rows[b : b + 1]), axis=0)
        folded = jnp.dot(both, tcat[...], preferred_element_type=F32)
        both = folded[0:256, 0:128] + folded[0:256, 128:256] + folded[256:512, 0:128]
        high, low = split2(both)
        ab[b, :, 0:128] = high
        ab[b, :, 128:256] = low
        shifts[b] = jnp.broadcast_to(moved[:, b : b + 1], (256, 128))

    factor = math.log2(math.e) / math.sqrt(HEAD)
    block = 256

    each(NX, lambda k: finish(ox_copies(k)))
    each(4, lambda k: oy_copy(k).start())

    def prepare(b):
        shift = jnp.concatenate([shifts[b]] * NT, axis=1)
        qkv = jnp.dot(ab[b], xs[b], preferred_element_type=F32) * invs[b] + shift
        queries = jnp.concatenate([qkv[0:HEAD] * factor, jnp.zeros((128 - HEAD, TOKENS), F32)], axis=0)
        query_s[b % 2] = queries.astype(BF16)
        key_s[b % 2] = jnp.transpose(qkv[HEAD : HEAD + 128]).astype(BF16)
        values = jnp.concatenate([qkv[2 * HEAD : 3 * HEAD], jnp.ones((8, TOKENS), F32)], axis=0)
        value_s[b % 2] = values.astype(BF16)

    def scores_of(b, i):
        here = query_s[b % 2, :, i * block : (i + 1) * block]
        return jnp.dot(key_s[b % 2], here, preferred_element_type=F32)

    blocks = TOKENS // block
    prepare(0)
    for b in range(IMAGES):
        scores = scores_of(b, 0)
        for i in range(blocks):
            following = scores_of(b, i + 1) if i + 1 < blocks else None
            if i == 1 and b + 1 < IMAGES:
                prepare(b + 1)
            weights = jnp.exp2(scores).astype(BF16)
            summed = jnp.dot(value_s[b % 2], weights, preferred_element_type=F32)
            out = (summed * (1.0 / summed[HEAD : HEAD + 1])).astype(BF16)
            for t in range(2):
                att_s[b, 2 * i + t] = out[:, t * 128 : t * 128 + 128]
            scores = following
        att_r[b, tok] = att_s[b, tok]
        each(NT, lambda k: att_copy(b, k).start())
        if b == 2:
            each(4, lambda k: oy_copy(k).wait())
            start(share_copies(core))

    for copy in share_copies(core):
        copy.wait_send()
    for copy in share_copies(1 - core):
        copy.wait_recv()
    for t in range(NT):
        wot[128 * t : 128 * t + 128] = jnp.transpose(wob[t].reshape(HEADS * HP, 128))
    wot[1024:D] = jnp.transpose((w8[0] + w8[1]).reshape(HEADS * HP, 128))
    each(NT, lambda k: [att_copy(b, k).wait() for b in range(IMAGES)])
    attended = jnp.concatenate([att_r[b].reshape(HEADS * HP, 128) for b in range(IMAGES)], axis=1)
    emb[...] = jnp.dot(wot[...], attended, preferred_element_type=F32)

    def hidden(r, total):
        here = pl.ds(pl.multiple_of(r * rows, rows), rows)
        sums = []
        for b in range(IMAGES):
            cut = slice(b * 128, b * 128 + 128)
            value = own[here, cut] + gate_t[here, cut] * emb[here, cut]
            emb[here, cut] = value
            sums.append(jnp.sum(value.reshape(rows // 8, 8, 128), axis=0))
        return total + jnp.concatenate(sums, axis=1)

    total = lax.fori_loop(0, D // rows, hidden, jnp.zeros((8, HALF), F32))
    mean = jnp.sum(total, axis=0, keepdims=True) * (1.0 / D)

    def square(r, total):
        chunk = emb[pl.ds(pl.multiple_of(r * rows, rows), rows)] - mean
        return total + jnp.sum((chunk * chunk).reshape(rows // 8, 8, HALF), axis=0)

    total = lax.fori_loop(0, D // rows, square, jnp.zeros((8, HALF), F32))
    inverse = lax.rsqrt(jnp.sum(total, axis=0, keepdims=True) * (1.0 / D) + 1e-06)
    final = ((emb[...] - mean) * inverse).astype(BF16)
    predicted = jnp.dot(fw_ref[...], final, preferred_element_type=F32)

    keep, noise, eps = coefficients(t_from, t_to)
    for b in range(IMAGES):
        dr_r[z, b] = (keep - 1.0) * pr[tok, b] + eps * predicted[0:CHAN, b * 128 : b * 128 + 128] + noise * noise_ref[0, b]

    def dr_copy(k):
        return remote(dr_r.at[z], dr_r.at[z], dr_send.at[k], dr_recv.at[k], z_peer(k))

    def tx_copy(k):
        return remote(tx_r.at[x], tx_r.at[x], tx_send.at[k], tx_recv.at[k], x_peer(k))

    each(NZ, lambda k: dr_copy(k).start())
    each(NZ, lambda k: dr_copy(k).wait())
    nothing = jnp.zeros((IMAGES, CHAN, 128), F32)
    whole, reached = nothing, nothing
    for i in range(NZ):
        term = dr_r[i]
        whole = whole + term
        reached = reached + jnp.where(i <= z, term, nothing)
    tx_r[x] = whole
    each(NX, lambda k: tx_copy(k).start())
    each(NX, lambda k: tx_copy(k).wait())
    earlier = nothing
    for i in range(NX):
        earlier = earlier + jnp.where(i < x, tx_r[i], nothing)
    updated = anchor_ref[...] + (earlier + reached)
    upd_ref[0] = updated
    change = updated - lat_ref[0]
    er_s[...] = jnp.sum(change * change, axis=1)
    er_r[tok] = er_s[...]

    def er_copy(k):
        return remote(er_s, er_r.at[tok], er_send.at[k], er_recv.at[k], t_peer(k))

    each(NT, lambda k: er_copy(k).start())
    each(NT, lambda k: er_copy(k).wait())
    summed = jnp.sum(jnp.sum(er_r[...], axis=0), axis=1, keepdims=True) * (1.0 / (CHAN * TOKENS))
    spot = lax.broadcasted_iota(jnp.int32, (IMAGES, 128), 0) == lax.broadcasted_iota(jnp.int32, (IMAGES, 128), 1)
    err_ref[...] = jnp.sum(jnp.where(spot, summed, 0.0), axis=0, keepdims=True)[:, 0:IMAGES]


def body(
    anchor, latents, noise_draws, slot_steps, class_labels, in_weight, time_weight, class_table,
    mod_weight, qkv_weight, out_weight, final_weight,
):
    table, spread, freq = (jnp.asarray(value) for value in position_constants())
    vmem = pl.BlockSpec(memory_space=pltpu.VMEM)
    anywhere = pl.BlockSpec(memory_space=pl.ANY)
    dma = pltpu.SemaphoreType.DMA
    updated, errors = pl.pallas_call(
        kernel,
        out_shape=(
            jax.ShapeDtypeStruct((1, IMAGES, CHAN, 128), F32),
            jax.ShapeDtypeStruct((1, IMAGES), F32),
        ),
        in_specs=[pl.BlockSpec(memory_space=pltpu.SMEM)] * 2 + [vmem] * 10 + [anywhere] * 3,
        out_specs=(vmem, vmem),
        scratch_shapes=[
            pltpu.VMEM((FREQ, D), BF16),
            pltpu.VMEM((432, D), BF16),
            pltpu.VMEM((D, 128), F32),
            pltpu.VMEM((D, 256), BF16),
            pltpu.VMEM((IMAGES, 256, TOKENS), BF16),
            pltpu.VMEM((256, HALF), BF16),
            pltpu.VMEM((IMAGES, CHAN, 128), F32),
            pltpu.VMEM((NT, IMAGES, CHAN, 128), F32),
            pltpu.VMEM((8, 512), F32),
            pltpu.VMEM((NT, 8, 512), F32),
            pltpu.VMEM((8, D), F32),
            pltpu.VMEM((D, HALF), F32),
            pltpu.VMEM((IMAGES, 256, 256), BF16),
            pltpu.VMEM((IMAGES, 256, 128), F32),
            pltpu.VMEM((NZ, 16, 256), BF16),
            pltpu.VMEM((NZ, 2, 256), F32),
            pltpu.VMEM((18 * NZ, 256), F32),
            pltpu.VMEM((NX, 18 * NZ, 256), BF16),
            pltpu.VMEM((256, D), BF16),
            pltpu.VMEM((NZ, 16, 128), BF16),
            pltpu.VMEM((2, 2 * HP, 128), F32),
            pltpu.VMEM((NT, NX, 2 * HP, 128), BF16),
            pltpu.VMEM((2, NX, 2 * HP, 128), BF16),
            pltpu.VMEM((D, 640), BF16),
            pltpu.VMEM((D, HALF), F32),
            pltpu.VMEM((D, HALF), F32),
            pltpu.VMEM((2, 128, TOKENS), BF16),
            pltpu.VMEM((2, TOKENS, 128), BF16),
            pltpu.VMEM((2, HP, TOKENS), BF16),
            pltpu.VMEM((IMAGES, NT, HP, 128), BF16),
            pltpu.VMEM((IMAGES, NT, HP, 128), BF16),
            pltpu.VMEM((NZ, IMAGES, CHAN, 128), F32),
            pltpu.VMEM((NX, IMAGES, CHAN, 128), F32),
            pltpu.VMEM((NT, IMAGES, 128), F32),
            pltpu.VMEM((IMAGES, 128), F32),
            pltpu.VMEM((IMAGES, 1, TOKENS), F32),
            dma((3,)),
            dma((NT,)), dma((NT,)),
            dma((NT,)), dma((NT,)),
            dma((NZ,)), dma((NZ,)),
            dma((NZ,)), dma((NZ,)),
            dma((NX,)), dma((NX,)),
            dma((NZ,)), dma((NZ,)),
            dma((2 * NX,)), dma((2 * NX,)),
            dma((4,)), dma((4,)),
            dma((5,)), dma((5,)),
            dma((IMAGES, NT)), dma((IMAGES, NT)),
            dma((NZ,)), dma((NZ,)),
            dma((NX,)), dma((NX,)),
            dma((NT,)), dma((NT,)),
        ],
        compiler_params=pltpu.CompilerParams(
            collective_id=0, has_side_effects=True, vmem_limit_bytes=56 * 1024 * 1024
        ),
        cost_estimate=pl.CostEstimate(flops=6_000_000_000, bytes_accessed=8_000_000, transcendentals=4_200_000),
    )(
        slot_steps, class_labels, latents, anchor, noise_draws, freq, class_table, final_weight, in_weight, spread,
        qkv_weight, out_weight, time_weight, mod_weight.T, table,
    )
    return updated, errors


def solution(mesh):
    in_specs = (
        P(None, None, "tok"),
        P("tm", None, None, "tok"),
        P("tm", None, None, "tok"),
        P("tm", None),
        P(),
        P(),
        P(),
        P(),
        P(None, "tok"),
        P("tm", None),
        P("tm", None),
        P(),
    )
    out_specs = (P("tm", None, None, "tok"), P("tm", None))
    return jax.shard_map(body, mesh=mesh, in_specs=in_specs, out_specs=out_specs, check_vma=False)
```

```python
import math

import jax
import jax.numpy as jnp
import ml_dtypes
import numpy as np
from jax import lax
from jax.experimental import pallas as pl
from jax.experimental.pallas import tpu as pltpu
from jax.sharding import PartitionSpec as P

MESH = pl.DeviceIdType.MESH
D = 1152
HEAD = 72
HEADS = 8
CHAN = 4
CLASSES = 1000
FREQ = 256
SIDE = 32
TOKENS = 1024
IMAGES = 4
NX, NZ, NT = 4, 16, 8
SLOTS = NX * NZ
HP = 80
CHUNK = 9
HALF = 512
F32 = jnp.float32
BF16 = jnp.bfloat16


def split3(values):
    high = values.astype(BF16).astype(F32)
    rest = values - high
    mid = rest.astype(BF16).astype(F32)
    return high, mid, rest - mid


def split2(values):
    high = values.astype(BF16)
    return high, (values - high.astype(F32)).astype(BF16)


def position_constants():
    quarter = D // 4
    angular = np.exp(np.float32(-math.log(10000.0)) * np.arange(quarter, dtype=np.float32) / np.float32(quarter)).astype(np.float32)
    angles = (np.arange(SIDE, dtype=np.float32)[:, None] * angular[None, :]).astype(np.float64)
    pair = np.concatenate([np.sin(angles), np.cos(angles)], axis=1)
    table = np.zeros((D, 128))
    table[: D // 2, 0:SIDE] = pair.T
    table[D // 2 :, SIDE : 2 * SIDE] = pair.T
    table = table - table.mean(axis=0, keepdims=True)
    tokens = np.arange(TOKENS)
    spread = (table[:, tokens // SIDE] + table[:, SIDE + tokens % SIDE]) ** 2
    half_freq = FREQ // 2
    freq = np.exp(-math.log(10000.0) * np.arange(half_freq) / half_freq)
    return (
        table.astype(np.float32),
        spread.mean(axis=0)[None, :].astype(np.float32),
        freq[None, :].astype(np.float32),
    )


def signal_level(step_value):
    return 0.005 + 0.99 * jnp.cos(0.4 * math.pi * step_value / 1000.0) ** 2


def coefficients(t_from, t_to):
    level_from = signal_level(t_from)
    level_to = signal_level(t_to)
    keep_coef = jnp.sqrt(level_to / level_from)
    noise_coef = 0.5 * jnp.sqrt((1.0 - level_to) / (1.0 - level_from)) * jnp.sqrt(1.0 - level_from / level_to)
    eps_coef = jnp.sqrt(1.0 - level_to - noise_coef * noise_coef) - keep_coef * jnp.sqrt(1.0 - level_from)
    return (keep_coef, noise_coef, eps_coef)


def kernel(
    steps_ref, labels_ref, lat_ref, anchor_ref, noise_ref, freq_ref, cls_ref, fw_ref, inw_ref, spread_ref,
    wq_ref, wo_ref, time_hbm, mod_hbm, table_hbm,
    upd_ref, err_ref,
    time_w, mod_w, table, tcat, xs, xo, psrc, pr, mod_s, mod_r, mod_t, rb, gate_t, ab, shifts,
    zw, zr, wf, wx, wt, zo, of, wob, w8, wot, emb, own, att_s, att_r,
    dr_r, tx_r, er_r, er_s, invs,
    loc_sem, pr_send, pr_recv, mod_send, mod_recv, zw_send, zw_recv, zr_send, zr_recv,
    wx_send, wx_recv, zo_send, zo_recv, ox_send, ox_recv, oy_send, oy_recv, sib_send, sib_recv,
    att_send, att_recv, dr_send, dr_recv, tx_send, tx_recv, er_send, er_recv,
):
    slot = lax.axis_index("tm")
    tok = lax.axis_index("tok")
    x = lax.div(slot, NZ)
    z = lax.rem(slot, NZ)
    core = lax.rem(tok, 2)
    sibling = tok + 1 - 2 * core

    def z_peer(k):
        return (x * NZ + lax.rem(z + k, NZ), tok)

    def x_peer(k):
        return (lax.rem(x + k, NX) * NZ + z, tok)

    def t_peer(k):
        return (slot, lax.rem(tok + k, NT))

    def each(count, action, first=1):
        for k in range(first, count):
            action(k)

    def remote(src, dst, send, recv, device):
        return pltpu.make_async_remote_copy(
            src_ref=src, dst_ref=dst, send_sem=send, recv_sem=recv, device_id=device, device_id_type=MESH
        )

    loads = [
        pltpu.make_async_copy(time_hbm, time_w, loc_sem.at[0]),
        pltpu.make_async_copy(mod_hbm, mod_w, loc_sem.at[1]),
        pltpu.make_async_copy(table_hbm, table, loc_sem.at[2]),
    ]
    for load in loads:
        load.start()

    barrier = pltpu.get_barrier_semaphore()

    def greet(device):
        pl.semaphore_signal(barrier, inc=1, device_id=device, device_id_type=MESH)

    each(NZ, lambda k: greet(z_peer(k)))
    each(NX, lambda k: greet(x_peer(k)))
    each(NT, lambda k: greet(t_peer(k)))
    before = lax.rem(slot + SLOTS - 1, SLOTS)
    after = lax.rem(slot + 1, SLOTS)
    each(NT, lambda k: greet((before, k)), first=0)
    psrc[...] = jnp.where(slot == SLOTS - 1, anchor_ref[...], lat_ref[0])
    for t in range(NT):

        @pl.when(tok == t)
        def _():
            wide = wq_ref[...].astype(F32)
            cols = [wide[:, HEAD * (HEADS * i + t) : HEAD * (HEADS * i + t + 1)] for i in range(3)]
            packed = jnp.concatenate(cols + [jnp.zeros((18, 40), F32)], axis=1)
            zw[z] = packed[0:16].astype(BF16)
            zr[z] = packed[16:18]

    own_rows = wo_ref[:, pl.ds(pl.multiple_of(tok * 128, 128), 128)].astype(F32)
    last_rows = wo_ref[:, 8 * 128 : 9 * 128].astype(F32)
    last_rows = jnp.where(core == 0, last_rows[0:7], jnp.concatenate([last_rows[7:9], jnp.zeros((5, 128), F32)], axis=0))
    zo[z] = jnp.concatenate([own_rows, last_rows], axis=0).astype(BF16)
    pl.semaphore_wait(barrier, NZ - 1 + NX - 1 + NT - 1 + NT)

    def prior_copy(k):
        return remote(psrc, pr.at[tok], pr_send.at[k], pr_recv.at[tok], (after, k))

    def prior_arrival(k):
        return remote(psrc, pr.at[k], pr_send.at[k], pr_recv.at[k], (after, k))

    def zw_copy(k):
        return remote(zw.at[z], zw.at[z], zw_send.at[k], zw_recv.at[k], z_peer(k))

    def zr_copy(k):
        return remote(zr.at[z], zr.at[z], zr_send.at[k], zr_recv.at[k], z_peer(k))

    def zo_copy(k):
        return remote(zo.at[z], zo.at[z], zo_send.at[k], zo_recv.at[k], z_peer(k))

    def wx_copy(k):
        return remote(wx.at[x], wx.at[x], wx_send.at[k], wx_recv.at[k], x_peer(k))

    def ox_copies(k):
        return [
            remote(wob.at[tok, x], wob.at[tok, x], ox_send.at[k], ox_recv.at[k], x_peer(k)),
            remote(w8.at[core, x], w8.at[core, x], ox_send.at[NX + k], ox_recv.at[NX + k], x_peer(k)),
        ]

    def oy_copy(k):
        there = 2 * lax.rem(lax.div(tok, 2) + k, 4) + core
        return remote(wob.at[tok], wob.at[tok], oy_send.at[k], oy_recv.at[k], (slot, there))

    def share_copies(side):
        return [
            remote(wob.at[2 * q + side], wob.at[2 * q + side], sib_send.at[q], sib_recv.at[q], (slot, sibling))
            for q in range(4)
        ] + [remote(w8.at[side], w8.at[side], sib_send.at[4], sib_recv.at[4], (slot, sibling))]

    def start(copies):
        for copy in copies:
            copy.start()

    def finish(copies):
        for copy in copies:
            copy.wait()

    def mod_copy(k):
        return remote(mod_s, mod_r.at[tok], mod_send.at[k], mod_recv.at[k], t_peer(k))

    def att_copy(b, k):
        there = lax.rem(tok + k, NT)
        return remote(att_s.at[b, there], att_r.at[b, tok], att_send.at[b, k], att_recv.at[b, k], t_peer(k))

    def start_w(k):
        zw_copy(k).start()
        zr_copy(k).start()

    each(NZ, start_w)
    each(NT, lambda k: prior_copy(k).start(), first=0)
    each(NZ, lambda k: zo_copy(k).start())

    grid = lax.broadcasted_iota(jnp.int32, (SIDE, TOKENS), 1)
    line = lax.broadcasted_iota(jnp.int32, (SIDE, TOKENS), 0)
    chosen = [jnp.where(line == (grid >> 5), 1.0, 0.0), jnp.where(line == (grid & 31), 1.0, 0.0)]
    chosen = jnp.concatenate(chosen + [jnp.zeros((64, TOKENS), F32)], axis=0).astype(BF16)
    for b in range(IMAGES):
        xs[b, 0:128] = chosen
        xs[b, 128:256] = chosen
    t_from = jnp.full((1, 128), steps_ref[0, 0].astype(F32))
    t_to = jnp.full((1, 128), steps_ref[0, 1].astype(F32))
    phases = t_from * freq_ref[...]
    features = jnp.concatenate([jnp.cos(phases), jnp.sin(phases)], axis=1)
    high, mid, low = split3(features)
    feats = jnp.concatenate([high, mid, low, jnp.zeros((5, FREQ), F32)], axis=0).astype(BF16)
    row8 = lax.broadcasted_iota(jnp.int32, (8, CLASSES), 0)
    col8 = lax.broadcasted_iota(jnp.int32, (8, CLASSES), 1)
    hot = jnp.zeros((8, CLASSES), F32)
    for b in range(IMAGES):
        hot = hot + jnp.where((row8 == b) & (col8 == labels_ref[b]), 1.0, 0.0)
    classes = jnp.dot(hot.astype(BF16), cls_ref[...], preferred_element_type=F32)
    loads[0].wait()
    parts = jnp.dot(feats, time_w[...], preferred_element_type=F32)
    value = parts[0:1] + parts[1:2] + parts[2:3] + classes
    condition = (value / (1.0 + jnp.exp(-value))).astype(BF16)
    loads[1].wait()
    mod_s[:, 432:512] = jnp.zeros((8, 80), F32)
    mod_s[:, 0:432] = lax.dot_general(
        condition, mod_w[...], (((1,), (1,)), ((), ())), preferred_element_type=F32
    )
    mod_r[tok] = mod_s[...]
    each(NT, lambda k: mod_copy(k).start())

    loads[2].wait()
    inw = inw_ref[...].astype(F32)
    inw = inw - jnp.mean(inw, axis=1, keepdims=True)
    pad = jnp.concatenate([jnp.zeros((64, D), F32), inw, inw, jnp.zeros((56, D), F32)], axis=0)
    centred = table[...] + jnp.transpose(pad)
    table[...] = centred
    high, low = split2(centred)
    tcat[:, 0:128] = high
    tcat[:, 128:256] = low
    inner = jnp.dot(
        jnp.concatenate([inw, inw], axis=0), centred, preferred_element_type=F32, precision=lax.Precision.HIGHEST
    )
    lane = lax.broadcasted_iota(jnp.int32, (8, 128), 1)
    cross = jnp.where(lane < 64, inner, 0.0)
    crosses = jnp.concatenate(list(split3(cross)) + [jnp.zeros((8, 128), F32)], axis=0).astype(BF16)
    crosses = jnp.dot(crosses, chosen, preferred_element_type=F32)
    crosses = (crosses[0:8] + crosses[8:16] + crosses[16:24])[0:CHAN]

    each(NT, lambda k: mod_copy(k).wait())
    for source in range(NT):
        mod_t[source * 432 : source * 432 + 432] = jnp.transpose(mod_r[source])[0:432]
    rows = 128
    lanes = lax.broadcasted_iota(jnp.int32, (rows, 128), 1)
    for r in range(D // rows):
        here = slice(r * rows, r * rows + rows)
        shift = mod_t[r * rows : r * rows + rows]
        gain = 1.0 + mod_t[D + r * rows : D + r * rows + rows]
        base = table[here]
        for b in range(IMAGES):
            value = jnp.where(lanes == 72, shift[:, b : b + 1], gain[:, b : b + 1] * base)
            high, low = split2(value)
            rb[here, 256 * b : 256 * b + 128] = high
            rb[here, 256 * b + 128 : 256 * b + 256] = low
    each(NT, lambda k: prior_arrival(k).wait(), first=0)

    def place(b):
        line = jnp.concatenate([pr[t, b] for t in range(NT)], axis=1)
        high = line.astype(BF16).astype(F32)
        low = line - high
        nought = jnp.zeros((CHAN, TOKENS), F32)
        xs[b, 64:80] = jnp.concatenate([high, low, nought, nought], axis=0).astype(BF16)
        xs[b, 192:208] = jnp.concatenate([high, nought, nought, nought], axis=0).astype(BF16)
        return line

    for b in range(IMAGES):
        line = place(b)
        squares = 2.0 * crosses
        for c in range(CHAN):
            squares = squares + inner[0:CHAN, 64 + c : 65 + c] * line[c : c + 1]
        variance = spread_ref[...] + jnp.sum(line * squares, axis=0, keepdims=True) * (1.0 / D)
        invs[b] = lax.rsqrt(jnp.maximum(variance, 0.0) + 1e-06)
        xo[:, b * 128 : b * 128 + 128] = xs[b, :, pl.ds(pl.multiple_of(tok * 128, 128), 128)]

    def arrive_w(k):
        zw_copy(k).wait()
        zr_copy(k).wait()

    each(NZ, arrive_w)
    for i in range(NZ):
        wf[18 * i : 18 * i + 16] = zw[i].astype(F32)
        wf[18 * i + 16 : 18 * i + 18] = zr[i]
    wx[x] = wf[...].astype(BF16)
    each(NX, lambda k: wx_copy(k).start())
    each(NZ, lambda k: zo_copy(k).wait())
    of[...] = jnp.zeros((2, 2 * HP, 128), F32)
    for i in range(NZ):
        base = 9 * i + (HP - HEAD) * (i // 8)
        of[0, base : base + CHUNK] = zo[i].astype(F32)[0:CHUNK]
    for c in range(2):

        @pl.when(core == c)
        def _():
            for i in range(NZ):
                base = 9 * i + (HP - HEAD) * (i // 8)
                piece = zo[i].astype(F32)
                if c == 0:
                    of[1, base : base + 7] = piece[9:16]
                else:
                    of[1, base + 7 : base + 9] = piece[9:11]

    wob[tok, x] = of[0].astype(BF16)
    w8[core, x] = of[1].astype(BF16)
    each(NX, lambda k: start(ox_copies(k)))
    own[...] = jnp.dot(tcat[...], xo[...], preferred_element_type=F32)
    for r in range(D // rows):
        gate = mod_t[2 * D + r * rows : 2 * D + r * rows + rows]
        for b in range(IMAGES):
            gate_t[r * rows : r * rows + rows, b * 128 : b * 128 + 128] = jnp.broadcast_to(gate[:, b : b + 1], (rows, 128))
    each(NX, lambda k: wx_copy(k).wait())
    wt[...] = jnp.transpose(wx[...].reshape(D, 256))
    folded = jnp.dot(wt[...], rb[...], preferred_element_type=F32)
    for b in range(IMAGES):
        both = folded[:, 256 * b : 256 * b + 128] + folded[:, 256 * b + 128 : 256 * b + 256]
        high, low = split2(both)
        ab[b, :, 0:128] = high
        ab[b, :, 128:256] = low
        shifts[b] = jnp.broadcast_to(both[:, 72:73], (256, 128))

    factor = math.log2(math.e) / math.sqrt(HEAD)
    block = 256

    each(NX, lambda k: finish(ox_copies(k)))
    each(4, lambda k: oy_copy(k).start())

    def attend(b, carry):
        shift = jnp.concatenate([shifts[b]] * NT, axis=1)
        qkv = jnp.dot(ab[b], xs[b], preferred_element_type=F32) * invs[b] + shift
        queries = jnp.concatenate([qkv[0:HEAD] * factor, jnp.zeros((128 - HEAD, TOKENS), F32)], axis=0).astype(BF16)
        keys = jnp.transpose(qkv[HEAD : HEAD + 128]).astype(BF16)
        values = jnp.concatenate([qkv[2 * HEAD : 3 * HEAD], jnp.ones((8, TOKENS), F32)], axis=0).astype(BF16)
        for i in range(TOKENS // block):
            scores = jnp.dot(keys, queries[:, i * block : (i + 1) * block], preferred_element_type=F32)
            weights = jnp.exp2(scores).astype(BF16)
            summed = jnp.dot(values, weights, preferred_element_type=F32)
            out = (summed * (1.0 / summed[HEAD : HEAD + 1])).astype(BF16)
            for t in range(2):
                att_s[b, 2 * i + t] = out[:, t * 128 : t * 128 + 128]
        att_r[b, tok] = att_s[b, tok]
        each(NT, lambda k: att_copy(b, k).start())
        return carry

    lax.fori_loop(0, 1, attend, 0)
    each(4, lambda k: oy_copy(k).wait())
    start(share_copies(core))
    lax.fori_loop(1, IMAGES, attend, 0)
    for copy in share_copies(core):
        copy.wait_send()
    for copy in share_copies(1 - core):
        copy.wait_recv()
    for t in range(NT):
        wot[128 * t : 128 * t + 128] = jnp.transpose(wob[t].reshape(HEADS * HP, 128))
    wot[1024:D] = jnp.transpose((w8[0] + w8[1]).reshape(HEADS * HP, 128))
    each(NT, lambda k: [att_copy(b, k).wait() for b in range(IMAGES)])
    attended = jnp.concatenate([att_r[b].reshape(HEADS * HP, 128) for b in range(IMAGES)], axis=1)
    emb[...] = jnp.dot(wot[...], attended, preferred_element_type=F32)

    total = jnp.zeros((8, HALF), F32)
    for r in range(D // rows):
        here = slice(r * rows, r * rows + rows)
        value = own[here] + gate_t[here] * emb[here]
        emb[here] = value
        total = total + jnp.sum(value.reshape(rows // 8, 8, HALF), axis=0)
    mean = jnp.sum(total, axis=0, keepdims=True) * (1.0 / D)
    total = jnp.zeros((8, HALF), F32)
    for r in range(D // rows):
        chunk = emb[r * rows : r * rows + rows] - mean
        total = total + jnp.sum((chunk * chunk).reshape(rows // 8, 8, HALF), axis=0)
    inverse = lax.rsqrt(jnp.sum(total, axis=0, keepdims=True) * (1.0 / D) + 1e-06)
    final = ((emb[...] - mean) * inverse).astype(BF16)
    predicted = jnp.dot(fw_ref[...], final, preferred_element_type=F32)

    keep, noise, eps = coefficients(t_from, t_to)
    for b in range(IMAGES):
        dr_r[z, b] = (keep - 1.0) * pr[tok, b] + eps * predicted[0:CHAN, b * 128 : b * 128 + 128] + noise * noise_ref[0, b]

    def dr_copy(k):
        return remote(dr_r.at[z], dr_r.at[z], dr_send.at[k], dr_recv.at[k], z_peer(k))

    def tx_copy(k):
        return remote(tx_r.at[x], tx_r.at[x], tx_send.at[k], tx_recv.at[k], x_peer(k))

    each(NZ, lambda k: dr_copy(k).start())
    each(NZ, lambda k: dr_copy(k).wait())
    nothing = jnp.zeros((IMAGES, CHAN, 128), F32)
    whole, reached = nothing, nothing
    for i in range(NZ):
        term = dr_r[i]
        whole = whole + term
        reached = reached + jnp.where(i <= z, term, nothing)
    tx_r[x] = whole
    each(NX, lambda k: tx_copy(k).start())
    each(NX, lambda k: tx_copy(k).wait())
    earlier = nothing
    for i in range(NX):
        earlier = earlier + jnp.where(i < x, tx_r[i], nothing)
    updated = anchor_ref[...] + (earlier + reached)
    upd_ref[0] = updated
    change = updated - lat_ref[0]
    er_s[...] = jnp.sum(change * change, axis=1)
    er_r[tok] = er_s[...]

    def er_copy(k):
        return remote(er_s, er_r.at[tok], er_send.at[k], er_recv.at[k], t_peer(k))

    each(NT, lambda k: er_copy(k).start())
    each(NT, lambda k: er_copy(k).wait())
    summed = jnp.sum(jnp.sum(er_r[...], axis=0), axis=1, keepdims=True) * (1.0 / (CHAN * TOKENS))
    spot = lax.broadcasted_iota(jnp.int32, (IMAGES, 128), 0) == lax.broadcasted_iota(jnp.int32, (IMAGES, 128), 1)
    err_ref[...] = jnp.sum(jnp.where(spot, summed, 0.0), axis=0, keepdims=True)[:, 0:IMAGES]


def body(
    anchor, latents, noise_draws, slot_steps, class_labels, in_weight, time_weight, class_table,
    mod_weight, qkv_weight, out_weight, final_weight,
):
    table, spread, freq = (jnp.asarray(value) for value in position_constants())
    vmem = pl.BlockSpec(memory_space=pltpu.VMEM)
    anywhere = pl.BlockSpec(memory_space=pl.ANY)
    dma = pltpu.SemaphoreType.DMA
    updated, errors = pl.pallas_call(
        kernel,
        out_shape=(
            jax.ShapeDtypeStruct((1, IMAGES, CHAN, 128), F32),
            jax.ShapeDtypeStruct((1, IMAGES), F32),
        ),
        in_specs=[pl.BlockSpec(memory_space=pltpu.SMEM)] * 2 + [vmem] * 10 + [anywhere] * 3,
        out_specs=(vmem, vmem),
        scratch_shapes=[
            pltpu.VMEM((FREQ, D), BF16),
            pltpu.VMEM((432, D), BF16),
            pltpu.VMEM((D, 128), F32),
            pltpu.VMEM((D, 256), BF16),
            pltpu.VMEM((IMAGES, 256, TOKENS), BF16),
            pltpu.VMEM((256, HALF), BF16),
            pltpu.VMEM((IMAGES, CHAN, 128), F32),
            pltpu.VMEM((NT, IMAGES, CHAN, 128), F32),
            pltpu.VMEM((8, 512), F32),
            pltpu.VMEM((NT, 8, 512), F32),
            pltpu.VMEM((3 * D, 8), F32),
            pltpu.VMEM((D, 256 * IMAGES), BF16),
            pltpu.VMEM((D, HALF), F32),
            pltpu.VMEM((IMAGES, 256, 256), BF16),
            pltpu.VMEM((IMAGES, 256, 128), F32),
            pltpu.VMEM((NZ, 16, 256), BF16),
            pltpu.VMEM((NZ, 2, 256), F32),
            pltpu.VMEM((18 * NZ, 256), F32),
            pltpu.VMEM((NX, 18 * NZ, 256), BF16),
            pltpu.VMEM((256, D), BF16),
            pltpu.VMEM((NZ, 16, 128), BF16),
            pltpu.VMEM((2, 2 * HP, 128), F32),
            pltpu.VMEM((NT, NX, 2 * HP, 128), BF16),
            pltpu.VMEM((2, NX, 2 * HP, 128), BF16),
            pltpu.VMEM((D, 640), BF16),
            pltpu.VMEM((D, HALF), F32),
            pltpu.VMEM((D, HALF), F32),
            pltpu.VMEM((IMAGES, NT, HP, 128), BF16),
            pltpu.VMEM((IMAGES, NT, HP, 128), BF16),
            pltpu.VMEM((NZ, IMAGES, CHAN, 128), F32),
            pltpu.VMEM((NX, IMAGES, CHAN, 128), F32),
            pltpu.VMEM((NT, IMAGES, 128), F32),
            pltpu.VMEM((IMAGES, 128), F32),
            pltpu.VMEM((IMAGES, 1, TOKENS), F32),
            dma((3,)),
            dma((NT,)), dma((NT,)),
            dma((NT,)), dma((NT,)),
            dma((NZ,)), dma((NZ,)),
            dma((NZ,)), dma((NZ,)),
            dma((NX,)), dma((NX,)),
            dma((NZ,)), dma((NZ,)),
            dma((2 * NX,)), dma((2 * NX,)),
            dma((4,)), dma((4,)),
            dma((5,)), dma((5,)),
            dma((IMAGES, NT)), dma((IMAGES, NT)),
            dma((NZ,)), dma((NZ,)),
            dma((NX,)), dma((NX,)),
            dma((NT,)), dma((NT,)),
        ],
        compiler_params=pltpu.CompilerParams(
            collective_id=0, has_side_effects=True, vmem_limit_bytes=56 * 1024 * 1024
        ),
        cost_estimate=pl.CostEstimate(flops=6_000_000_000, bytes_accessed=8_000_000, transcendentals=4_200_000),
    )(
        slot_steps, class_labels, latents, anchor, noise_draws, freq, class_table, final_weight, in_weight, spread,
        qkv_weight, out_weight, time_weight, mod_weight.T, table,
    )
    return updated, errors


def solution(mesh):
    in_specs = (
        P(None, None, "tok"),
        P("tm", None, None, "tok"),
        P("tm", None, None, "tok"),
        P("tm", None),
        P(),
        P(),
        P(),
        P(),
        P(None, "tok"),
        P("tm", None),
        P("tm", None),
        P(),
    )
    out_specs = (P("tm", None, None, "tok"), P("tm", None))
    return jax.shard_map(body, mesh=mesh, in_specs=in_specs, out_specs=out_specs, check_vma=False)
```

```python
import math

import jax
import jax.numpy as jnp
import ml_dtypes
import numpy as np
from jax import lax
from jax.experimental import pallas as pl
from jax.experimental.pallas import tpu as pltpu
from jax.sharding import PartitionSpec as P

MESH = pl.DeviceIdType.MESH
D = 1152
HEAD = 72
HEADS = 8
CHAN = 4
CLASSES = 1000
FREQ = 256
SIDE = 32
TOKENS = 1024
IMAGES = 4
NX, NZ, NT = 4, 16, 8
SLOTS = NX * NZ
HP = 80
CHUNK = 9
HALF = 512
F32 = jnp.float32
BF16 = jnp.bfloat16


def split3(values):
    high = values.astype(BF16).astype(F32)
    rest = values - high
    mid = rest.astype(BF16).astype(F32)
    return high, mid, rest - mid


def split2(values):
    high = values.astype(BF16)
    return high, (values - high.astype(F32)).astype(BF16)


def position_constants():
    quarter = D // 4
    angular = np.exp(np.float32(-math.log(10000.0)) * np.arange(quarter, dtype=np.float32) / np.float32(quarter)).astype(np.float32)
    angles = (np.arange(SIDE, dtype=np.float32)[:, None] * angular[None, :]).astype(np.float64)
    pair = np.concatenate([np.sin(angles), np.cos(angles)], axis=1)
    table = np.zeros((D, 128))
    table[: D // 2, 0:SIDE] = pair.T
    table[D // 2 :, SIDE : 2 * SIDE] = pair.T
    table = table - table.mean(axis=0, keepdims=True)
    tokens = np.arange(TOKENS)
    spread = (table[:, tokens // SIDE] + table[:, SIDE + tokens % SIDE]) ** 2
    half_freq = FREQ // 2
    freq = np.exp(-math.log(10000.0) * np.arange(half_freq) / half_freq)
    return (
        table.astype(np.float32),
        spread.mean(axis=0)[None, :].astype(np.float32),
        freq[None, :].astype(np.float32),
    )


def signal_level(step_value):
    return 0.005 + 0.99 * jnp.cos(0.4 * math.pi * step_value / 1000.0) ** 2


def coefficients(t_from, t_to):
    level_from = signal_level(t_from)
    level_to = signal_level(t_to)
    keep_coef = jnp.sqrt(level_to / level_from)
    noise_coef = 0.5 * jnp.sqrt((1.0 - level_to) / (1.0 - level_from)) * jnp.sqrt(1.0 - level_from / level_to)
    eps_coef = jnp.sqrt(1.0 - level_to - noise_coef * noise_coef) - keep_coef * jnp.sqrt(1.0 - level_from)
    return (keep_coef, noise_coef, eps_coef)


def kernel(
    steps_ref, labels_ref, lat_ref, anchor_ref, noise_ref, freq_ref, cls_ref, fw_ref, inw_ref, spread_ref,
    wq_ref, wo_ref, time_hbm, mod_hbm, table_hbm,
    upd_ref, err_ref,
    time_w, mod_w, table, tcat, xs, xo, psrc, pr, mod_s, mod_r, mod_t, rb, gate_t, ab, shifts,
    zw, zr, wf, wx, zo, of, wob, w8, emb, own, query_s, key_s, value_s, att_s, att_r,
    dr_r, tx_r, er_r, er_s, invs, coef,
    loc_sem, pr_send, pr_recv, mod_send, mod_recv, zw_send, zw_recv, zr_send, zr_recv,
    wx_send, wx_recv, zo_send, zo_recv, ox_send, ox_recv, oy_send, oy_recv, sib_send, sib_recv,
    att_send, att_recv, dr_send, dr_recv, tx_send, tx_recv, er_send, er_recv,
):
    slot = lax.axis_index("tm")
    tok = lax.axis_index("tok")
    x = lax.div(slot, NZ)
    z = lax.rem(slot, NZ)
    core = lax.rem(tok, 2)
    sibling = tok + 1 - 2 * core

    def z_peer(k):
        return (x * NZ + lax.rem(z + k, NZ), tok)

    def x_peer(k):
        return (lax.rem(x + k, NX) * NZ + z, tok)

    def t_peer(k):
        return (slot, lax.rem(tok + k, NT))

    def each(count, action, first=1):
        for k in range(first, count):
            action(k)

    def remote(src, dst, send, recv, device):
        return pltpu.make_async_remote_copy(
            src_ref=src, dst_ref=dst, send_sem=send, recv_sem=recv, device_id=device, device_id_type=MESH
        )

    loads = [
        pltpu.make_async_copy(time_hbm, time_w, loc_sem.at[0]),
        pltpu.make_async_copy(mod_hbm, mod_w, loc_sem.at[1]),
        pltpu.make_async_copy(table_hbm, table, loc_sem.at[2]),
    ]
    for load in loads:
        load.start()

    barrier = pltpu.get_barrier_semaphore()

    def greet(device):
        pl.semaphore_signal(barrier, inc=1, device_id=device, device_id_type=MESH)

    each(NZ, lambda k: greet(z_peer(k)))
    each(NX, lambda k: greet(x_peer(k)))
    each(NT, lambda k: greet(t_peer(k)))
    before = lax.rem(slot + SLOTS - 1, SLOTS)
    after = lax.rem(slot + 1, SLOTS)
    each(NT, lambda k: greet((before, k)), first=0)
    psrc[...] = jnp.where(slot == SLOTS - 1, anchor_ref[...], lat_ref[0])
    for t in range(NT):

        @pl.when(tok == t)
        def _():
            wide = wq_ref[...].astype(F32)
            cols = [wide[:, HEAD * (HEADS * i + t) : HEAD * (HEADS * i + t + 1)] for i in range(3)]
            packed = jnp.concatenate(cols + [jnp.zeros((18, 40), F32)], axis=1)
            zw[z] = packed[0:16].astype(BF16)
            zr[z] = packed[16:18]

    own_rows = wo_ref[:, pl.ds(pl.multiple_of(tok * 128, 128), 128)].astype(F32)
    last_rows = wo_ref[:, 8 * 128 : 9 * 128].astype(F32)
    last_rows = jnp.where(core == 0, last_rows[0:7], jnp.concatenate([last_rows[7:9], jnp.zeros((5, 128), F32)], axis=0))
    zo[z] = jnp.concatenate([own_rows, last_rows], axis=0).astype(BF16)
    pl.semaphore_wait(barrier, NZ - 1 + NX - 1 + NT - 1 + NT)

    def prior_copy(k):
        return remote(psrc, pr.at[tok], pr_send.at[k], pr_recv.at[tok], (after, k))

    def prior_arrival(k):
        return remote(psrc, pr.at[k], pr_send.at[k], pr_recv.at[k], (after, k))

    def zw_copy(k):
        return remote(zw.at[z], zw.at[z], zw_send.at[k], zw_recv.at[k], z_peer(k))

    def zr_copy(k):
        return remote(zr.at[z], zr.at[z], zr_send.at[k], zr_recv.at[k], z_peer(k))

    def zo_copy(k):
        return remote(zo.at[z], zo.at[z], zo_send.at[k], zo_recv.at[k], z_peer(k))

    def wx_copy(k):
        return remote(wx.at[x], wx.at[x], wx_send.at[k], wx_recv.at[k], x_peer(k))

    def ox_copies(k):
        return [
            remote(wob.at[tok, x], wob.at[tok, x], ox_send.at[k], ox_recv.at[k], x_peer(k)),
            remote(w8.at[core, x], w8.at[core, x], ox_send.at[NX + k], ox_recv.at[NX + k], x_peer(k)),
        ]

    def oy_copy(k):
        there = 2 * lax.rem(lax.div(tok, 2) + k, 4) + core
        return remote(wob.at[tok], wob.at[tok], oy_send.at[k], oy_recv.at[k], (slot, there))

    def share_copies(side):
        return [
            remote(wob.at[2 * q + side], wob.at[2 * q + side], sib_send.at[q], sib_recv.at[q], (slot, sibling))
            for q in range(4)
        ] + [remote(w8.at[side], w8.at[side], sib_send.at[4], sib_recv.at[4], (slot, sibling))]

    def start(copies):
        for copy in copies:
            copy.start()

    def finish(copies):
        for copy in copies:
            copy.wait()

    def mod_copy(k):
        return remote(mod_s, mod_r.at[tok], mod_send.at[k], mod_recv.at[k], t_peer(k))

    def att_copy(b, k):
        there = lax.rem(tok + k, NT)
        return remote(att_s.at[b, there], att_r.at[b, tok], att_send.at[b, k], att_recv.at[b, k], t_peer(k))

    def start_w(k):
        zw_copy(k).start()
        zr_copy(k).start()

    each(NZ, start_w)
    each(NT, lambda k: prior_copy(k).start(), first=0)
    each(NZ, lambda k: zo_copy(k).start())

    grid = lax.broadcasted_iota(jnp.int32, (SIDE, TOKENS), 1)
    line = lax.broadcasted_iota(jnp.int32, (SIDE, TOKENS), 0)
    chosen = [jnp.where(line == (grid >> 5), 1.0, 0.0), jnp.where(line == (grid & 31), 1.0, 0.0)]
    chosen = jnp.concatenate(chosen + [jnp.zeros((64, TOKENS), F32)], axis=0).astype(BF16)
    for b in range(IMAGES):
        xs[b, 0:128] = chosen
        xs[b, 128:256] = chosen
    t_from = jnp.full((1, 128), steps_ref[0, 0].astype(F32))
    t_to = jnp.full((1, 128), steps_ref[0, 1].astype(F32))
    phases = t_from * freq_ref[...]
    features = jnp.concatenate([jnp.cos(phases), jnp.sin(phases)], axis=1)
    high, mid, low = split3(features)
    feats = jnp.concatenate([high, mid, low, jnp.zeros((5, FREQ), F32)], axis=0).astype(BF16)
    row8 = lax.broadcasted_iota(jnp.int32, (8, CLASSES), 0)
    col8 = lax.broadcasted_iota(jnp.int32, (8, CLASSES), 1)
    hot = jnp.zeros((8, CLASSES), F32)
    for b in range(IMAGES):
        hot = hot + jnp.where((row8 == b) & (col8 == labels_ref[b]), 1.0, 0.0)
    classes = jnp.dot(hot.astype(BF16), cls_ref[...], preferred_element_type=F32)
    loads[0].wait()
    parts = jnp.dot(feats, time_w[...], preferred_element_type=F32)
    value = parts[0:1] + parts[1:2] + parts[2:3] + classes
    condition = (value / (1.0 + jnp.exp(-value))).astype(BF16)
    loads[1].wait()
    mod_s[:, 432:512] = jnp.zeros((8, 80), F32)
    mod_s[:, 0:432] = lax.dot_general(
        condition, mod_w[...], (((1,), (1,)), ((), ())), preferred_element_type=F32
    )
    mod_r[tok] = mod_s[...]
    each(NT, lambda k: mod_copy(k).start())
    for i, value in enumerate(coefficients(t_from, t_to)):
        coef[i : i + 1] = value

    loads[2].wait()
    inw = inw_ref[...].astype(F32)
    inw = inw - jnp.mean(inw, axis=1, keepdims=True)
    pad = jnp.concatenate([jnp.zeros((64, D), F32), inw, inw, jnp.zeros((56, D), F32)], axis=0)
    centred = table[...] + jnp.transpose(pad)
    table[...] = centred
    high, low = split2(centred)
    tcat[:, 0:128] = high
    tcat[:, 128:256] = low
    inner = jnp.dot(
        jnp.concatenate([inw, inw], axis=0), centred, preferred_element_type=F32, precision=lax.Precision.HIGHEST
    )
    lane = lax.broadcasted_iota(jnp.int32, (8, 128), 1)
    cross = jnp.where(lane < 64, inner, 0.0)
    crosses = jnp.concatenate(list(split3(cross)) + [jnp.zeros((8, 128), F32)], axis=0).astype(BF16)
    crosses = jnp.dot(crosses, chosen, preferred_element_type=F32)
    crosses = (crosses[0:8] + crosses[8:16] + crosses[16:24])[0:CHAN]

    each(NT, lambda k: mod_copy(k).wait())
    for source in range(NT):
        mod_t[source * 432 : source * 432 + 432] = jnp.transpose(mod_r[source])[0:432]
    rows = 128
    lanes = lax.broadcasted_iota(jnp.int32, (rows, 128), 1)
    for r in range(D // rows):
        here = slice(r * rows, r * rows + rows)
        shift = mod_t[r * rows : r * rows + rows]
        gain = 1.0 + mod_t[D + r * rows : D + r * rows + rows]
        base = table[here]
        for b in range(IMAGES):
            value = jnp.where(lanes == 72, shift[:, b : b + 1], gain[:, b : b + 1] * base)
            high, low = split2(value)
            rb[here, 256 * b : 256 * b + 128] = high
            rb[here, 256 * b + 128 : 256 * b + 256] = low
    each(NT, lambda k: prior_arrival(k).wait(), first=0)

    def place(b):
        line = jnp.concatenate([pr[t, b] for t in range(NT)], axis=1)
        high = line.astype(BF16).astype(F32)
        low = line - high
        nought = jnp.zeros((CHAN, TOKENS), F32)
        xs[b, 64:80] = jnp.concatenate([high, low, nought, nought], axis=0).astype(BF16)
        xs[b, 192:208] = jnp.concatenate([high, nought, nought, nought], axis=0).astype(BF16)
        return line

    for b in range(IMAGES):
        line = place(b)
        squares = 2.0 * crosses
        for c in range(CHAN):
            squares = squares + inner[0:CHAN, 64 + c : 65 + c] * line[c : c + 1]
        variance = spread_ref[...] + jnp.sum(line * squares, axis=0, keepdims=True) * (1.0 / D)
        invs[b] = lax.rsqrt(jnp.maximum(variance, 0.0) + 1e-06)
        xo[:, b * 128 : b * 128 + 128] = xs[b, :, pl.ds(pl.multiple_of(tok * 128, 128), 128)]

    def arrive_w(k):
        zw_copy(k).wait()
        zr_copy(k).wait()

    each(NZ, arrive_w)
    for i in range(NZ):
        wf[18 * i : 18 * i + 16] = zw[i].astype(F32)
        wf[18 * i + 16 : 18 * i + 18] = zr[i]
    wx[x] = wf[...].astype(BF16)
    each(NX, lambda k: wx_copy(k).start())
    each(NZ, lambda k: zo_copy(k).wait())
    of[...] = jnp.zeros((2, 2 * HP, 128), F32)
    for i in range(NZ):
        base = 9 * i + (HP - HEAD) * (i // 8)
        of[0, base : base + CHUNK] = zo[i].astype(F32)[0:CHUNK]
    for c in range(2):

        @pl.when(core == c)
        def _():
            for i in range(NZ):
                base = 9 * i + (HP - HEAD) * (i // 8)
                piece = zo[i].astype(F32)
                if c == 0:
                    of[1, base : base + 7] = piece[9:16]
                else:
                    of[1, base + 7 : base + 9] = piece[9:11]

    wob[tok, x] = of[0].astype(BF16)
    w8[core, x] = of[1].astype(BF16)
    each(NX, lambda k: start(ox_copies(k)))
    own[...] = jnp.dot(tcat[...], xo[...], preferred_element_type=F32)
    for r in range(D // rows):
        gate = mod_t[2 * D + r * rows : 2 * D + r * rows + rows]
        for b in range(IMAGES):
            gate_t[r * rows : r * rows + rows, b * 128 : b * 128 + 128] = jnp.broadcast_to(gate[:, b : b + 1], (rows, 128))
    each(NX, lambda k: wx_copy(k).wait())
    folded = lax.dot_general(
        wx[...].reshape(D, 256), rb[...], (((0,), (0,)), ((), ())), preferred_element_type=F32
    )
    for b in range(IMAGES):
        both = folded[:, 256 * b : 256 * b + 128] + folded[:, 256 * b + 128 : 256 * b + 256]
        high, low = split2(both)
        ab[b, :, 0:128] = high
        ab[b, :, 128:256] = low
        shifts[b] = jnp.broadcast_to(both[:, 72:73], (256, 128))

    factor = math.log2(math.e) / math.sqrt(HEAD)
    block = 256

    each(NX, lambda k: finish(ox_copies(k)))
    each(4, lambda k: oy_copy(k).start())

    def prepare(b):
        shift = jnp.concatenate([shifts[b]] * NT, axis=1)
        qkv = jnp.dot(ab[b], xs[b], preferred_element_type=F32) * invs[b] + shift
        queries = jnp.concatenate([qkv[0:HEAD] * factor, jnp.zeros((128 - HEAD, TOKENS), F32)], axis=0)
        query_s[b % 2] = queries.astype(BF16)
        key_s[b % 2] = jnp.transpose(qkv[HEAD : HEAD + 128]).astype(BF16)
        values = jnp.concatenate([qkv[2 * HEAD : 3 * HEAD], jnp.ones((8, TOKENS), F32)], axis=0)
        value_s[b % 2] = values.astype(BF16)

    def scores_of(b, i):
        here = query_s[b % 2, :, i * block : (i + 1) * block]
        return jnp.dot(key_s[b % 2], here, preferred_element_type=F32)

    blocks = TOKENS // block
    prepare(0)
    for b in range(IMAGES):
        scores = scores_of(b, 0)
        for i in range(blocks):
            following = scores_of(b, i + 1) if i + 1 < blocks else None
            if i == 1 and b + 1 < IMAGES:
                prepare(b + 1)
            weights = jnp.exp2(scores).astype(BF16)
            summed = jnp.dot(value_s[b % 2], weights, preferred_element_type=F32)
            out = (summed * (1.0 / summed[HEAD : HEAD + 1])).astype(BF16)
            for t in range(2):
                att_s[b, 2 * i + t] = out[:, t * 128 : t * 128 + 128]
            scores = following
        att_r[b, tok] = att_s[b, tok]
        each(NT, lambda k: att_copy(b, k).start())
        if b == 2:
            each(4, lambda k: oy_copy(k).wait())
            start(share_copies(core))

    for copy in share_copies(core):
        copy.wait_send()
    for copy in share_copies(1 - core):
        copy.wait_recv()
    each(NT, lambda k: [att_copy(b, k).wait() for b in range(IMAGES)])
    attended = jnp.concatenate([att_r[b].reshape(HEADS * HP, 128) for b in range(IMAGES)], axis=1)
    columns = [wob[t].reshape(HEADS * HP, 128) for t in range(NT)] + [(w8[0] + w8[1]).reshape(HEADS * HP, 128)]
    emb[...] = lax.dot_general(
        jnp.concatenate(columns, axis=1), attended, (((0,), (0,)), ((), ())), preferred_element_type=F32
    )

    total = jnp.zeros((8, HALF), F32)
    for r in range(D // rows):
        here = slice(r * rows, r * rows + rows)
        value = own[here] + gate_t[here] * emb[here]
        emb[here] = value
        total = total + jnp.sum(value.reshape(rows // 8, 8, HALF), axis=0)
    mean = jnp.sum(total, axis=0, keepdims=True) * (1.0 / D)
    total = jnp.zeros((8, HALF), F32)
    for r in range(D // rows):
        chunk = emb[r * rows : r * rows + rows] - mean
        total = total + jnp.sum((chunk * chunk).reshape(rows // 8, 8, HALF), axis=0)
    inverse = lax.rsqrt(jnp.sum(total, axis=0, keepdims=True) * (1.0 / D) + 1e-06)
    final = ((emb[...] - mean) * inverse).astype(BF16)
    predicted = jnp.dot(fw_ref[...], final, preferred_element_type=F32)

    keep, noise, eps = coef[0:1], coef[1:2], coef[2:3]
    for b in range(IMAGES):
        dr_r[z, b] = (keep - 1.0) * pr[tok, b] + eps * predicted[0:CHAN, b * 128 : b * 128 + 128] + noise * noise_ref[0, b]

    def dr_copy(k):
        return remote(dr_r.at[z], dr_r.at[z], dr_send.at[k], dr_recv.at[k], z_peer(k))

    def tx_copy(k):
        return remote(tx_r.at[x], tx_r.at[x], tx_send.at[k], tx_recv.at[k], x_peer(k))

    each(NZ, lambda k: dr_copy(k).start())
    each(NZ, lambda k: dr_copy(k).wait())
    nothing = jnp.zeros((IMAGES, CHAN, 128), F32)
    whole, reached = nothing, nothing
    for i in range(NZ):
        term = dr_r[i]
        whole = whole + term
        reached = reached + jnp.where(i <= z, term, nothing)
    tx_r[x] = whole
    each(NX, lambda k: tx_copy(k).start())
    each(NX, lambda k: tx_copy(k).wait())
    earlier = nothing
    for i in range(NX):
        earlier = earlier + jnp.where(i < x, tx_r[i], nothing)
    updated = anchor_ref[...] + (earlier + reached)
    upd_ref[0] = updated
    change = updated - lat_ref[0]
    er_s[...] = jnp.sum(change * change, axis=1)
    er_r[tok] = er_s[...]

    def er_copy(k):
        return remote(er_s, er_r.at[tok], er_send.at[k], er_recv.at[k], t_peer(k))

    each(NT, lambda k: er_copy(k).start())
    each(NT, lambda k: er_copy(k).wait())
    summed = jnp.sum(jnp.sum(er_r[...], axis=0), axis=1, keepdims=True) * (1.0 / (CHAN * TOKENS))
    spot = lax.broadcasted_iota(jnp.int32, (IMAGES, 128), 0) == lax.broadcasted_iota(jnp.int32, (IMAGES, 128), 1)
    err_ref[...] = jnp.sum(jnp.where(spot, summed, 0.0), axis=0, keepdims=True)[:, 0:IMAGES]


def body(
    anchor, latents, noise_draws, slot_steps, class_labels, in_weight, time_weight, class_table,
    mod_weight, qkv_weight, out_weight, final_weight,
):
    table, spread, freq = (jnp.asarray(value) for value in position_constants())
    vmem = pl.BlockSpec(memory_space=pltpu.VMEM)
    anywhere = pl.BlockSpec(memory_space=pl.ANY)
    dma = pltpu.SemaphoreType.DMA
    updated, errors = pl.pallas_call(
        kernel,
        out_shape=(
            jax.ShapeDtypeStruct((1, IMAGES, CHAN, 128), F32),
            jax.ShapeDtypeStruct((1, IMAGES), F32),
        ),
        in_specs=[pl.BlockSpec(memory_space=pltpu.SMEM)] * 2 + [vmem] * 10 + [anywhere] * 3,
        out_specs=(vmem, vmem),
        scratch_shapes=[
            pltpu.VMEM((FREQ, D), BF16),
            pltpu.VMEM((432, D), BF16),
            pltpu.VMEM((D, 128), F32),
            pltpu.VMEM((D, 256), BF16),
            pltpu.VMEM((IMAGES, 256, TOKENS), BF16),
            pltpu.VMEM((256, HALF), BF16),
            pltpu.VMEM((IMAGES, CHAN, 128), F32),
            pltpu.VMEM((NT, IMAGES, CHAN, 128), F32),
            pltpu.VMEM((8, 512), F32),
            pltpu.VMEM((NT, 8, 512), F32),
            pltpu.VMEM((3 * D, 8), F32),
            pltpu.VMEM((D, 256 * IMAGES), BF16),
            pltpu.VMEM((D, HALF), F32),
            pltpu.VMEM((IMAGES, 256, 256), BF16),
            pltpu.VMEM((IMAGES, 256, 128), F32),
            pltpu.VMEM((NZ, 16, 256), BF16),
            pltpu.VMEM((NZ, 2, 256), F32),
            pltpu.VMEM((18 * NZ, 256), F32),
            pltpu.VMEM((NX, 18 * NZ, 256), BF16),
            pltpu.VMEM((NZ, 16, 128), BF16),
            pltpu.VMEM((2, 2 * HP, 128), F32),
            pltpu.VMEM((NT, NX, 2 * HP, 128), BF16),
            pltpu.VMEM((2, NX, 2 * HP, 128), BF16),
            pltpu.VMEM((D, HALF), F32),
            pltpu.VMEM((D, HALF), F32),
            pltpu.VMEM((2, 128, TOKENS), BF16),
            pltpu.VMEM((2, TOKENS, 128), BF16),
            pltpu.VMEM((2, HP, TOKENS), BF16),
            pltpu.VMEM((IMAGES, NT, HP, 128), BF16),
            pltpu.VMEM((IMAGES, NT, HP, 128), BF16),
            pltpu.VMEM((NZ, IMAGES, CHAN, 128), F32),
            pltpu.VMEM((NX, IMAGES, CHAN, 128), F32),
            pltpu.VMEM((NT, IMAGES, 128), F32),
            pltpu.VMEM((IMAGES, 128), F32),
            pltpu.VMEM((IMAGES, 1, TOKENS), F32),
            pltpu.VMEM((8, 128), F32),
            dma((3,)),
            dma((NT,)), dma((NT,)),
            dma((NT,)), dma((NT,)),
            dma((NZ,)), dma((NZ,)),
            dma((NZ,)), dma((NZ,)),
            dma((NX,)), dma((NX,)),
            dma((NZ,)), dma((NZ,)),
            dma((2 * NX,)), dma((2 * NX,)),
            dma((4,)), dma((4,)),
            dma((5,)), dma((5,)),
            dma((IMAGES, NT)), dma((IMAGES, NT)),
            dma((NZ,)), dma((NZ,)),
            dma((NX,)), dma((NX,)),
            dma((NT,)), dma((NT,)),
        ],
        compiler_params=pltpu.CompilerParams(
            collective_id=0, has_side_effects=True, vmem_limit_bytes=56 * 1024 * 1024
        ),
        cost_estimate=pl.CostEstimate(flops=6_000_000_000, bytes_accessed=8_000_000, transcendentals=4_200_000),
    )(
        slot_steps, class_labels, latents, anchor, noise_draws, freq, class_table, final_weight, in_weight, spread,
        qkv_weight, out_weight, time_weight, mod_weight.T, table,
    )
    return updated, errors


def solution(mesh):
    in_specs = (
        P(None, None, "tok"),
        P("tm", None, None, "tok"),
        P("tm", None, None, "tok"),
        P("tm", None),
        P(),
        P(),
        P(),
        P(),
        P(None, "tok"),
        P("tm", None),
        P("tm", None),
        P(),
    )
    out_specs = (P("tm", None, None, "tok"), P("tm", None))
    return jax.shard_map(body, mesh=mesh, in_specs=in_specs, out_specs=out_specs, check_vma=False)
```

```python
import math

import jax
import jax.numpy as jnp
import ml_dtypes
import numpy as np
from jax import lax
from jax.experimental import pallas as pl
from jax.experimental.pallas import tpu as pltpu
from jax.sharding import PartitionSpec as P

MESH = pl.DeviceIdType.MESH
D = 1152
HEAD = 72
HEADS = 8
CHAN = 4
CLASSES = 1000
FREQ = 256
SIDE = 32
TOKENS = 1024
IMAGES = 4
NX, NZ, NT = 4, 16, 8
SLOTS = NX * NZ
HP = 80
CHUNK = 9
PIECE = 48
HALF = 512
F32 = jnp.float32
BF16 = jnp.bfloat16


def split3(values):
    high = values.astype(BF16).astype(F32)
    rest = values - high
    mid = rest.astype(BF16).astype(F32)
    return high, mid, rest - mid


def split2(values):
    high = values.astype(BF16)
    return high, (values - high.astype(F32)).astype(BF16)


def position_constants():
    quarter = D // 4
    angular = np.exp(np.float32(-math.log(10000.0)) * np.arange(quarter, dtype=np.float32) / np.float32(quarter)).astype(np.float32)
    angles = (np.arange(SIDE, dtype=np.float32)[:, None] * angular[None, :]).astype(np.float64)
    pair = np.concatenate([np.sin(angles), np.cos(angles)], axis=1)
    table = np.zeros((D, 128))
    table[: D // 2, 0:SIDE] = pair.T
    table[D // 2 :, SIDE : 2 * SIDE] = pair.T
    table = table - table.mean(axis=0, keepdims=True)
    tokens = np.arange(TOKENS)
    spread = (table[:, tokens // SIDE] + table[:, SIDE + tokens % SIDE]) ** 2
    half_freq = FREQ // 2
    freq = np.exp(-math.log(10000.0) * np.arange(half_freq) / half_freq)
    return (
        table.astype(np.float32),
        spread.mean(axis=0)[None, :].astype(np.float32),
        freq[None, :].astype(np.float32),
    )


def signal_level(step_value):
    return 0.005 + 0.99 * jnp.cos(0.4 * math.pi * step_value / 1000.0) ** 2


def coefficients(t_from, t_to):
    level_from = signal_level(t_from)
    level_to = signal_level(t_to)
    keep_coef = jnp.sqrt(level_to / level_from)
    noise_coef = 0.5 * jnp.sqrt((1.0 - level_to) / (1.0 - level_from)) * jnp.sqrt(1.0 - level_from / level_to)
    eps_coef = jnp.sqrt(1.0 - level_to - noise_coef * noise_coef) - keep_coef * jnp.sqrt(1.0 - level_from)
    return (keep_coef, noise_coef, eps_coef)


def kernel(
    steps_ref, labels_ref, lat_ref, anchor_ref, noise_ref, freq_ref, cls_ref, fw_ref, inw_ref, spread_ref,
    wq_ref, wo_ref, time_hbm, mod_hbm, table_hbm,
    upd_ref, err_ref,
    time_w, mod_w, table, tcat, xs, xo, psrc, pr, mod_s, mod_r, mod_t, rb, ab, shifts,
    zw, zr, wf, wx, zo, po, of, wob, emb, own, att_s, att_r,
    dr_r, tx_r, er_r, er_s, invs, coef,
    loc_sem, pr_send, pr_recv, mod_send, mod_recv, zw_send, zw_recv, zr_send, zr_recv,
    wx_send, wx_recv, zo_send, zo_recv, ox_send, ox_recv, sib_send, sib_recv,
    att_send, att_recv, dr_send, dr_recv, tx_send, tx_recv, er_send, er_recv,
):
    slot = lax.axis_index("tm")
    tok = lax.axis_index("tok")
    x = lax.div(slot, NZ)
    z = lax.rem(slot, NZ)
    core = lax.rem(tok, 2)
    sibling = tok + 1 - 2 * core

    def z_peer(k):
        return (x * NZ + lax.rem(z + k, NZ), tok)

    def x_peer(k):
        return (lax.rem(x + k, NX) * NZ + z, tok)

    def t_peer(k):
        return (slot, lax.rem(tok + k, NT))

    def each(count, action, first=1):
        def step(k, carry):
            action(k)
            return carry

        lax.fori_loop(first, count, step, 0)

    def remote(src, dst, send, recv, device):
        return pltpu.make_async_remote_copy(
            src_ref=src, dst_ref=dst, send_sem=send, recv_sem=recv, device_id=device, device_id_type=MESH
        )

    loads = [
        pltpu.make_async_copy(time_hbm, time_w, loc_sem.at[0]),
        pltpu.make_async_copy(mod_hbm, mod_w, loc_sem.at[1]),
        pltpu.make_async_copy(table_hbm, table, loc_sem.at[2]),
    ]
    for load in loads:
        load.start()

    barrier = pltpu.get_barrier_semaphore()

    def greet(device):
        pl.semaphore_signal(barrier, inc=1, device_id=device, device_id_type=MESH)

    each(NZ, lambda k: greet(z_peer(k)))
    each(NX, lambda k: greet(x_peer(k)))
    each(NT, lambda k: greet(t_peer(k)))
    before = lax.rem(slot + SLOTS - 1, SLOTS)
    after = lax.rem(slot + 1, SLOTS)
    each(NT, lambda k: greet((before, k)), first=0)
    psrc[...] = jnp.where(slot == SLOTS - 1, anchor_ref[...], lat_ref[0])
    for t in range(NT):

        @pl.when(tok == t)
        def _():
            wide = wq_ref[...].astype(F32)
            cols = [wide[:, HEAD * (HEADS * i + t) : HEAD * (HEADS * i + t + 1)] for i in range(3)]
            packed = jnp.concatenate(cols + [jnp.zeros((18, 40), F32)], axis=1)
            zw[z] = packed[0:16].astype(BF16)
            zr[z] = packed[16:18]

    grid = lax.broadcasted_iota(jnp.int32, (SIDE, TOKENS), 1)
    line = lax.broadcasted_iota(jnp.int32, (SIDE, TOKENS), 0)
    chosen = [jnp.where(line == (grid >> 5), 1.0, 0.0), jnp.where(line == (grid & 31), 1.0, 0.0)]
    chosen = jnp.concatenate(chosen + [jnp.zeros((64, TOKENS), F32)], axis=0).astype(BF16)
    xs[0:128] = chosen
    xs[128:256] = chosen
    po[...] = jnp.zeros((PIECE, 128), F32)
    for c in range(2):

        @pl.when(core == c)
        def _():
            wide = wo_ref[...].astype(F32)
            for i in range(5 - c):
                k = 5 * c + i
                po[CHUNK * i : CHUNK * i + CHUNK] = wide[:, 128 * k : 128 * k + 128]

    zo[z] = po[...].astype(BF16)
    pl.semaphore_wait(barrier, NZ - 1 + NX - 1 + NT - 1 + NT)

    def prior_copy(k):
        return remote(psrc, pr.at[tok], pr_send.at[k], pr_recv.at[tok], (after, k))

    def prior_arrival(k):
        return remote(psrc, pr.at[k], pr_send.at[k], pr_recv.at[k], (after, k))

    def zw_copy(k):
        return remote(zw.at[z], zw.at[z], zw_send.at[k], zw_recv.at[k], z_peer(k))

    def zr_copy(k):
        return remote(zr.at[z], zr.at[z], zr_send.at[k], zr_recv.at[k], z_peer(k))

    def zo_copy(k):
        return remote(zo.at[z], zo.at[z], zo_send.at[k], zo_recv.at[k], z_peer(k))

    def wx_copy(k):
        return remote(wx.at[x], wx.at[x], wx_send.at[k], wx_recv.at[k], x_peer(k))

    def ox_copy(k):
        return remote(wob.at[core, x], wob.at[core, x], ox_send.at[k], ox_recv.at[k], x_peer(k))

    def mod_copy(k):
        return remote(mod_s, mod_r.at[tok], mod_send.at[k], mod_recv.at[k], t_peer(k))

    def att_copy(b, k):
        there = lax.rem(tok + k, NT)
        return remote(att_s.at[b, there], att_r.at[b, tok], att_send.at[b, k], att_recv.at[b, k], t_peer(k))

    each(NT, lambda k: prior_copy(k).start(), first=0)

    def start_w(k):
        zw_copy(k).start()
        zr_copy(k).start()

    each(NZ, start_w)

    t_from = jnp.full((1, 128), steps_ref[0, 0].astype(F32))
    t_to = jnp.full((1, 128), steps_ref[0, 1].astype(F32))
    phases = t_from * freq_ref[...]
    features = jnp.concatenate([jnp.cos(phases), jnp.sin(phases)], axis=1)
    high, mid, low = split3(features)
    feats = jnp.concatenate([high, mid, low, jnp.zeros((5, FREQ), F32)], axis=0).astype(BF16)
    row8 = lax.broadcasted_iota(jnp.int32, (8, CLASSES), 0)
    col8 = lax.broadcasted_iota(jnp.int32, (8, CLASSES), 1)
    hot = jnp.zeros((8, CLASSES), F32)
    for b in range(IMAGES):
        hot = hot + jnp.where((row8 == b) & (col8 == labels_ref[b]), 1.0, 0.0)
    classes = jnp.dot(hot.astype(BF16), cls_ref[...], preferred_element_type=F32)
    loads[0].wait()
    parts = jnp.dot(feats, time_w[...], preferred_element_type=F32)
    value = parts[0:1] + parts[1:2] + parts[2:3] + classes
    condition = (value / (1.0 + jnp.exp(-value))).astype(BF16)
    loads[1].wait()
    mod_s[:, 432:512] = jnp.zeros((8, 80), F32)
    mod_s[:, 0:432] = lax.dot_general(
        condition, mod_w[...], (((1,), (1,)), ((), ())), preferred_element_type=F32
    )
    mod_r[tok] = mod_s[...]
    each(NT, lambda k: mod_copy(k).start())
    for i, value in enumerate(coefficients(t_from, t_to)):
        coef[i : i + 1] = value

    loads[2].wait()
    inw = inw_ref[...].astype(F32)
    inw = inw - jnp.mean(inw, axis=1, keepdims=True)
    pad = jnp.concatenate([jnp.zeros((64, D), F32), inw, inw, jnp.zeros((56, D), F32)], axis=0)
    centred = table[...] + jnp.transpose(pad)
    table[...] = centred
    high, low = split2(centred)
    tcat[:, 0:128] = high
    tcat[:, 128:256] = low
    inner = jnp.dot(
        jnp.concatenate([inw, inw], axis=0), centred, preferred_element_type=F32, precision=lax.Precision.HIGHEST
    )
    lane = lax.broadcasted_iota(jnp.int32, (8, 128), 1)
    cross = jnp.where(lane < 64, inner, 0.0)
    crosses = jnp.concatenate(list(split3(cross)) + [jnp.zeros((8, 128), F32)], axis=0).astype(BF16)
    crosses = jnp.dot(crosses, xs[0:128], preferred_element_type=F32)
    crosses = (crosses[0:8] + crosses[8:16] + crosses[16:24])[0:CHAN]

    each(NT, lambda k: mod_copy(k).wait())
    for source in range(NT):
        mod_t[source * 432 : source * 432 + 432] = jnp.transpose(mod_r[source])[0:432]
    rows = 128

    def gains(r, carry):
        here = pl.ds(pl.multiple_of(r * rows, rows), rows)
        shift = mod_t[here]
        gain = 1.0 + mod_t[pl.ds(pl.multiple_of(D + r * rows, rows), rows)]
        lanes = lax.broadcasted_iota(jnp.int32, (rows, 128), 1)
        base = table[here]
        for b in range(IMAGES):
            value = jnp.where(lanes == 72, shift[:, b : b + 1], gain[:, b : b + 1] * base)
            high, low = split2(value)
            rb[here, 256 * b : 256 * b + 128] = high
            rb[here, 256 * b + 128 : 256 * b + 256] = low
        return carry

    lax.fori_loop(0, D // rows, gains, 0)
    each(NT, lambda k: prior_arrival(k).wait(), first=0)

    def place(b):
        line = jnp.concatenate([pr[t, b] for t in range(NT)], axis=1)
        high = line.astype(BF16).astype(F32)
        low = line - high
        nought = jnp.zeros((CHAN, TOKENS), F32)
        xs[64:80] = jnp.concatenate([high, low, nought, nought], axis=0).astype(BF16)
        xs[192:208] = jnp.concatenate([high, nought, nought, nought], axis=0).astype(BF16)
        return line

    for b in range(IMAGES):
        line = place(b)
        squares = 2.0 * crosses
        for c in range(CHAN):
            squares = squares + inner[0:CHAN, 64 + c : 65 + c] * line[c : c + 1]
        variance = spread_ref[...] + jnp.sum(line * squares, axis=0, keepdims=True) * (1.0 / D)
        invs[b] = lax.rsqrt(jnp.maximum(variance, 0.0) + 1e-06)
        xo[:, b * 128 : b * 128 + 128] = xs[:, pl.ds(pl.multiple_of(tok * 128, 128), 128)]

    def arrive_w(k):
        zw_copy(k).wait()
        zr_copy(k).wait()

    each(NZ, arrive_w)
    each(NZ, lambda k: zo_copy(k).start())
    for i in range(NZ):
        wf[18 * i : 18 * i + 16] = zw[i].astype(F32)
        wf[18 * i + 16 : 18 * i + 18] = zr[i]
    wx[x] = wf[...].astype(BF16)
    each(NX, lambda k: wx_copy(k).start())
    own[...] = jnp.dot(tcat[...], xo[...], preferred_element_type=F32)
    each(NX, lambda k: wx_copy(k).wait())
    folded = lax.dot_general(
        wx[...].reshape(D, 256), rb[...], (((0,), (0,)), ((), ())), preferred_element_type=F32
    )
    for b in range(IMAGES):
        both = folded[:, 256 * b : 256 * b + 128] + folded[:, 256 * b + 128 : 256 * b + 256]
        high, low = split2(both)
        ab[b, :, 0:128] = high
        ab[b, :, 128:256] = low
        shifts[b] = jnp.broadcast_to(both[:, 72:73], (256, 128))

    factor = math.log2(math.e) / math.sqrt(HEAD)
    block = 256

    def attend(b, carry):
        @pl.when(b == 1)
        def _():
            each(NZ, lambda k: zo_copy(k).wait())
            for i in range(NZ):
                base = 9 * i + (HP - HEAD) * (i // 8)
                piece = zo[i].astype(F32)
                for k in range(5):
                    of[base : base + CHUNK, 128 * k : 128 * k + 128] = piece[CHUNK * k : CHUNK * k + CHUNK]
            for h in range(2):
                of[h * HP + HEAD : (h + 1) * HP] = jnp.zeros((HP - HEAD, 640), F32)
            wob[core, x] = of[...].astype(BF16)
            each(NX, lambda k: ox_copy(k).start())

        place(b)
        shift = jnp.concatenate([shifts[b]] * NT, axis=1)
        qkv = jnp.dot(ab[b], xs[...], preferred_element_type=F32) * invs[b] + shift
        queries = jnp.concatenate([qkv[0:HEAD], jnp.zeros((128 - HEAD, TOKENS), F32)], axis=0).astype(BF16)
        keys = jnp.transpose(qkv[HEAD : HEAD + 128]).astype(BF16)
        values = jnp.concatenate([qkv[2 * HEAD : 3 * HEAD], jnp.ones((8, TOKENS), F32)], axis=0).astype(BF16)
        for i in range(TOKENS // block):
            scores = jnp.dot(keys, queries[:, i * block : (i + 1) * block], preferred_element_type=F32)
            weights = jnp.exp2(scores * factor).astype(BF16)
            summed = jnp.dot(values, weights, preferred_element_type=F32)
            out = (summed / summed[HEAD : HEAD + 1]).astype(BF16)
            for t in range(2):
                att_s[b, 2 * i + t] = out[:, t * 128 : t * 128 + 128]
        att_r[b, tok] = att_s[b, tok]
        each(NT, lambda k: att_copy(b, k).start())
        return carry

    lax.fori_loop(0, IMAGES, attend, 0)
    each(NX, lambda k: ox_copy(k).wait())
    share = remote(wob.at[core], wob.at[core], sib_send, sib_recv, (slot, sibling))
    share.start()
    other = remote(wob.at[1 - core], wob.at[1 - core], sib_send, sib_recv, (slot, sibling))
    each(NT, lambda k: [att_copy(b, k).wait() for b in range(IMAGES)])
    share.wait_send()
    other.wait_recv()

    attended = jnp.concatenate([att_r[b].reshape(HEADS * HP, 128) for b in range(IMAGES)], axis=1)
    contract = (((0,), (0,)), ((), ()))
    emb[0:640] = lax.dot_general(wob[0].reshape(HEADS * HP, 640), attended, contract, preferred_element_type=F32)
    emb[640:D] = lax.dot_general(wob[1].reshape(HEADS * HP, 640)[:, 0:512], attended, contract, preferred_element_type=F32)

    def hidden(r, total):
        here = pl.ds(pl.multiple_of(r * rows, rows), rows)
        gates = mod_t[pl.ds(pl.multiple_of(2 * D + r * rows, rows), rows)]
        sums = []
        for b in range(IMAGES):
            cut = slice(b * 128, b * 128 + 128)
            value = own[here, cut] + gates[:, b : b + 1] * emb[here, cut]
            emb[here, cut] = value
            sums.append(jnp.sum(value.reshape(rows // 8, 8, 128), axis=0))
        return total + jnp.concatenate(sums, axis=1)

    total = lax.fori_loop(0, D // rows, hidden, jnp.zeros((8, HALF), F32))
    mean = jnp.sum(total, axis=0, keepdims=True) * (1.0 / D)

    def square(r, total):
        chunk = emb[pl.ds(pl.multiple_of(r * rows, rows), rows)] - mean
        return total + jnp.sum((chunk * chunk).reshape(rows // 8, 8, HALF), axis=0)

    total = lax.fori_loop(0, D // rows, square, jnp.zeros((8, HALF), F32))
    inverse = lax.rsqrt(jnp.sum(total, axis=0, keepdims=True) * (1.0 / D) + 1e-06)
    final = ((emb[...] - mean) * inverse).astype(BF16)
    predicted = jnp.dot(fw_ref[...], final, preferred_element_type=F32)

    keep, noise, eps = coef[0:1], coef[1:2], coef[2:3]
    for b in range(IMAGES):
        dr_r[z, b] = (keep - 1.0) * pr[tok, b] + eps * predicted[0:CHAN, b * 128 : b * 128 + 128] + noise * noise_ref[0, b]

    def dr_copy(k):
        return remote(dr_r.at[z], dr_r.at[z], dr_send.at[k], dr_recv.at[k], z_peer(k))

    def tx_copy(k):
        return remote(tx_r.at[x], tx_r.at[x], tx_send.at[k], tx_recv.at[k], x_peer(k))

    each(NZ, lambda k: dr_copy(k).start())
    each(NZ, lambda k: dr_copy(k).wait())
    nothing = jnp.zeros((IMAGES, CHAN, 128), F32)
    whole, reached = nothing, nothing
    for i in range(NZ):
        term = dr_r[i]
        whole = whole + term
        reached = reached + jnp.where(i <= z, term, nothing)
    tx_r[x] = whole
    each(NX, lambda k: tx_copy(k).start())
    each(NX, lambda k: tx_copy(k).wait())
    earlier = nothing
    for i in range(NX):
        earlier = earlier + jnp.where(i < x, tx_r[i], nothing)
    updated = anchor_ref[...] + (earlier + reached)
    upd_ref[0] = updated
    change = updated - lat_ref[0]
    er_s[...] = jnp.sum(change * change, axis=1)
    er_r[tok] = er_s[...]

    def er_copy(k):
        return remote(er_s, er_r.at[tok], er_send.at[k], er_recv.at[k], t_peer(k))

    each(NT, lambda k: er_copy(k).start())
    each(NT, lambda k: er_copy(k).wait())
    summed = jnp.sum(jnp.sum(er_r[...], axis=0), axis=1, keepdims=True) * (1.0 / (CHAN * TOKENS))
    spot = lax.broadcasted_iota(jnp.int32, (IMAGES, 128), 0) == lax.broadcasted_iota(jnp.int32, (IMAGES, 128), 1)
    err_ref[...] = jnp.sum(jnp.where(spot, summed, 0.0), axis=0, keepdims=True)[:, 0:IMAGES]


def body(
    anchor, latents, noise_draws, slot_steps, class_labels, in_weight, time_weight, class_table,
    mod_weight, qkv_weight, out_weight, final_weight,
):
    table, spread, freq = (jnp.asarray(value) for value in position_constants())
    vmem = pl.BlockSpec(memory_space=pltpu.VMEM)
    anywhere = pl.BlockSpec(memory_space=pl.ANY)
    dma = pltpu.SemaphoreType.DMA
    updated, errors = pl.pallas_call(
        kernel,
        out_shape=(
            jax.ShapeDtypeStruct((1, IMAGES, CHAN, 128), F32),
            jax.ShapeDtypeStruct((1, IMAGES), F32),
        ),
        in_specs=[pl.BlockSpec(memory_space=pltpu.SMEM)] * 2 + [vmem] * 10 + [anywhere] * 3,
        out_specs=(vmem, vmem),
        scratch_shapes=[
            pltpu.VMEM((FREQ, D), BF16),
            pltpu.VMEM((432, D), BF16),
            pltpu.VMEM((D, 128), F32),
            pltpu.VMEM((D, 256), BF16),
            pltpu.VMEM((256, TOKENS), BF16),
            pltpu.VMEM((256, HALF), BF16),
            pltpu.VMEM((IMAGES, CHAN, 128), F32),
            pltpu.VMEM((NT, IMAGES, CHAN, 128), F32),
            pltpu.VMEM((8, 512), F32),
            pltpu.VMEM((NT, 8, 512), F32),
            pltpu.VMEM((3 * D, 8), F32),
            pltpu.VMEM((D, 256 * IMAGES), BF16),
            pltpu.VMEM((IMAGES, 256, 256), BF16),
            pltpu.VMEM((IMAGES, 256, 128), F32),
            pltpu.VMEM((NZ, 16, 256), BF16),
            pltpu.VMEM((NZ, 2, 256), F32),
            pltpu.VMEM((18 * NZ, 256), F32),
            pltpu.VMEM((NX, 18 * NZ, 256), BF16),
            pltpu.VMEM((NZ, PIECE, 128), BF16),
            pltpu.VMEM((PIECE, 128), F32),
            pltpu.VMEM((2 * HP, 640), F32),
            pltpu.VMEM((2, NX, 2 * HP, 640), BF16),
            pltpu.VMEM((D, HALF), F32),
            pltpu.VMEM((D, HALF), F32),
            pltpu.VMEM((IMAGES, NT, HP, 128), BF16),
            pltpu.VMEM((IMAGES, NT, HP, 128), BF16),
            pltpu.VMEM((NZ, IMAGES, CHAN, 128), F32),
            pltpu.VMEM((NX, IMAGES, CHAN, 128), F32),
            pltpu.VMEM((NT, IMAGES, 128), F32),
            pltpu.VMEM((IMAGES, 128), F32),
            pltpu.VMEM((IMAGES, 1, TOKENS), F32),
            pltpu.VMEM((8, 128), F32),
            dma((3,)),
            dma((NT,)), dma((NT,)),
            dma((NT,)), dma((NT,)),
            dma((NZ,)), dma((NZ,)),
            dma((NZ,)), dma((NZ,)),
            dma((NX,)), dma((NX,)),
            dma((NZ,)), dma((NZ,)),
            dma((NX,)), dma((NX,)),
            dma, dma,
            dma((IMAGES, NT)), dma((IMAGES, NT)),
            dma((NZ,)), dma((NZ,)),
            dma((NX,)), dma((NX,)),
            dma((NT,)), dma((NT,)),
        ],
        compiler_params=pltpu.CompilerParams(
            collective_id=0, has_side_effects=True, vmem_limit_bytes=56 * 1024 * 1024
        ),
        cost_estimate=pl.CostEstimate(flops=6_000_000_000, bytes_accessed=8_000_000, transcendentals=4_200_000),
    )(
        slot_steps, class_labels, latents, anchor, noise_draws, freq, class_table, final_weight, in_weight, spread,
        qkv_weight, out_weight, time_weight, mod_weight.T, table,
    )
    return updated, errors


def solution(mesh):
    in_specs = (
        P(None, None, "tok"),
        P("tm", None, None, "tok"),
        P("tm", None, None, "tok"),
        P("tm", None),
        P(),
        P(),
        P(),
        P(),
        P(None, "tok"),
        P("tm", None),
        P("tm", None),
        P(),
    )
    out_specs = (P("tm", None, None, "tok"), P("tm", None))
    return jax.shard_map(body, mesh=mesh, in_specs=in_specs, out_specs=out_specs, check_vma=False)
```

```python
import math

import jax
import jax.numpy as jnp
import ml_dtypes
import numpy as np
from jax import lax
from jax.experimental import pallas as pl
from jax.experimental.pallas import tpu as pltpu
from jax.sharding import PartitionSpec as P

MESH = pl.DeviceIdType.MESH
D = 1152
HEAD = 72
HEADS = 8
CHAN = 4
CLASSES = 1000
FREQ = 256
SIDE = 32
TOKENS = 1024
IMAGES = 4
NX, NZ, NT = 4, 16, 8
SLOTS = NX * NZ
HP = 80
CHUNK = 9
PIECE = 48
HALF = 512
F32 = jnp.float32
BF16 = jnp.bfloat16


def split3(values):
    high = values.astype(BF16).astype(F32)
    rest = values - high
    mid = rest.astype(BF16).astype(F32)
    return high, mid, rest - mid


def split2(values):
    high = values.astype(BF16)
    return high, (values - high.astype(F32)).astype(BF16)


def position_constants():
    quarter = D // 4
    angular = np.exp(np.float32(-math.log(10000.0)) * np.arange(quarter, dtype=np.float32) / np.float32(quarter)).astype(np.float32)
    angles = (np.arange(SIDE, dtype=np.float32)[:, None] * angular[None, :]).astype(np.float64)
    pair = np.concatenate([np.sin(angles), np.cos(angles)], axis=1)
    table = np.zeros((D, 128))
    table[: D // 2, 0:SIDE] = pair.T
    table[D // 2 :, SIDE : 2 * SIDE] = pair.T
    table = table - table.mean(axis=0, keepdims=True)
    tokens = np.arange(TOKENS)
    spread = (table[:, tokens // SIDE] + table[:, SIDE + tokens % SIDE]) ** 2
    half_freq = FREQ // 2
    freq = np.exp(-math.log(10000.0) * np.arange(half_freq) / half_freq)
    return (
        table.astype(np.float32),
        spread.mean(axis=0)[None, :].astype(np.float32),
        freq[None, :].astype(np.float32),
    )


def signal_level(step_value):
    return 0.005 + 0.99 * jnp.cos(0.4 * math.pi * step_value / 1000.0) ** 2


def coefficients(t_from, t_to):
    level_from = signal_level(t_from)
    level_to = signal_level(t_to)
    keep_coef = jnp.sqrt(level_to / level_from)
    noise_coef = 0.5 * jnp.sqrt((1.0 - level_to) / (1.0 - level_from)) * jnp.sqrt(1.0 - level_from / level_to)
    eps_coef = jnp.sqrt(1.0 - level_to - noise_coef * noise_coef) - keep_coef * jnp.sqrt(1.0 - level_from)
    return (keep_coef, noise_coef, eps_coef)


def kernel(
    steps_ref, labels_ref, lat_ref, anchor_ref, noise_ref, freq_ref, cls_ref, fw_ref, inw_ref, spread_ref,
    wq_ref, wo_ref, time_hbm, mod_hbm, table_hbm,
    upd_ref, err_ref,
    time_w, mod_w, table, tcat, xs, xo, psrc, pr, mod_s, mod_r, mod_t, rb, ab, shifts,
    zw, zr, wf, wx, zo, po, of, wob, emb, own, att_s, att_r,
    dr_r, tx_r, er_r, er_s, invs, coef,
    loc_sem, pr_send, pr_recv, mod_send, mod_recv, zw_send, zw_recv, zr_send, zr_recv,
    wx_send, wx_recv, zo_send, zo_recv, ox_send, ox_recv, sib_send, sib_recv,
    att_send, att_recv, dr_send, dr_recv, tx_send, tx_recv, er_send, er_recv,
):
    slot = lax.axis_index("tm")
    tok = lax.axis_index("tok")
    x = lax.div(slot, NZ)
    z = lax.rem(slot, NZ)
    core = lax.rem(tok, 2)
    sibling = tok + 1 - 2 * core

    def z_peer(k):
        return (x * NZ + lax.rem(z + k, NZ), tok)

    def x_peer(k):
        return (lax.rem(x + k, NX) * NZ + z, tok)

    def t_peer(k):
        return (slot, lax.rem(tok + k, NT))

    def each(count, action, first=1):
        def step(k, carry):
            action(k)
            return carry

        lax.fori_loop(first, count, step, 0)

    def remote(src, dst, send, recv, device):
        return pltpu.make_async_remote_copy(
            src_ref=src, dst_ref=dst, send_sem=send, recv_sem=recv, device_id=device, device_id_type=MESH
        )

    loads = [
        pltpu.make_async_copy(time_hbm, time_w, loc_sem.at[0]),
        pltpu.make_async_copy(mod_hbm, mod_w, loc_sem.at[1]),
        pltpu.make_async_copy(table_hbm, table, loc_sem.at[2]),
    ]
    for load in loads:
        load.start()

    barrier = pltpu.get_barrier_semaphore()

    def greet(device):
        pl.semaphore_signal(barrier, inc=1, device_id=device, device_id_type=MESH)

    each(NZ, lambda k: greet(z_peer(k)))
    each(NX, lambda k: greet(x_peer(k)))
    each(NT, lambda k: greet(t_peer(k)))
    before = lax.rem(slot + SLOTS - 1, SLOTS)
    after = lax.rem(slot + 1, SLOTS)
    each(NT, lambda k: greet((before, k)), first=0)
    psrc[...] = jnp.where(slot == SLOTS - 1, anchor_ref[...], lat_ref[0])
    for t in range(NT):

        @pl.when(tok == t)
        def _():
            wide = wq_ref[...].astype(F32)
            cols = [wide[:, HEAD * (HEADS * i + t) : HEAD * (HEADS * i + t + 1)] for i in range(3)]
            packed = jnp.concatenate(cols + [jnp.zeros((18, 40), F32)], axis=1)
            zw[z] = packed[0:16].astype(BF16)
            zr[z] = packed[16:18]

    pl.semaphore_wait(barrier, NZ - 1 + NX - 1 + NT - 1 + NT)

    def prior_copy(k):
        return remote(psrc, pr.at[tok], pr_send.at[k], pr_recv.at[tok], (after, k))

    def prior_arrival(k):
        return remote(psrc, pr.at[k], pr_send.at[k], pr_recv.at[k], (after, k))

    def zw_copy(k):
        return remote(zw.at[z], zw.at[z], zw_send.at[k], zw_recv.at[k], z_peer(k))

    def zr_copy(k):
        return remote(zr.at[z], zr.at[z], zr_send.at[k], zr_recv.at[k], z_peer(k))

    def zo_copy(k):
        return remote(zo.at[z], zo.at[z], zo_send.at[k], zo_recv.at[k], z_peer(k))

    def wx_copy(k):
        return remote(wx.at[x], wx.at[x], wx_send.at[k], wx_recv.at[k], x_peer(k))

    def ox_copy(k):
        return remote(wob.at[core, x], wob.at[core, x], ox_send.at[k], ox_recv.at[k], x_peer(k))

    def mod_copy(k):
        return remote(mod_s, mod_r.at[tok], mod_send.at[k], mod_recv.at[k], t_peer(k))

    def att_copy(b, k):
        there = lax.rem(tok + k, NT)
        return remote(att_s.at[b, there], att_r.at[b, tok], att_send.at[b, k], att_recv.at[b, k], t_peer(k))

    def start_w(k):
        zw_copy(k).start()
        zr_copy(k).start()

    each(NZ, start_w)
    each(NT, lambda k: prior_copy(k).start(), first=0)

    grid = lax.broadcasted_iota(jnp.int32, (SIDE, TOKENS), 1)
    line = lax.broadcasted_iota(jnp.int32, (SIDE, TOKENS), 0)
    chosen = [jnp.where(line == (grid >> 5), 1.0, 0.0), jnp.where(line == (grid & 31), 1.0, 0.0)]
    chosen = jnp.concatenate(chosen + [jnp.zeros((64, TOKENS), F32)], axis=0).astype(BF16)
    xs[0:128] = chosen
    xs[128:256] = chosen
    po[...] = jnp.zeros((PIECE, 128), F32)
    for c in range(2):

        @pl.when(core == c)
        def _():
            wide = wo_ref[...].astype(F32)
            for i in range(5 - c):
                k = 5 * c + i
                po[CHUNK * i : CHUNK * i + CHUNK] = wide[:, 128 * k : 128 * k + 128]

    zo[z] = po[...].astype(BF16)
    t_from = jnp.full((1, 128), steps_ref[0, 0].astype(F32))
    t_to = jnp.full((1, 128), steps_ref[0, 1].astype(F32))
    phases = t_from * freq_ref[...]
    features = jnp.concatenate([jnp.cos(phases), jnp.sin(phases)], axis=1)
    high, mid, low = split3(features)
    feats = jnp.concatenate([high, mid, low, jnp.zeros((5, FREQ), F32)], axis=0).astype(BF16)
    row8 = lax.broadcasted_iota(jnp.int32, (8, CLASSES), 0)
    col8 = lax.broadcasted_iota(jnp.int32, (8, CLASSES), 1)
    hot = jnp.zeros((8, CLASSES), F32)
    for b in range(IMAGES):
        hot = hot + jnp.where((row8 == b) & (col8 == labels_ref[b]), 1.0, 0.0)
    classes = jnp.dot(hot.astype(BF16), cls_ref[...], preferred_element_type=F32)
    loads[0].wait()
    parts = jnp.dot(feats, time_w[...], preferred_element_type=F32)
    value = parts[0:1] + parts[1:2] + parts[2:3] + classes
    condition = (value / (1.0 + jnp.exp(-value))).astype(BF16)
    loads[1].wait()
    mod_s[:, 432:512] = jnp.zeros((8, 80), F32)
    mod_s[:, 0:432] = lax.dot_general(
        condition, mod_w[...], (((1,), (1,)), ((), ())), preferred_element_type=F32
    )
    mod_r[tok] = mod_s[...]
    each(NT, lambda k: mod_copy(k).start())
    for i, value in enumerate(coefficients(t_from, t_to)):
        coef[i : i + 1] = value

    loads[2].wait()
    inw = inw_ref[...].astype(F32)
    inw = inw - jnp.mean(inw, axis=1, keepdims=True)
    pad = jnp.concatenate([jnp.zeros((64, D), F32), inw, inw, jnp.zeros((56, D), F32)], axis=0)
    centred = table[...] + jnp.transpose(pad)
    table[...] = centred
    high, low = split2(centred)
    tcat[:, 0:128] = high
    tcat[:, 128:256] = low
    inner = jnp.dot(
        jnp.concatenate([inw, inw], axis=0), centred, preferred_element_type=F32, precision=lax.Precision.HIGHEST
    )
    lane = lax.broadcasted_iota(jnp.int32, (8, 128), 1)
    cross = jnp.where(lane < 64, inner, 0.0)
    crosses = jnp.concatenate(list(split3(cross)) + [jnp.zeros((8, 128), F32)], axis=0).astype(BF16)
    crosses = jnp.dot(crosses, xs[0:128], preferred_element_type=F32)
    crosses = (crosses[0:8] + crosses[8:16] + crosses[16:24])[0:CHAN]

    def arrive_w(k):
        zw_copy(k).wait()
        zr_copy(k).wait()

    each(NZ, arrive_w)
    for i in range(NZ):
        wf[18 * i : 18 * i + 16] = zw[i].astype(F32)
        wf[18 * i + 16 : 18 * i + 18] = zr[i]
    wx[x] = wf[...].astype(BF16)
    each(NX, lambda k: wx_copy(k).start())
    each(NZ, lambda k: zo_copy(k).start())
    each(NT, lambda k: mod_copy(k).wait())
    for source in range(NT):
        mod_t[source * 432 : source * 432 + 432] = jnp.transpose(mod_r[source])[0:432]
    rows = 128

    def gains(r, carry):
        here = pl.ds(pl.multiple_of(r * rows, rows), rows)
        shift = mod_t[here]
        gain = 1.0 + mod_t[pl.ds(pl.multiple_of(D + r * rows, rows), rows)]
        lanes = lax.broadcasted_iota(jnp.int32, (rows, 128), 1)
        base = table[here]
        for b in range(IMAGES):
            value = jnp.where(lanes == 72, shift[:, b : b + 1], gain[:, b : b + 1] * base)
            high, low = split2(value)
            rb[here, 256 * b : 256 * b + 128] = high
            rb[here, 256 * b + 128 : 256 * b + 256] = low
        return carry

    lax.fori_loop(0, D // rows, gains, 0)
    each(NT, lambda k: prior_arrival(k).wait(), first=0)

    def place(b):
        line = jnp.concatenate([pr[t, b] for t in range(NT)], axis=1)
        high = line.astype(BF16).astype(F32)
        low = line - high
        nought = jnp.zeros((CHAN, TOKENS), F32)
        xs[64:80] = jnp.concatenate([high, low, nought, nought], axis=0).astype(BF16)
        xs[192:208] = jnp.concatenate([high, nought, nought, nought], axis=0).astype(BF16)
        return line

    for b in range(IMAGES):
        line = place(b)
        squares = 2.0 * crosses
        for c in range(CHAN):
            squares = squares + inner[0:CHAN, 64 + c : 65 + c] * line[c : c + 1]
        variance = spread_ref[...] + jnp.sum(line * squares, axis=0, keepdims=True) * (1.0 / D)
        invs[b] = lax.rsqrt(jnp.maximum(variance, 0.0) + 1e-06)
        xo[:, b * 128 : b * 128 + 128] = xs[:, pl.ds(pl.multiple_of(tok * 128, 128), 128)]

    own[...] = jnp.dot(tcat[...], xo[...], preferred_element_type=F32)
    each(NX, lambda k: wx_copy(k).wait())
    folded = lax.dot_general(
        wx[...].reshape(D, 256), rb[...], (((0,), (0,)), ((), ())), preferred_element_type=F32
    )
    for b in range(IMAGES):
        both = folded[:, 256 * b : 256 * b + 128] + folded[:, 256 * b + 128 : 256 * b + 256]
        high, low = split2(both)
        ab[b, :, 0:128] = high
        ab[b, :, 128:256] = low
        shifts[b] = jnp.broadcast_to(both[:, 72:73], (256, 128))

    factor = math.log2(math.e) / math.sqrt(HEAD)
    block = 256

    def attend(b, carry):
        @pl.when(b == 1)
        def _():
            each(NZ, lambda k: zo_copy(k).wait())
            for i in range(NZ):
                base = 9 * i + (HP - HEAD) * (i // 8)
                piece = zo[i].astype(F32)
                for k in range(5):
                    of[base : base + CHUNK, 128 * k : 128 * k + 128] = piece[CHUNK * k : CHUNK * k + CHUNK]
            for h in range(2):
                of[h * HP + HEAD : (h + 1) * HP] = jnp.zeros((HP - HEAD, 640), F32)
            wob[core, x] = of[...].astype(BF16)
            each(NX, lambda k: ox_copy(k).start())

        place(b)
        shift = jnp.concatenate([shifts[b]] * NT, axis=1)
        qkv = jnp.dot(ab[b], xs[...], preferred_element_type=F32) * invs[b] + shift
        queries = jnp.concatenate([qkv[0:HEAD], jnp.zeros((128 - HEAD, TOKENS), F32)], axis=0).astype(BF16)
        keys = jnp.transpose(qkv[HEAD : HEAD + 128]).astype(BF16)
        values = jnp.concatenate([qkv[2 * HEAD : 3 * HEAD], jnp.ones((8, TOKENS), F32)], axis=0).astype(BF16)
        for i in range(TOKENS // block):
            scores = jnp.dot(keys, queries[:, i * block : (i + 1) * block], preferred_element_type=F32)
            weights = jnp.exp2(scores * factor).astype(BF16)
            summed = jnp.dot(values, weights, preferred_element_type=F32)
            out = (summed / summed[HEAD : HEAD + 1]).astype(BF16)
            for t in range(2):
                att_s[b, 2 * i + t] = out[:, t * 128 : t * 128 + 128]
        att_r[b, tok] = att_s[b, tok]
        each(NT, lambda k: att_copy(b, k).start())
        return carry

    lax.fori_loop(0, IMAGES, attend, 0)
    each(NX, lambda k: ox_copy(k).wait())
    share = remote(wob.at[core], wob.at[core], sib_send, sib_recv, (slot, sibling))
    share.start()
    other = remote(wob.at[1 - core], wob.at[1 - core], sib_send, sib_recv, (slot, sibling))
    each(NT, lambda k: [att_copy(b, k).wait() for b in range(IMAGES)])
    share.wait_send()
    other.wait_recv()

    attended = jnp.concatenate([att_r[b].reshape(HEADS * HP, 128) for b in range(IMAGES)], axis=1)
    contract = (((0,), (0,)), ((), ()))
    emb[0:640] = lax.dot_general(wob[0].reshape(HEADS * HP, 640), attended, contract, preferred_element_type=F32)
    emb[640:D] = lax.dot_general(wob[1].reshape(HEADS * HP, 640)[:, 0:512], attended, contract, preferred_element_type=F32)

    def hidden(r, total):
        here = pl.ds(pl.multiple_of(r * rows, rows), rows)
        gates = mod_t[pl.ds(pl.multiple_of(2 * D + r * rows, rows), rows)]
        sums = []
        for b in range(IMAGES):
            cut = slice(b * 128, b * 128 + 128)
            value = own[here, cut] + gates[:, b : b + 1] * emb[here, cut]
            emb[here, cut] = value
            sums.append(jnp.sum(value.reshape(rows // 8, 8, 128), axis=0))
        return total + jnp.concatenate(sums, axis=1)

    total = lax.fori_loop(0, D // rows, hidden, jnp.zeros((8, HALF), F32))
    mean = jnp.sum(total, axis=0, keepdims=True) * (1.0 / D)

    def square(r, total):
        chunk = emb[pl.ds(pl.multiple_of(r * rows, rows), rows)] - mean
        return total + jnp.sum((chunk * chunk).reshape(rows // 8, 8, HALF), axis=0)

    total = lax.fori_loop(0, D // rows, square, jnp.zeros((8, HALF), F32))
    inverse = lax.rsqrt(jnp.sum(total, axis=0, keepdims=True) * (1.0 / D) + 1e-06)
    final = ((emb[...] - mean) * inverse).astype(BF16)
    predicted = jnp.dot(fw_ref[...], final, preferred_element_type=F32)

    keep, noise, eps = coef[0:1], coef[1:2], coef[2:3]
    for b in range(IMAGES):
        dr_r[z, b] = (keep - 1.0) * pr[tok, b] + eps * predicted[0:CHAN, b * 128 : b * 128 + 128] + noise * noise_ref[0, b]

    def dr_copy(k):
        return remote(dr_r.at[z], dr_r.at[z], dr_send.at[k], dr_recv.at[k], z_peer(k))

    def tx_copy(k):
        return remote(tx_r.at[x], tx_r.at[x], tx_send.at[k], tx_recv.at[k], x_peer(k))

    each(NZ, lambda k: dr_copy(k).start())
    each(NZ, lambda k: dr_copy(k).wait())
    nothing = jnp.zeros((IMAGES, CHAN, 128), F32)
    whole, reached = nothing, nothing
    for i in range(NZ):
        term = dr_r[i]
        whole = whole + term
        reached = reached + jnp.where(i <= z, term, nothing)
    tx_r[x] = whole
    each(NX, lambda k: tx_copy(k).start())
    each(NX, lambda k: tx_copy(k).wait())
    earlier = nothing
    for i in range(NX):
        earlier = earlier + jnp.where(i < x, tx_r[i], nothing)
    updated = anchor_ref[...] + (earlier + reached)
    upd_ref[0] = updated
    change = updated - lat_ref[0]
    er_s[...] = jnp.sum(change * change, axis=1)
    er_r[tok] = er_s[...]

    def er_copy(k):
        return remote(er_s, er_r.at[tok], er_send.at[k], er_recv.at[k], t_peer(k))

    each(NT, lambda k: er_copy(k).start())
    each(NT, lambda k: er_copy(k).wait())
    summed = jnp.sum(jnp.sum(er_r[...], axis=0), axis=1, keepdims=True) * (1.0 / (CHAN * TOKENS))
    spot = lax.broadcasted_iota(jnp.int32, (IMAGES, 128), 0) == lax.broadcasted_iota(jnp.int32, (IMAGES, 128), 1)
    err_ref[...] = jnp.sum(jnp.where(spot, summed, 0.0), axis=0, keepdims=True)[:, 0:IMAGES]


def body(
    anchor, latents, noise_draws, slot_steps, class_labels, in_weight, time_weight, class_table,
    mod_weight, qkv_weight, out_weight, final_weight,
):
    table, spread, freq = (jnp.asarray(value) for value in position_constants())
    vmem = pl.BlockSpec(memory_space=pltpu.VMEM)
    anywhere = pl.BlockSpec(memory_space=pl.ANY)
    dma = pltpu.SemaphoreType.DMA
    updated, errors = pl.pallas_call(
        kernel,
        out_shape=(
            jax.ShapeDtypeStruct((1, IMAGES, CHAN, 128), F32),
            jax.ShapeDtypeStruct((1, IMAGES), F32),
        ),
        in_specs=[pl.BlockSpec(memory_space=pltpu.SMEM)] * 2 + [vmem] * 10 + [anywhere] * 3,
        out_specs=(vmem, vmem),
        scratch_shapes=[
            pltpu.VMEM((FREQ, D), BF16),
            pltpu.VMEM((432, D), BF16),
            pltpu.VMEM((D, 128), F32),
            pltpu.VMEM((D, 256), BF16),
            pltpu.VMEM((256, TOKENS), BF16),
            pltpu.VMEM((256, HALF), BF16),
            pltpu.VMEM((IMAGES, CHAN, 128), F32),
            pltpu.VMEM((NT, IMAGES, CHAN, 128), F32),
            pltpu.VMEM((8, 512), F32),
            pltpu.VMEM((NT, 8, 512), F32),
            pltpu.VMEM((3 * D, 8), F32),
            pltpu.VMEM((D, 256 * IMAGES), BF16),
            pltpu.VMEM((IMAGES, 256, 256), BF16),
            pltpu.VMEM((IMAGES, 256, 128), F32),
            pltpu.VMEM((NZ, 16, 256), BF16),
            pltpu.VMEM((NZ, 2, 256), F32),
            pltpu.VMEM((18 * NZ, 256), F32),
            pltpu.VMEM((NX, 18 * NZ, 256), BF16),
            pltpu.VMEM((NZ, PIECE, 128), BF16),
            pltpu.VMEM((PIECE, 128), F32),
            pltpu.VMEM((2 * HP, 640), F32),
            pltpu.VMEM((2, NX, 2 * HP, 640), BF16),
            pltpu.VMEM((D, HALF), F32),
            pltpu.VMEM((D, HALF), F32),
            pltpu.VMEM((IMAGES, NT, HP, 128), BF16),
            pltpu.VMEM((IMAGES, NT, HP, 128), BF16),
            pltpu.VMEM((NZ, IMAGES, CHAN, 128), F32),
            pltpu.VMEM((NX, IMAGES, CHAN, 128), F32),
            pltpu.VMEM((NT, IMAGES, 128), F32),
            pltpu.VMEM((IMAGES, 128), F32),
            pltpu.VMEM((IMAGES, 1, TOKENS), F32),
            pltpu.VMEM((8, 128), F32),
            dma((3,)),
            dma((NT,)), dma((NT,)),
            dma((NT,)), dma((NT,)),
            dma((NZ,)), dma((NZ,)),
            dma((NZ,)), dma((NZ,)),
            dma((NX,)), dma((NX,)),
            dma((NZ,)), dma((NZ,)),
            dma((NX,)), dma((NX,)),
            dma, dma,
            dma((IMAGES, NT)), dma((IMAGES, NT)),
            dma((NZ,)), dma((NZ,)),
            dma((NX,)), dma((NX,)),
            dma((NT,)), dma((NT,)),
        ],
        compiler_params=pltpu.CompilerParams(
            collective_id=0, has_side_effects=True, vmem_limit_bytes=56 * 1024 * 1024
        ),
        cost_estimate=pl.CostEstimate(flops=6_000_000_000, bytes_accessed=8_000_000, transcendentals=4_200_000),
    )(
        slot_steps, class_labels, latents, anchor, noise_draws, freq, class_table, final_weight, in_weight, spread,
        qkv_weight, out_weight, time_weight, mod_weight.T, table,
    )
    return updated, errors


def solution(mesh):
    in_specs = (
        P(None, None, "tok"),
        P("tm", None, None, "tok"),
        P("tm", None, None, "tok"),
        P("tm", None),
        P(),
        P(),
        P(),
        P(),
        P(None, "tok"),
        P("tm", None),
        P("tm", None),
        P(),
    )
    out_specs = (P("tm", None, None, "tok"), P("tm", None))
    return jax.shard_map(body, mesh=mesh, in_specs=in_specs, out_specs=out_specs, check_vma=False)
```
